256 devices in a mesh: face: 4 (over z_hi), blk: 64 (over x, y, z_lo, core).
Axes of the slice: x: 4, y: 4, z: 8 (z_hi: 4, z_lo: 2; z = z_hi * 2 + z_lo), core: 2. Of those that a mesh axis runs over, the one named last changes fastest.
Arguments:
- state: float32 [256, 16, 4, 8, 4, 360], P(('face', 'blk')), may hold values from -6 to 6
- jacobian: float32 [256, 16, 4, 8, 4], P(('face', 'blk')), may hold values from 0.5 to 2
- metric_xx: float32 [256, 16, 4, 8, 4], P(('face', 'blk')), may hold values from 0.5 to 2
- metric_yy: float32 [256, 16, 4, 8, 4], P(('face', 'blk')), may hold values from 0.5 to 2
- metric_xy: float32 [256, 16, 4, 8, 4], P(('face', 'blk')), may hold values from -0.3 to 0.3
Outputs:
- smoothed: float32 [256, 16, 4, 8, 4, 360], P(('face', 'blk'))
The draws below stay inside these ranges and needn't reach their ends.
All inputs are finite; a program needn't handle non-finite values.
Results may differ from the reference program's by a relative error of at most 0.0001.
Values sent between devices are 32-bit elements; how exact they have to be, the bound alone decides.
No kernel may reach another device: no remote copies, remote signals or barrier semaphores. Data moves between devices by JAX's collectives and lax.ppermute only.
A program may use at most 64 MiB of HBM per device.

```python
import math
import jax
import jax.numpy as jnp
import numpy as np
from jax import lax

NP = 4
LEV = 72
FIELDS = 5
SUBCYCLES = 2
PY = 8
EX = 16
EY = 8
FL = 360
PATCHES = 256


def block_scale(stream_key, extent, shards, least, top_value):
    def one(position, parts):
        heights = jax.random.uniform(jax.random.fold_in(jax.random.fold_in(stream_key, 6), position), (parts,), jnp.float32, least / len(shards), top_value / len(shards))
        return jnp.repeat(jnp.exp(heights), extent[position] // parts).reshape((-1,) + (1,) * (len(extent) - position - 1))

    factor_of = one(*shards[0])
    for cut in shards[1:]:
        factor_of = factor_of * one(*cut)
    return factor_of


def centred(own_key, extent, deviation, bound, pieces=(), kind=jnp.bfloat16):
    values = deviation * jax.random.normal(own_key, extent, jnp.float32)
    if pieces:
        values = values * block_scale(own_key, extent, pieces, -0.22, 0.18)
    return jnp.clip(values, -bound, bound).astype(kind)


def setup_inputs(seed: int = 0) -> dict:
    seeds = jax.random.split(jax.random.key(seed), 6)
    return {
        "state": centred(seeds[0], (PATCHES, EX, NP, EY, NP, FL), 1.0, 6.0, ((0, 256),), jnp.float32),
        "jacobian": jnp.clip(jnp.exp(math.log(2.0) - 1.3862944 * jax.random.uniform(seeds[1], (PATCHES, EX, NP, EY, NP), jnp.float32) ** block_scale(seeds[1], (PATCHES, EX, NP, EY, NP), ((0, 256),), -0.2, 0.2)), 0.5, 2.0),
        "metric_xx": jnp.clip(jnp.exp(math.log(2.0) - 1.3862944 * jax.random.uniform(seeds[2], (PATCHES, EX, NP, EY, NP), jnp.float32) ** block_scale(seeds[2], (PATCHES, EX, NP, EY, NP), ((0, 256),), -0.2, 0.2)), 0.5, 2.0),
        "metric_yy": jnp.clip(jnp.exp(math.log(2.0) - 1.3862944 * jax.random.uniform(seeds[3], (PATCHES, EX, NP, EY, NP), jnp.float32) ** block_scale(seeds[3], (PATCHES, EX, NP, EY, NP), ((0, 256),), -0.2, 0.2)), 0.5, 2.0),
        "metric_xy": jnp.clip(jax.random.uniform(seeds[4], (PATCHES, EX, NP, EY, NP), jnp.float32, -0.3, 0.3) * block_scale(seeds[4], (PATCHES, EX, NP, EY, NP), ((0, 256),), -0.4, 0.0), -0.3, 0.3),
    }


viscosity = 0.0001

def gll_tables():
    root = 1.0 / math.sqrt(5.0)
    points = np.array([-1.0, -root, root, 1.0])
    weights = np.array([1.0 / 6.0, 5.0 / 6.0, 5.0 / 6.0, 1.0 / 6.0])
    scales = np.array([np.prod([points[target] - points[other] for other in range(4) if other != target]) for target in range(4)])
    derivative = np.zeros((4, 4))
    for target in range(4):
        for source in range(4):
            if target != source:
                derivative[target, source] = scales[target] / (scales[source] * (points[target] - points[source]))
        derivative[target, target] = -np.sum(derivative[target])
    return (weights, derivative)

def rim(values, dimension, element, point):
    picked = lax.index_in_dim(values, point, dimension + 1, keepdims=False)
    return lax.index_in_dim(picked, element, dimension, keepdims=False)

def edge_sum(values, before, after, dimension):
    number = values.shape[dimension]
    points_along = values.shape[dimension + 1]
    lower_rim = lax.slice_in_dim(values, 0, 1, axis=dimension + 1)
    upper_rim = lax.slice_in_dim(values, points_along - 1, points_along, axis=dimension + 1)
    before_full = jnp.expand_dims(before, (dimension, dimension + 1))
    after_full = jnp.expand_dims(after, (dimension, dimension + 1))
    shared = lax.slice_in_dim(upper_rim, 0, number - 1, axis=dimension) + lax.slice_in_dim(lower_rim, 1, number, axis=dimension)
    lower_new = jnp.concatenate([lax.slice_in_dim(lower_rim, 0, 1, axis=dimension) + before_full, shared], axis=dimension)
    upper_new = jnp.concatenate([shared, lax.slice_in_dim(upper_rim, number - 1, number, axis=dimension) + after_full], axis=dimension)
    middle = lax.slice_in_dim(values, 1, points_along - 1, axis=dimension + 1)
    return jnp.concatenate([lower_new, middle, upper_new], axis=dimension + 1)

def assemble_global(values):
    last = values.shape[0] - 1
    values = edge_sum(values, rim(values, 0, last, NP - 1), rim(values, 0, 0, 0), 0)
    zeros = jnp.zeros_like(rim(values, 2, 0, 0))
    return edge_sum(values, zeros, zeros, 2)

def laplace(field, geometry, assemble):
    weight, metric_one, metric_two, metric_cross, mass = geometry
    derivative = jnp.asarray(gll_tables()[1], jnp.float32)
    best = lax.Precision.HIGHEST
    slope_first = jnp.einsum('ai,xiyjf->xayjf', derivative, field, precision=best)
    slope_second = jnp.einsum('bj,xiyjf->xiybf', derivative, field, precision=best)
    flux_first = weight * (metric_one * slope_first + metric_cross * slope_second)
    flux_second = weight * (metric_cross * slope_first + metric_two * slope_second)
    weak = -(jnp.einsum('ai,xayjf->xiyjf', derivative, flux_first, precision=best) + jnp.einsum('bj,xiybf->xiyjf', derivative, flux_second, precision=best))
    return assemble(weak) / mass

def to_global(values):
    columns = values.shape[0] // PY
    rest = values.shape[5:]
    shaped = values.reshape((columns, PY) + values.shape[1:])
    shaped = jnp.moveaxis(shaped, 1, 3)
    return shaped.reshape((columns * EX, NP, PY * EY, NP) + rest)

def from_global(grid):
    columns = grid.shape[0] // EX
    rest = grid.shape[4:]
    shaped = grid.reshape((columns, EX, NP, PY, EY, NP) + rest)
    shaped = jnp.moveaxis(shaped, 3, 1)
    return shaped.reshape((columns * PY, EX, NP, EY, NP) + rest)

def reference(state, jacobian, metric_xx, metric_yy, metric_xy):
    gll_weights = gll_tables()[0]
    cell_weights = jnp.asarray(np.outer(gll_weights, gll_weights), jnp.float32)
    weight = to_global(jacobian)[..., None] * cell_weights[None, :, None, :, None]
    mass = assemble_global(weight)
    geometry = (weight, to_global(metric_xx)[..., None], to_global(metric_yy)[..., None], to_global(metric_xy)[..., None], mass)
    grid = to_global(state)
    blocks = jnp.moveaxis(grid.reshape(grid.shape[:4] + (FIELDS, LEV)), 4, 0)

    def smooth(block):
        for substep in range(SUBCYCLES):
            block = block - viscosity * laplace(laplace(block, geometry, assemble_global), geometry, assemble_global)
        return block
    result = lax.map(smooth, blocks)
    grid_out = jnp.moveaxis(result, 0, 4).reshape(grid.shape)
    return from_global(grid_out)
```

```python
import math

import jax
import jax.numpy as jnp
import numpy as np
from jax import lax
from jax.experimental import pallas as pl
from jax.experimental.pallas import tpu as pltpu
from jax.sharding import PartitionSpec as P

PY = 8
EX = 16
FL = 360
LANES = 384
PTS = 128
HALO = 3
WIDE = EX + 2 * HALO
AXES = ("face", "blk")
VISCOSITY = 1e-4
F32 = jnp.float32
BF16 = jnp.bfloat16


def gll_tables():
    root = 1.0 / math.sqrt(5.0)
    points = np.array([-1.0, -root, root, 1.0])
    weights = np.array([1.0 / 6.0, 5.0 / 6.0, 5.0 / 6.0, 1.0 / 6.0])
    scales = np.array(
        [np.prod([points[t] - points[o] for o in range(4) if o != t]) for t in range(4)]
    )
    derivative = np.zeros((4, 4))
    for t in range(4):
        for s in range(4):
            if t != s:
                derivative[t, s] = scales[t] / (scales[s] * (points[t] - points[s]))
        derivative[t, t] = -np.sum(derivative[t])
    return weights, derivative


def tables():
    weights, derivative = gll_tables()
    d_x = np.kron(derivative, np.eye(32))
    d_y = np.kron(np.eye(32), derivative)
    share = np.eye(PTS)
    for r in range(PTS):
        if r % 4 == 3 and r % 32 != 31:
            share[r, r + 1] = 1.0
            share[r + 1, r] = 1.0
    left = -share @ np.concatenate([d_x.T, d_y.T], axis=1)
    left = left.astype(np.float32)
    left_hi = left.astype(jnp.bfloat16)
    left_lo = (left - left_hi.astype(np.float32)).astype(jnp.bfloat16)
    cell = np.kron(weights, np.kron(np.ones(8), weights)).reshape(PTS, 1)
    return (
        np.stack([left_hi, left_lo]),
        np.stack([d_x, d_y]).astype(np.float32),
        cell.astype(np.float32),
    )


def halves(value):
    high = value.astype(BF16)
    low = (value - high.astype(F32)).astype(BF16)
    return high, low


def dot(a, b):
    return jnp.dot(a, b, preferred_element_type=F32)


def product(a_hi, a_lo, b):
    b_hi, b_lo = halves(b)
    return dot(a_hi, b_hi) + (dot(a_hi, b_lo) + dot(a_lo, b_hi))


def form(left_ref, diff_ref, fxx, fxy, fyy):
    d_x = diff_ref[0]
    d_y = diff_ref[1]
    top = fxx * d_x + fxy * d_y
    bottom = fxy * d_x + fyy * d_y
    return product(left_ref[0], left_ref[1], jnp.concatenate([top, bottom], axis=0))


def join(out_ref, e, q):
    shared = out_ref[e - 1, 3] + q[0:32]
    out_ref[e - 1, 3] = shared
    out_ref[e, 0] = shared


def pack_edges(field_ref, lo, hi, south_ref, north_ref):
    for e in range(lo, hi + 1):
        for i in range(4 if e == hi else 3):
            row = 3 * (e - lo) + i
            south_ref[row : row + 1, :] = field_ref[e, i, 0:1, :]
            north_ref[row : row + 1, :] = field_ref[e, i, 31:32, :]


def with_edges(value, south_ref, north_ref, row, flags_ref):
    sub = lax.broadcasted_iota(jnp.int32, (8, LANES), 0)
    from_south = south_ref[pl.ds(row, 1), :]
    from_north = north_ref[pl.ds(row, 1), :]
    south_ok = (sub == 0) & (flags_ref[0] != 0)
    north_ok = (sub == 7) & (flags_ref[1] != 0)
    first = value[0:8] + jnp.where(south_ok, from_south, 0.0)
    last = value[24:32] + jnp.where(north_ok, from_north, 0.0)
    return jnp.concatenate([first, value[8:24], last], axis=0)


def first_kernel(u_ref, jac_ref, xx_ref, yy_ref, xy_ref, left_ref, diff_ref, cell_ref, q_ref, m_ref, west_ref, east_ref):
    weight = jac_ref[...] * cell_ref[...]
    fxx = weight * xx_ref[...]
    fxy = weight * xy_ref[...]
    fyy = weight * yy_ref[...]
    row = lax.broadcasted_iota(jnp.int32, (PTS, EX), 0)
    up = jnp.concatenate([weight[1:], weight[:1]], axis=0)
    down = jnp.concatenate([weight[-1:], weight[:-1]], axis=0)
    mass = weight + jnp.where((row % 4 == 3) & (row % 32 != 31), up, 0.0)
    mass = mass + jnp.where((row % 4 == 0) & (row % 32 != 0), down, 0.0)
    for c in range(EX):
        m = form(left_ref, diff_ref, fxx[:, c : c + 1], fxy[:, c : c + 1], fyy[:, c : c + 1])
        m_ref[c] = m
        m_hi, m_lo = halves(m)
        q = product(m_hi, m_lo, u_ref[c])
        for i in range(4):
            q_ref[c, i, :, 0:FL] = q[32 * i : 32 * i + 32]
            q_ref[c, i, :, FL:LANES] = jnp.broadcast_to(mass[32 * i : 32 * i + 32, c : c + 1], (32, LANES - FL))
        if c > 0:
            shared = q_ref[c - 1, 3] + q_ref[c, 0]
            q_ref[c - 1, 3] = shared
            q_ref[c, 0] = shared
    lane = lax.broadcasted_iota(jnp.int32, (32, LANES - FL), 1)
    for ref, base in ((west_ref, 0), (east_ref, EX - HALO)):
        for k in range(HALO):
            c = base + k
            for i in range(3 if k < HALO - 1 else 4):
                g = 3 * k + i
                ref[g] = q_ref[c, i]
                if i == 3:
                    continue
                tail = q_ref[c, i, :, FL:LANES]
                for p in range(2 if i == 2 else 1):
                    for t, f in enumerate((fxx, fxy, fyy)):
                        s = 32 * (i + p)
                        tail = jnp.where(lane == 1 + 3 * p + t, f[s : s + 32, c : c + 1], tail)
                ref[g, :, FL:LANES] = tail


def merge_kernel(q_ref, west_ref, east_ref, f_ref, south_ref, north_ref):
    f_ref[HALO : HALO + EX] = q_ref[...]
    for k in range(HALO):
        for i in range(4):
            g = 3 * k + i
            f_ref[k, i] = west_ref[g]
            f_ref[HALO + EX + k, i] = east_ref[g]
    shared = west_ref[3 * HALO] + q_ref[0, 0]
    f_ref[HALO - 1, 3] = shared
    f_ref[HALO, 0] = shared
    shared = q_ref[EX - 1, 3] + east_ref[0]
    f_ref[HALO + EX - 1, 3] = shared
    f_ref[HALO + EX, 0] = shared
    south_ref[...] = jnp.zeros_like(south_ref)
    north_ref[...] = jnp.zeros_like(north_ref)
    pack_edges(f_ref, 0, WIDE - 1, south_ref, north_ref)


def halo_kernel(west_ref, east_ref, left_ref, diff_ref, m_ref):
    for side, ref in enumerate((west_ref, east_ref)):
        for k in range(HALO):
            fs = []
            for t in range(3):
                parts = []
                for i in range(4):
                    g = 3 * k + min(i, 2)
                    at = FL + 1 + t + (3 if i == 3 else 0)
                    parts.append(ref[g, :, at : at + 1])
                fs.append(jnp.concatenate(parts, axis=0))
            m_ref[HALO * side + k] = form(left_ref, diff_ref, *fs)


def second_kernel(flags_ref, f_ref, south_ref, north_ref, m_ref, mh_ref, out_ref, hi_ref, lo_ref, to_south_ref, to_north_ref):
    for e in range(WIDE):
        tiles = [with_edges(f_ref[e, i], south_ref, north_ref, 3 * e + i, flags_ref) for i in range(4)]
        value = jnp.concatenate(tiles, axis=0)
        inverse = 1.0 / value[:, FL : FL + 1]
        if e < HALO:
            m = mh_ref[e]
        elif e < HALO + EX:
            m = m_ref[e - HALO]
        else:
            m = mh_ref[e - EX]
        m_hi, m_lo = halves(m * inverse)
        hi_ref[e] = m_hi
        lo_ref[e] = m_lo
        q = product(m_hi, m_lo, value * inverse)
        for i in range(4):
            out_ref[e, i] = q[32 * i : 32 * i + 32]
        if e > 0:
            join(out_ref, e, q)
    to_south_ref[...] = jnp.zeros_like(to_south_ref)
    to_north_ref[...] = jnp.zeros_like(to_north_ref)
    pack_edges(out_ref, 1, WIDE - 2, to_south_ref, to_north_ref)


def later_kernel(lo, keep, flags_ref, f_ref, south_ref, north_ref, hi_ref, lo_ref, *refs):
    if keep:
        u_ref, out_ref, to_south_ref, to_north_ref, kept_ref = refs
    else:
        out_ref, to_south_ref, to_north_ref = refs
    hi = WIDE - 1 - lo
    for e in range(lo, hi + 1):
        tiles = [with_edges(f_ref[e, i], south_ref, north_ref, 3 * (e - lo) + i, flags_ref) for i in range(4)]
        value = jnp.concatenate(tiles, axis=0)
        if keep and HALO <= e < HALO + EX:
            kept_ref[e - HALO] = u_ref[e - HALO] - (2.0 * VISCOSITY) * value[:, 0:FL]
        q = product(hi_ref[e], lo_ref[e], value)
        for i in range(4):
            out_ref[e, i] = q[32 * i : 32 * i + 32]
        if e > lo:
            join(out_ref, e, q)
    to_south_ref[...] = jnp.zeros_like(to_south_ref)
    to_north_ref[...] = jnp.zeros_like(to_north_ref)
    pack_edges(out_ref, lo + 1, hi - 1, to_south_ref, to_north_ref)


def last_kernel(flags_ref, f_ref, south_ref, north_ref, kept_ref, out_ref):
    for c in range(EX):
        e = c + HALO
        tiles = [with_edges(f_ref[e, i], south_ref, north_ref, 3 * c + i, flags_ref) for i in range(4)]
        value = jnp.concatenate(tiles, axis=0)
        out_ref[c] = kept_ref[c] + (VISCOSITY * VISCOSITY) * value[:, 0:FL]


VM = pl.BlockSpec(memory_space=pltpu.VMEM)
SM = pl.BlockSpec(memory_space=pltpu.SMEM)


def call(body, outs, specs, name):
    return pl.pallas_call(
        body,
        out_shape=[jax.ShapeDtypeStruct(s, d) for s, d in outs],
        in_specs=specs,
        out_specs=[VM] * len(outs),
        compiler_params=pltpu.CompilerParams(vmem_limit_bytes=48 * 1024 * 1024),
        name=name,
    )


def moved(array, columns, rows):
    pairs = []
    for i in range(256):
        c, r = divmod(i, PY)
        pairs.append((i, (c + columns) % 32 * PY + (r + rows) % PY))
    return lax.ppermute(array, AXES, pairs)


def per_device(state, jacobian, metric_xx, metric_yy, metric_xy):
    left, diff, cell = (jnp.asarray(t) for t in tables())
    u = state.reshape(EX, PTS, FL)
    flat = [jnp.transpose(g[0], (1, 2, 3, 0)).reshape(PTS, EX) for g in (jacobian, metric_xx, metric_yy, metric_xy)]
    row = lax.axis_index(AXES) % PY
    flags = jnp.stack([row != 0, row != PY - 1]).astype(jnp.int32)

    q, m, to_west, to_east = call(
        first_kernel,
        [((EX, 4, 32, LANES), F32), ((EX, PTS, PTS), F32), ((10, 32, LANES), F32), ((10, 32, LANES), F32)],
        [VM] * 8,
        "first",
    )(u, *flat, left, diff, cell)
    from_west = moved(to_east, 1, 0)
    from_east = moved(to_west, -1, 0)
    wide = ((WIDE, 4, 32, LANES), F32)
    f, to_south, to_north = call(
        merge_kernel, [wide, ((72, LANES), F32), ((72, LANES), F32)], [VM] * 3, "merge"
    )(q, from_west, from_east)
    from_south = moved(to_north, 0, 1)
    from_north = moved(to_south, 0, -1)
    (mh,) = call(halo_kernel, [((2 * HALO, PTS, PTS), F32)], [VM] * 4, "halo")(from_west, from_east, left, diff)
    f, m_hi, m_lo, to_south, to_north = call(
        second_kernel,
        [wide, ((WIDE, PTS, PTS), BF16), ((WIDE, PTS, PTS), BF16), ((64, LANES), F32), ((64, LANES), F32)],
        [SM] + [VM] * 5,
        "second",
    )(flags, f, from_south, from_north, m, mh)
    from_south = moved(to_north, 0, 1)
    from_north = moved(to_south, 0, -1)
    f, to_south, to_north, kept = call(
        lambda *refs: later_kernel(1, True, *refs),
        [wide, ((56, LANES), F32), ((56, LANES), F32), ((EX, PTS, FL), F32)],
        [SM] + [VM] * 6,
        "third",
    )(flags, f, from_south, from_north, m_hi, m_lo, u)
    from_south = moved(to_north, 0, 1)
    from_north = moved(to_south, 0, -1)
    f, to_south, to_north = call(
        lambda *refs: later_kernel(2, False, *refs),
        [wide, ((56, LANES), F32), ((56, LANES), F32)],
        [SM] + [VM] * 5,
        "fourth",
    )(flags, f, from_south, from_north, m_hi, m_lo)
    from_south = moved(to_north, 0, 1)
    from_north = moved(to_south, 0, -1)
    (out,) = call(last_kernel, [((EX, PTS, FL), F32)], [SM] + [VM] * 4, "last")(flags, f, from_south, from_north, kept)
    return out.reshape(1, EX, 4, 8, 4, FL)


def solution(mesh):
    spec = P(AXES)
    return jax.shard_map(
        per_device, mesh=mesh, in_specs=(spec,) * 5, out_specs=spec, check_vma=False
    )
```

```python
import math

import jax
import jax.numpy as jnp
import numpy as np
from jax import lax
from jax.experimental import pallas as pl
from jax.experimental.pallas import tpu as pltpu
from jax.sharding import PartitionSpec as P

PY = 8
EX = 16
FL = 360
LANES = 384
PTS = 128
HALO = 3
WIDE = EX + 2 * HALO
GROUPS = 3 * HALO + 1
LINE = 25
RIM = 8 * GROUPS
SENT = RIM + 8
REST = 17
TAIL = LANES - FL
AXES = ("face", "blk")
VISCOSITY = 1e-4
F32 = jnp.float32
BF16 = jnp.bfloat16


def gll_tables():
    root = 1.0 / math.sqrt(5.0)
    points = np.array([-1.0, -root, root, 1.0])
    weights = np.array([1.0 / 6.0, 5.0 / 6.0, 5.0 / 6.0, 1.0 / 6.0])
    scales = np.array(
        [np.prod([points[t] - points[o] for o in range(4) if o != t]) for t in range(4)]
    )
    derivative = np.zeros((4, 4))
    for t in range(4):
        for s in range(4):
            if t != s:
                derivative[t, s] = scales[t] / (scales[s] * (points[t] - points[s]))
        derivative[t, t] = -np.sum(derivative[t])
    return weights, derivative


def tables():
    derivative = gll_tables()[1]
    d_x = np.kron(derivative, np.eye(32))
    d_y = np.kron(np.eye(32), derivative)
    share = np.eye(PTS)
    for r in range(PTS):
        if r % 4 == 3 and r % 32 != 31:
            share[r, r + 1] = 1.0
            share[r + 1, r] = 1.0
    left = (-share @ np.concatenate([d_x.T, d_y.T], axis=1)).astype(np.float32)
    ends = np.concatenate([np.r_[32 * i : 32 * i + 4, 32 * i + 28 : 32 * i + 32] for i in range(4)])
    rim = np.zeros((16, 64), np.float32)
    rim[0:4] = left[0::32][:, np.concatenate([ends, PTS + ends])]
    rim[4:8] = left[31::32][:, np.concatenate([ends, PTS + ends])]
    diff = np.stack([d_x, d_y]).astype(np.float32)
    spread_rim = np.zeros((32 * GROUPS, RIM), np.float32)
    spread = np.zeros((32 * GROUPS, 176), np.float32)
    for g in range(GROUPS):
        for ey in range(8):
            for j in range(4):
                k = 3 * ey + j
                row = 32 * g + 4 * ey + j
                if k < 4:
                    spread_rim[row, 8 * g + k] = 1.0
                elif k > 20:
                    spread_rim[row, 8 * g + k - 17] = 1.0
                else:
                    spread[row, REST * g + k - 4] = 1.0

    def pair(a):
        high = a.astype(jnp.bfloat16)
        return np.stack([high, (a - high.astype(np.float32)).astype(jnp.bfloat16)])

    return (
        pair(left),
        pair(rim),
        diff,
        diff[:, ends][:, :, ends],
        spread_rim.astype(jnp.bfloat16),
        spread.astype(jnp.bfloat16),
    )


def halves(value):
    high = value.astype(BF16)
    low = (value - high.astype(F32)).astype(BF16)
    return high, low


def dot(a, b):
    return jnp.dot(a, b, preferred_element_type=F32)


def product(a_hi, a_lo, b):
    b_hi, b_lo = halves(b)
    return dot(a_hi, b_hi) + (dot(a_hi, b_lo) + dot(a_lo, b_hi))


def applied(m_twice, m_lo, value):
    v_hi, v_lo = halves(value)
    return dot(m_twice, jnp.concatenate([v_hi, v_lo], axis=0)) + dot(m_lo, v_hi)


def moved_rows(choice, value):
    a = value.astype(BF16)
    rest = value - a.astype(F32)
    b = rest.astype(BF16)
    c = (rest - b.astype(F32)).astype(BF16)
    return (dot(choice, c) + dot(choice, b)) + dot(choice, a)


def fluxes(diff_ref, fxx, fxy, fyy):
    d_x = diff_ref[0]
    d_y = diff_ref[1]
    return jnp.concatenate([fxx * d_x + fxy * d_y, fxy * d_x + fyy * d_y], axis=0)


def form(left_ref, diff_ref, f):
    return product(left_ref[0], left_ref[1], fluxes(diff_ref, *f))


def geometry(jac_ref, xx_ref, yy_ref, xy_ref):
    ends, inner = (float(w) for w in gll_tables()[0][0:2])
    row = lax.broadcasted_iota(jnp.int32, (PTS, EX), 0)
    along = jnp.where((row < 32) | (row >= 96), ends, inner)
    weight = jac_ref[...] * (along * jnp.where((row % 4 == 0) | (row % 4 == 3), ends, inner))
    f = (weight * xx_ref[...], weight * xy_ref[...], weight * yy_ref[...])
    up = jnp.concatenate([weight[1:], weight[:1]], axis=0)
    down = jnp.concatenate([weight[-1:], weight[:-1]], axis=0)
    mass = weight + jnp.where((row % 4 == 3) & (row % 32 != 31), up, 0.0)
    mass = mass + jnp.where((row % 4 == 0) & (row % 32 != 0), down, 0.0)
    return f, mass


def column(f, c):
    return [t[:, c : c + 1] for t in f]


def fetch(sources, buffers, sems):
    copies = [pltpu.make_async_copy(s, d, sems.at[k]) for k, (s, d) in enumerate(zip(sources, buffers))]
    for copy in copies:
        copy.start()
    return copies


def either(even, a, b):
    return jnp.where(even, a, b)


def side_columns(want_west, u_ref, f, mass, left_ref, diff_ref, rim_out_ref, layers_ref, q_ref, m_ref):
    lane = lax.broadcasted_iota(jnp.int32, (PTS, PTS), 1)
    raw, part = {}, {}
    for k in range(HALO + 1):
        m = form(left_ref, diff_ref, column(f, k))
        m_ref[jnp.where(want_west, k, EX - HALO - 1 + k)] = m
        m_hi, m_lo = halves(m)
        q = product(m_hi, m_lo, u_ref[k].reshape(PTS, FL))
        for i in range(4):
            raw[k, i] = q[32 * i : 32 * i + 32]
            part[k, i] = mass[32 * i : 32 * i + 32, k : k + 1]
    for values in (raw, part):
        for k in range(HALO):
            values[k, 3] = values[k + 1, 0] = values[k, 3] + values[k + 1, 0]
    for k in range(HALO + 1):
        c = jnp.where(want_west, k, EX - HALO - 1 + k)
        for i in range(4):
            q_ref[c, i, :, 0:FL] = raw[k, i]
            q_ref[c, i, :, FL:LANES] = jnp.broadcast_to(part[k, i], (32, TAIL))
    sub = lax.broadcasted_iota(jnp.int32, (8, LANES), 0)
    for g in range(GROUPS):
        k, i = (g // 3, g % 3) if g < GROUPS - 1 else (HALO - 1, 3)
        row = either(want_west, raw[k, i], raw[k + 1, i])
        tail = jnp.broadcast_to(either(want_west, part[k, i], part[k + 1, i]), (32, TAIL))
        for lanes, value in ((slice(0, FL), row), (slice(FL, LANES), tail)):
            rim_out_ref[8 * g : 8 * g + 8, lanes] = jnp.where(sub[:, lanes] < 4, value[0:8], value[24:32])
            layers_ref[32 * g : 32 * g + 32, lanes] = value
    x = jnp.zeros((PTS, PTS), F32)
    for t in range(3):
        for k in range(HALO):
            x = jnp.where(lane == HALO * t + k, either(want_west, f[t][:, k : k + 1], f[t][:, k + 1 : k + 2]), x)
    x = jnp.transpose(x)
    rim_out_ref[RIM:SENT, 0:PTS] = x[0:8]
    rim_out_ref[RIM:SENT, PTS : 2 * PTS] = x[8:16]
    rim_out_ref[RIM:SENT, 2 * PTS :] = jnp.zeros((8, PTS), F32)


def gather_rest(layers_ref, out_ref):
    for g in range(GROUPS):
        for ey in range(1, 7):
            size = 3 if ey < 6 else 2
            to = REST * g + 3 * (ey - 1)
            at = 32 * g + 4 * ey + 1
            out_ref[to : to + size, :] = layers_ref[at : at + size, :]
    out_ref[REST * GROUPS :, :] = jnp.zeros((6, LANES), F32)


def nearest(want_west, t):
    return either(want_west, t[:, 0 : HALO + 1], t[:, EX - HALO - 1 : EX])


def first_kernel(flags_ref, u_hbm, jac_hbm, xx_hbm, yy_hbm, xy_hbm, left_hbm, diff_hbm, rim_out_ref, layers_ref, other_ref, f_ref, mass_ref, left_ref, diff_ref, q_ref, m_ref, u_ref, jac_ref, xx_ref, yy_ref, xy_ref, sems):
    want_west = flags_ref[2] != 0
    size = HALO + 1
    here = jnp.where(want_west, 0, EX - size)
    there = jnp.where(want_west, EX - size, 0)
    copies = fetch(
        (jac_hbm, xx_hbm, yy_hbm, xy_hbm, left_hbm, diff_hbm, u_hbm.at[0, pl.ds(here, size)], u_hbm.at[0, pl.ds(there, size)]),
        (jac_ref, xx_ref, yy_ref, xy_ref, left_ref, diff_ref, u_ref, other_ref),
        sems,
    )
    for copy in copies[:6]:
        copy.wait()
    f, mass = geometry(jac_ref, xx_ref, yy_ref, xy_ref)
    for t in range(3):
        f_ref[t] = f[t]
    mass_ref[...] = mass
    copies[6].wait()
    side_columns(want_west, u_ref, [nearest(want_west, t) for t in f], nearest(want_west, mass), left_ref, diff_ref, rim_out_ref, layers_ref, q_ref, m_ref)
    copies[7].wait()


def other_kernel(flags_ref, u_ref, f_ref, mass_ref, left_ref, diff_ref, q_in, m_in, rim_out_ref, layers_ref, q_ref, m_ref):
    del q_in, m_in
    want_west = flags_ref[2] == 0
    f = [nearest(want_west, f_ref[t]) for t in range(3)]
    side_columns(want_west, u_ref, f, nearest(want_west, mass_ref[...]), left_ref, diff_ref, rim_out_ref, layers_ref, q_ref, m_ref)


def rest_kernel(first_ref, other_ref, one_ref, two_ref):
    gather_rest(first_ref, one_ref)
    gather_rest(other_ref, two_ref)


def end_rows(f):
    return [jnp.concatenate([t[32 * i + a : 32 * i + a + 4] for i in range(4) for a in (0, 28)], axis=0) for t in f]


def rows_kernel(u_hbm, rim_hbm, near_hbm, f_ref, mass_ref, e_ref, south_ref, north_ref, low_ref, high_ref, rim_ref, near_ref, sems):
    copies = fetch(
        (rim_hbm, near_hbm, u_hbm.at[0, :, :, 0], u_hbm.at[0, :, :, 7]), (rim_ref, near_ref, low_ref, high_ref), sems
    )
    for copy in copies[:2]:
        copy.wait()
    f = end_rows([f_ref[t] for t in range(3)])
    for c in range(EX):
        e_ref[c] = form(rim_ref, near_ref, column(f, c))[0:8]
    for copy in copies[2:]:
        copy.wait()
    res = {}
    for c in range(0, EX, 4):
        tiles = [ref[c + k, i] for k in range(4) for i in range(4) for ref in (low_ref, high_ref)]
        r = rim_product([e_ref[c + k] for k in range(4)], jnp.concatenate(tiles, axis=0))
        for k in range(4):
            res[c + k] = r[8 * k : 8 * k + 8]
    mass = mass_ref[...]
    for side, (out, at) in enumerate(((south_ref, 0), (north_ref, 31))):
        for c in range(EX):
            for i in range(4 if c == EX - 1 else 3):
                row = 3 * c + i
                value = res[c][4 * side + i : 4 * side + i + 1]
                part = mass[32 * i + at : 32 * i + at + 1, c : c + 1]
                if i == 0 and c > 0:
                    value = value + res[c - 1][4 * side + 3 : 4 * side + 4]
                    part = part + mass[96 + at : 97 + at, c - 1 : c]
                out[row : row + 1, 0:FL] = value
                out[row : row + 1, FL:LANES] = jnp.broadcast_to(part, (1, TAIL))
        out[49:56, :] = jnp.zeros((7, LANES), F32)


def rim_product(es, value):
    blocks = []
    for k, e in enumerate(es):
        parts = [jnp.zeros((8, 32), F32)] * 4
        parts[k] = e
        blocks.append(jnp.concatenate(parts, axis=1))
    m_hi, m_lo = halves(jnp.concatenate(blocks, axis=0))
    v_hi, v_lo = halves(value)
    both = dot(jnp.concatenate([m_hi, m_lo], axis=0), v_hi)
    return both[0:32] + (both[32:64] + dot(m_hi, v_lo))


def own_kernel(u_hbm, after_ref, f_ref, mass_ref, left_ref, diff_ref, q_in, m_in, q_ref, m_ref, u_ref, sems):
    del after_ref, q_in, m_in
    first, final = HALO + 1, EX - HALO - 2
    copies = fetch(
        [u_hbm.at[0, c : c + 4] for c in range(first, final, 4)], [u_ref.at[c : c + 4] for c in range(0, 8, 4)], sems
    )
    f = [f_ref[t] for t in range(3)]
    mass = mass_ref[...]
    for c in range(first, final + 1):
        m = form(left_ref, diff_ref, column(f, c))
        m_ref[c] = m
        m_hi, m_lo = halves(m)
        if (c - first) % 4 == 0:
            copies[(c - first) // 4].wait()
        q = product(m_hi, m_lo, u_ref[c - first].reshape(PTS, FL))
        for i in range(4):
            q_ref[c, i, :, 0:FL] = q[32 * i : 32 * i + 32]
            q_ref[c, i, :, FL:LANES] = jnp.broadcast_to(mass[32 * i : 32 * i + 32, c : c + 1], (32, TAIL))
        join_own(q_ref, c)
    join_own(q_ref, final + 1)


def join_own(q_ref, c):
    shared = q_ref[c - 1, 3] + q_ref[c, 0]
    q_ref[c - 1, 3] = shared
    q_ref[c, 0] = shared


def merge_kernel(flags_ref, one_ref, two_ref, own_south_ref, own_north_ref, south_ref, north_ref):
    even = flags_ref[2] != 0
    for out, own, at in ((south_ref, own_south_ref, 0), (north_ref, own_north_ref, 7)):
        out[10:57, :] = own[1:48, :]
        for g in range(GROUPS - 1):
            r = 8 * g + at
            out[g : g + 1, :] = either(even, one_ref[r : r + 1, :], two_ref[r : r + 1, :])
            r = 8 * (g + 1) + at
            out[58 + g : 59 + g, :] = either(even, two_ref[r : r + 1, :], one_ref[r : r + 1, :])
        r = 8 * (GROUPS - 1) + at
        out[9:10, :] = either(even, one_ref[r : r + 1, :], two_ref[r : r + 1, :]) + own[0:1, :]
        out[57:58, :] = own[48:49, :] + either(even, two_ref[at : at + 1, :], one_ref[at : at + 1, :])
        out[67:72, :] = jnp.zeros((5, LANES), F32)


def halo_kernel(flags_ref, one_ref, two_ref, left_ref, rim_ref, diff_ref, near_ref, m_ref, e_ref, west_ref, east_ref):
    even = flags_ref[2] != 0
    west_ref[...] = either(even, one_ref[...], two_ref[...])
    east_ref[...] = either(even, two_ref[...], one_ref[...])
    for side, ref in enumerate((west_ref, east_ref)):
        x = jnp.concatenate(
            [ref[RIM:SENT, 0:PTS], ref[RIM:SENT, PTS : 2 * PTS], jnp.zeros((PTS - 16, PTS), F32)], axis=0
        )
        x = jnp.transpose(x)
        for k in range(HALO):
            fs = [x[:, HALO * t + k : HALO * t + k + 1] for t in range(3)]
            m_ref[HALO * side + k] = form(left_ref, diff_ref, fs)
            e_ref[HALO * side + k] = form(rim_ref, near_ref, end_rows(fs))[0:8]


def edge_masks(flags_ref):
    sub = lax.broadcasted_iota(jnp.int32, (8, LANES), 0)
    return (sub == 0) & (flags_ref[0] != 0), (sub == 7) & (flags_ref[1] != 0)


def first_tile(value, south_ref, row, masks):
    return value + jnp.where(masks[0], south_ref[row : row + 1, :], 0.0)


def last_tile(value, north_ref, row, masks):
    return value + jnp.where(masks[1], north_ref[row : row + 1, :], 0.0)


def column_value(part, e, lo, south_ref, north_ref, masks):
    tiles = []
    for i in range(4):
        row = 3 * (e - lo) + i
        tiles.append(first_tile(part(e, i, 0, 8), south_ref, row, masks))
        tiles.append(part(e, i, 8, 24))
        tiles.append(last_tile(part(e, i, 24, 32), north_ref, row, masks))
    return jnp.concatenate(tiles, axis=0)


def rim_value(part, e, lo, south_ref, north_ref, masks):
    tiles = []
    for i in range(4):
        row = 3 * (e - lo) + i
        tiles.append(last_tile(first_tile(part(e, i), south_ref, row, masks), north_ref, row, masks))
    return jnp.concatenate(tiles, axis=0)


def both_ends(ref, k, i):
    sub = lax.broadcasted_iota(jnp.int32, (8, LANES), 0)
    return jnp.where(sub < 4, ref[k, i, 0:8], ref[k, i, 24:32])


def group_of(k, i):
    return 3 * k + i


def rim_part(q_ref, west_ref, east_ref):
    def part(e, i):
        if (e, i) in ((HALO - 1, 3), (HALO, 0)):
            g = 8 * (GROUPS - 1)
            return west_ref[g : g + 8] + both_ends(q_ref, 0, 0)
        if (e, i) in ((HALO + EX - 1, 3), (HALO + EX, 0)):
            return both_ends(q_ref, EX - 1, 3) + east_ref[0:8]
        if HALO <= e < HALO + EX:
            return both_ends(q_ref, e - HALO, i)
        ref, k = (west_ref, e) if e < HALO else (east_ref, e - HALO - EX)
        g = 8 * group_of(k, i)
        return ref[g : g + 8]

    return part


def edges(part, lo, scaled, flags_ref, from_south_ref, from_north_ref, matrix, south_ref, north_ref):
    hi = WIDE - 1 - lo
    masks = edge_masks(flags_ref)
    res = {}
    scale = {}
    for first in range(0, WIDE, 4):
        values, es = [], []
        for e in range(first, first + 4):
            if lo <= e <= hi:
                value = rim_value(part, e, lo, from_south_ref, from_north_ref, masks)
                if not scaled:
                    inverse = 1.0 / value[:, FL : FL + 1]
                    value = value * inverse
                    for i in range(4):
                        scale[e, i] = (inverse[8 * i : 8 * i + 1], inverse[8 * i + 7 : 8 * i + 8])
                values.append(value)
                es.append(matrix(e))
            else:
                values.append(jnp.zeros((32, LANES), F32))
                es.append(jnp.zeros((8, 32), F32))
        r = rim_product(es, jnp.concatenate(values, axis=0))
        for k in range(4):
            res[first + k] = r[8 * k : 8 * k + 8]
    first, final = lo + 1, hi - 1
    for side, out in enumerate((south_ref, north_ref)):
        for e in range(first, final + 1):
            for i in range(4 if e == final else 3):
                row = 3 * (e - first) + i
                value = res[e][4 * side + i : 4 * side + i + 1]
                if i == 0:
                    value = value + res[e - 1][4 * side + 3 : 4 * side + 4]
                if i == 3:
                    value = value + res[e + 1][4 * side : 4 * side + 1]
                if not scaled:
                    value = value * scale[e, i][side]
                out[row : row + 1, :] = value
        used = 3 * (final - first + 1) + 1
        out[used:, :] = jnp.zeros((out.shape[0] - used, LANES), F32)


def second_edges(flags_ref, q_ref, west_ref, east_ref, e_ref, halo_e_ref, from_south_ref, from_north_ref, south_ref, north_ref):
    part = rim_part(q_ref, west_ref, east_ref)
    edges(part, 0, False, flags_ref, from_south_ref, from_north_ref, rim_matrix(e_ref, halo_e_ref), south_ref, north_ref)


def rim_matrix(e_ref, halo_e_ref):
    def matrix(e):
        if HALO <= e < HALO + EX:
            return e_ref[e - HALO]
        return halo_e_ref[e if e < HALO else e - EX]

    return matrix


def split_matrix(inner_ref, outer_ref):
    def matrix(e):
        inner, k = split_at(e)
        return (inner_ref if inner else outer_ref)[k]

    return matrix


def third_edges(flags_ref, inner_ref, outer_ref, joint_ref, in_e_ref, out_e_ref, from_south_ref, from_north_ref, south_ref, north_ref):
    sub = lax.broadcasted_iota(jnp.int32, (8, LANES), 0)
    whole = split_part(inner_ref, outer_ref, joint_ref)

    def part(e, i):
        return jnp.where(sub < 4, whole(e, i, 0, 8), whole(e, i, 24, 32))

    edges(part, 1, True, flags_ref, from_south_ref, from_north_ref, split_matrix(in_e_ref, out_e_ref), south_ref, north_ref)


def fourth_edges(flags_ref, f_ref, in_e_ref, out_e_ref, from_south_ref, from_north_ref, south_ref, north_ref):
    def part(e, i):
        return both_ends(f_ref, e, i)

    edges(part, 2, True, flags_ref, from_south_ref, from_north_ref, split_matrix(in_e_ref, out_e_ref), south_ref, north_ref)


def join(out_ref, e, q):
    shared = out_ref[e - 1, 3] + q[0:32]
    out_ref[e - 1, 3] = shared
    out_ref[e, 0] = shared


def put(out_ref, e, first, q):
    for i in range(4):
        out_ref[e, i] = q[32 * i : 32 * i + 32]
    if e > first:
        join(out_ref, e, q)


INNER = range(HALO + 1, HALO + EX - 1)
OUTER = [e for e in range(WIDE) if e not in INNER]


def split_at(e):
    return (True, e - INNER[0]) if e in INNER else (False, OUTER.index(e))


def split_part(inner_ref, outer_ref, joint_ref):
    def part(e, i, a, b):
        if (e, i) in ((INNER[0] - 1, 3), (INNER[0], 0)):
            return joint_ref[0, a:b]
        if (e, i) in ((INNER[-1], 3), (INNER[-1] + 1, 0)):
            return joint_ref[1, a:b]
        inner, k = split_at(e)
        return (inner_ref if inner else outer_ref)[k, i, a:b]

    return part


def second_column(value, m, k, rim, out_ref, join_before, twice_ref, lo_ref, scaled_ref):
    inverse = 1.0 / value[:, FL : FL + 1]
    m_hi, m_lo = halves(m * inverse)
    twice = jnp.concatenate([m_hi, m_hi], axis=1)
    twice_ref[k] = twice
    lo_ref[k] = m_lo
    put(out_ref, k, 0 if join_before else k, applied(twice, m_lo, value * inverse))
    rows = jnp.concatenate(
        [inverse[32 * i : 32 * i + 1] for i in range(4)] + [inverse[32 * i + 31 : 32 * i + 32] for i in range(4)], axis=0
    )
    scaled_ref[k] = rim * rows


def second_inner(flags_ref, q_ref, e_ref, from_south_ref, from_north_ref, m_ref, out_ref, twice_ref, lo_ref, scaled_ref):
    def part(e, i, a, b):
        return q_ref[e - HALO, i, a:b]

    masks = edge_masks(flags_ref)
    for k, e in enumerate(INNER):
        value = column_value(part, e, 0, from_south_ref, from_north_ref, masks)
        second_column(value, m_ref[e - HALO], k, e_ref[e - HALO], out_ref, k > 0, twice_ref, lo_ref, scaled_ref)


def second_outer(flags_ref, q_ref, west_ref, east_ref, one_rest_ref, two_rest_ref, spread_rim_ref, spread_ref, e_ref, halo_e_ref, from_south_ref, from_north_ref, m_ref, mh_ref, inner_ref, out_ref, joint_ref, twice_ref, lo_ref, scaled_ref):
    even = flags_ref[2] != 0
    rests = (either(even, one_rest_ref[...], two_rest_ref[...]), either(even, two_rest_ref[...], one_rest_ref[...]))
    wide = [
        moved_rows(spread_rim_ref[...], rim[0:RIM]) + moved_rows(spread_ref[...], rest)
        for rim, rest in zip((west_ref, east_ref), rests)
    ]

    def part(e, i, a, b):
        if (e, i) in ((HALO - 1, 3), (HALO, 0)):
            g = 32 * (GROUPS - 1)
            return wide[0][g + a : g + b] + q_ref[0, 0, a:b]
        if (e, i) in ((HALO + EX - 1, 3), (HALO + EX, 0)):
            return q_ref[EX - 1, 3, a:b] + wide[1][a:b]
        if HALO <= e < HALO + EX:
            return q_ref[e - HALO, i, a:b]
        side, k = (0, e) if e < HALO else (1, e - HALO - EX)
        g = 32 * group_of(k, i)
        return wide[side][g + a : g + b]

    masks = edge_masks(flags_ref)
    for k, e in enumerate(OUTER):
        value = column_value(part, e, 0, from_south_ref, from_north_ref, masks)
        if e < HALO:
            m = mh_ref[e]
        elif e < HALO + EX:
            m = m_ref[e - HALO]
        else:
            m = mh_ref[e - EX]
        second_column(value, m, k, rim_matrix(e_ref, halo_e_ref)(e), out_ref, k not in (0, len(OUTER) // 2), twice_ref, lo_ref, scaled_ref)
    half = len(OUTER) // 2
    joint_ref[0] = out_ref[half - 1, 3] + inner_ref[0, 0]
    joint_ref[1] = inner_ref[len(INNER) - 1, 3] + out_ref[half, 0]


def matrices(e, inner, outer):
    is_inner, k = split_at(e)
    twice_ref, lo_ref = inner if is_inner else outer
    return twice_ref[k], lo_ref[k]


def third_full(flags_ref, inner_ref, outer_ref, joint_ref, from_south_ref, from_north_ref, in_twice, in_lo, out_twice, out_lo, u_ref, out_ref, kept_ref):
    part = split_part(inner_ref, outer_ref, joint_ref)
    masks = edge_masks(flags_ref)
    for e in range(1, WIDE - 1):
        value = column_value(part, e, 1, from_south_ref, from_north_ref, masks)
        if HALO <= e < HALO + EX:
            c = e - HALO
            kept_ref[c] = u_ref[0, c].reshape(PTS, FL) - (2.0 * VISCOSITY) * value[:, 0:FL]
        put(out_ref, e, 1, applied(*matrices(e, (in_twice, in_lo), (out_twice, out_lo)), value))


def fourth_full(flags_ref, f_ref, from_south_ref, from_north_ref, in_twice, in_lo, out_twice, out_lo, kept_ref, out_ref, rim_south_ref, rim_north_ref, z_ref):
    def part(e, i, a, b):
        return f_ref[e, i, a:b]

    masks = edge_masks(flags_ref)
    for e in range(2, WIDE - 2):
        value = column_value(part, e, 2, from_south_ref, from_north_ref, masks)
        put(z_ref, e, 2, applied(*matrices(e, (in_twice, in_lo), (out_twice, out_lo)), value))
        c = e - HALO - 1
        if 0 <= c < EX:
            z = jnp.concatenate([z_ref[e - 1, i, :, 0:FL] for i in range(4)], axis=0)
            done = (kept_ref[c] + (VISCOSITY * VISCOSITY) * z).reshape(4, 8, 4, FL)
            out_ref[0, c] = done
            rim_south_ref[c] = done[:, 0]
            rim_north_ref[c] = done[:, 7]


def patch_kernel(flags_ref, old_ref, rim_south_ref, rim_north_ref, from_south_ref, from_north_ref, out_ref, south_buf, north_buf, sems):
    del old_ref
    sub = lax.broadcasted_iota(jnp.int32, (4, FL), 0)
    masks = ((sub == 0) & (flags_ref[0] != 0), (sub == 3) & (flags_ref[1] != 0))
    copies = []
    for b in range(0, EX, 4):
        for side, (rim, got, buf) in enumerate(
            ((rim_south_ref, from_south_ref, south_buf), (rim_north_ref, from_north_ref, north_buf))
        ):
            for c in range(b, b + 4):
                for i in range(4):
                    row = 3 * c + i
                    more = (VISCOSITY * VISCOSITY) * got[row : row + 1, 0:FL]
                    buf[c, i] = rim[c, i] + jnp.where(masks[side], more, 0.0)
            copies.append(
                pltpu.make_async_copy(buf.at[b : b + 4], out_ref.at[0, b : b + 4, :, 7 * side], sems.at[len(copies)])
            )
            copies[-1].start()
    for copy in copies:
        copy.wait()


VM = pl.BlockSpec(memory_space=pltpu.VMEM)
SM = pl.BlockSpec(memory_space=pltpu.SMEM)
ANY = pl.BlockSpec(memory_space=pl.ANY)
HBM = pl.BlockSpec(memory_space=pltpu.HBM)


def call(body, outs, specs, name, scratch=(), out_specs=None, aliases=None):
    return pl.pallas_call(
        body,
        out_shape=[jax.ShapeDtypeStruct(s, d) for s, d in outs],
        in_specs=specs,
        out_specs=out_specs or [VM] * len(outs),
        scratch_shapes=list(scratch),
        input_output_aliases=aliases or {},
        compiler_params=pltpu.CompilerParams(vmem_limit_bytes=24 * 1024 * 1024),
        name=name,
    )


def moved(array, columns, rows):
    pairs = []
    for i in range(256):
        c, r = divmod(i, PY)
        pairs.append((i, (c + columns) % 32 * PY + (r + rows) % PY))
    return lax.ppermute(array, AXES, pairs)


def swapped(array, odd):
    pairs = []
    for i in range(256):
        c, r = divmod(i, PY)
        pairs.append((i, (((c + odd) ^ 1) - odd) % 32 * PY + r))
    return lax.ppermute(array, AXES, pairs)


def across(to_south, to_north):
    return moved(to_north, 0, 1), moved(to_south, 0, -1)


def per_device(state, jacobian, metric_xx, metric_yy, metric_xy):
    left, rim, diff, near, spread_rim, spread = (jnp.asarray(t) for t in tables())
    flat = [jnp.transpose(g[0], (1, 2, 3, 0)).reshape(PTS, EX) for g in (jacobian, metric_xx, metric_yy, metric_xy)]
    index = lax.axis_index(AXES)
    row = index % PY
    flags = jnp.stack([row != 0, row != PY - 1, index // PY % 2 == 0]).astype(jnp.int32)
    rows = lambda n: ((n, LANES), F32)
    wide = ((WIDE, 4, 32, LANES), F32)
    pinned = lambda *ts: [pltpu.with_memory_space_constraint(t, pltpu.HBM) for t in ts]
    four = (HALO + 1, 4, 8, 4, FL)

    own = [((EX, 4, 32, LANES), F32), ((EX, PTS, PTS), F32)]
    rim_one, layers_one, other, f, mass, left_in, diff_in, q, m = call(
        first_kernel,
        [rows(SENT), rows(32 * GROUPS), (four, F32), ((3, PTS, EX), F32), ((PTS, EX), F32), (left.shape, BF16), (diff.shape, F32), *own],
        [SM] + [HBM] * 7,
        "first",
        scratch=[pltpu.VMEM(four, F32), *[pltpu.VMEM((PTS, EX), F32)] * 4, pltpu.SemaphoreType.DMA((8,))],
    )(flags, *pinned(state, *flat, left, diff))
    one = swapped(rim_one, 1)
    rim_two, layers_two, q, m = call(
        other_kernel, [rows(SENT), rows(32 * GROUPS), *own], [SM] + [VM] * 7, "other", aliases={6: 2, 7: 3}
    )(flags, other, f, mass, left_in, diff_in, q, m)
    two = swapped(rim_two, 0)
    rest_one, rest_two = call(rest_kernel, [rows(176)] * 2, [VM] * 2, "rest")(layers_one, layers_two)
    rest_one = swapped(rest_one, 1)
    rest_two = swapped(rest_two, 0)
    e, own_south, own_north = call(
        rows_kernel,
        [((EX, 8, 32), F32), rows(56), rows(56)],
        [HBM] * 3 + [VM] * 2,
        "rows",
        scratch=[pltpu.VMEM((EX, 4, 4, FL), F32)] * 2
        + [pltpu.VMEM(rim.shape, BF16), pltpu.VMEM(near.shape, F32), pltpu.SemaphoreType.DMA((4,))],
    )(*pinned(state, rim, near), f, mass)
    to_south, to_north = call(merge_kernel, [rows(72)] * 2, [SM] + [VM] * 4, "merge")(flags, one, two, own_south, own_north)
    south1, north1 = across(to_south, to_north)
    q, m = call(
        own_kernel,
        own,
        [HBM, ANY] + [VM] * 6,
        "own",
        scratch=[pltpu.VMEM((8, 4, 8, 4, FL), F32), pltpu.SemaphoreType.DMA((2,))],
        aliases={6: 0, 7: 1},
    )(*pinned(state), to_south, f, mass, left_in, diff_in, q, m)
    mh, halo_e, west, east = call(
        halo_kernel,
        [((2 * HALO, PTS, PTS), F32), ((2 * HALO, 8, 32), F32), rows(SENT), rows(SENT)],
        [SM] + [VM] * 6,
        "halo",
    )(flags, one, two, left_in, rim, diff_in, near)
    to_south, to_north = call(second_edges, [rows(64)] * 2, [SM] + [VM] * 7, "edges2")(
        flags, q, west, east, e, halo_e, south1, north1
    )
    south2, north2 = across(to_south, to_north)
    matrix = lambda n: [((n, PTS, 2 * PTS), BF16), ((n, PTS, PTS), BF16), ((n, 8, 32), F32)]
    inner, in_twice, in_lo, in_pairs = call(
        second_inner, [((14, 4, 32, LANES), F32), *matrix(14)], [SM] + [VM] * 5, "inner2"
    )(flags, q, e, south1, north1, m)
    outer, joint, out_twice, out_lo, out_pairs = call(
        second_outer, [((8, 4, 32, LANES), F32), ((2, 32, LANES), F32), *matrix(8)], [SM] + [VM] * 14, "outer2"
    )(flags, q, west, east, rest_one, rest_two, spread_rim, spread, e, halo_e, south1, north1, m, mh, inner)
    to_south, to_north = call(third_edges, [rows(56)] * 2, [SM] + [VM] * 7, "edges3")(
        flags, inner, outer, joint, in_pairs, out_pairs, south2, north2
    )
    south3, north3 = across(to_south, to_north)
    f, kept = call(third_full, [wide, ((EX, PTS, FL), F32)], [SM] + [VM] * 10, "full3")(
        flags, inner, outer, joint, south2, north2, in_twice, in_lo, out_twice, out_lo, state
    )
    to_south, to_north = call(fourth_edges, [rows(56)] * 2, [SM] + [VM] * 5, "edges4")(
        flags, f, in_pairs, out_pairs, south3, north3
    )
    south4, north4 = across(to_south, to_north)
    out, rim_south, rim_north = call(
        fourth_full,
        [((1, EX, 4, 8, 4, FL), F32), ((EX, 4, 4, FL), F32), ((EX, 4, 4, FL), F32)],
        [SM] + [VM] * 8,
        "full4",
        scratch=[pltpu.VMEM((WIDE, 4, 32, LANES), F32)],
    )(flags, f, south3, north3, in_twice, in_lo, out_twice, out_lo, kept)
    (out,) = call(
        patch_kernel,
        [((1, EX, 4, 8, 4, FL), F32)],
        [SM, ANY] + [VM] * 4,
        "patch",
        scratch=[pltpu.VMEM((EX, 4, 4, FL), F32), pltpu.VMEM((EX, 4, 4, FL), F32), pltpu.SemaphoreType.DMA((8,))],
        out_specs=[ANY],
        aliases={1: 0},
    )(flags, out, rim_south, rim_north, south4, north4)
    return out


def solution(mesh):
    spec = P(AXES)
    return jax.shard_map(per_device, mesh=mesh, in_specs=(spec,) * 5, out_specs=spec, check_vma=False)
```

```python
import math

import jax
import jax.numpy as jnp
import numpy as np
from jax import lax
from jax.experimental import pallas as pl
from jax.experimental.pallas import tpu as pltpu
from jax.sharding import PartitionSpec as P

PY = 8
EX = 16
FL = 360
LANES = 384
PTS = 128
HALO = 3
WIDE = EX + 2 * HALO
GROUPS = 3 * HALO + 1
LINE = 25
RIM = 8 * GROUPS
SENT = RIM + 8
REST = 17
TAIL = LANES - FL
QUADS = -(-WIDE // 4)
AXES = ("face", "blk")
VISCOSITY = 1e-4
F32 = jnp.float32
BF16 = jnp.bfloat16


def gll_tables():
    root = 1.0 / math.sqrt(5.0)
    points = np.array([-1.0, -root, root, 1.0])
    weights = np.array([1.0 / 6.0, 5.0 / 6.0, 5.0 / 6.0, 1.0 / 6.0])
    scales = np.array(
        [np.prod([points[t] - points[o] for o in range(4) if o != t]) for t in range(4)]
    )
    derivative = np.zeros((4, 4))
    for t in range(4):
        for s in range(4):
            if t != s:
                derivative[t, s] = scales[t] / (scales[s] * (points[t] - points[s]))
        derivative[t, t] = -np.sum(derivative[t])
    return weights, derivative


def tables():
    derivative = gll_tables()[1]
    d_x = np.kron(derivative, np.eye(32))
    d_y = np.kron(np.eye(32), derivative)
    share = np.eye(PTS)
    for r in range(PTS):
        if r % 4 == 3 and r % 32 != 31:
            share[r, r + 1] = 1.0
            share[r + 1, r] = 1.0
    left = (-share @ np.concatenate([d_x.T, d_y.T], axis=1)).astype(np.float32)
    ends = np.concatenate([np.r_[32 * i : 32 * i + 4, 32 * i + 28 : 32 * i + 32] for i in range(4)])
    rim = np.zeros((16, 64), np.float32)
    rim[0:4] = left[0::32][:, np.concatenate([ends, PTS + ends])]
    rim[4:8] = left[31::32][:, np.concatenate([ends, PTS + ends])]
    diff = np.stack([d_x, d_y]).astype(np.float32)
    spread_rim = np.zeros((32 * GROUPS, RIM), np.float32)
    spread = np.zeros((32 * GROUPS, 176), np.float32)
    for g in range(GROUPS):
        for ey in range(8):
            for j in range(4):
                k = 3 * ey + j
                row = 32 * g + 4 * ey + j
                if k < 4:
                    spread_rim[row, 8 * g + k] = 1.0
                elif k > 20:
                    spread_rim[row, 8 * g + k - 17] = 1.0
                else:
                    spread[row, REST * g + k - 4] = 1.0

    def pair(a):
        high = a.astype(jnp.bfloat16)
        return np.stack([high, (a - high.astype(np.float32)).astype(jnp.bfloat16)])

    return (
        pair(left),
        pair(rim),
        diff,
        diff[:, ends][:, :, ends],
        spread_rim.astype(jnp.bfloat16),
        spread.astype(jnp.bfloat16),
    )


def halves(value):
    high = value.astype(BF16)
    low = (value - high.astype(F32)).astype(BF16)
    return high, low


def dot(a, b):
    return jnp.dot(a, b, preferred_element_type=F32)


def product(a_hi, a_lo, b):
    b_hi, b_lo = halves(b)
    return dot(a_hi, b_hi) + (dot(a_hi, b_lo) + dot(a_lo, b_hi))


def applied(m_twice, m_lo, value):
    v_hi, v_lo = halves(value)
    return dot(m_twice, jnp.concatenate([v_hi, v_lo], axis=0)) + dot(m_lo, v_hi)


def moved_rows(choice, value):
    a = value.astype(BF16)
    rest = value - a.astype(F32)
    b = rest.astype(BF16)
    c = (rest - b.astype(F32)).astype(BF16)
    return (dot(choice, c) + dot(choice, b)) + dot(choice, a)


def fluxes(diff_ref, fxx, fxy, fyy):
    d_x = diff_ref[0]
    d_y = diff_ref[1]
    return jnp.concatenate([fxx * d_x + fxy * d_y, fxy * d_x + fyy * d_y], axis=0)


def form(left_ref, diff_ref, f):
    return product(left_ref[0], left_ref[1], fluxes(diff_ref, *f))


def geometry(jac_ref, xx_ref, yy_ref, xy_ref):
    ends, inner = (float(w) for w in gll_tables()[0][0:2])
    row = lax.broadcasted_iota(jnp.int32, (PTS, EX), 0)
    along = jnp.where((row < 32) | (row >= 96), ends, inner)
    weight = jac_ref[...] * (along * jnp.where((row % 4 == 0) | (row % 4 == 3), ends, inner))
    f = (weight * xx_ref[...], weight * xy_ref[...], weight * yy_ref[...])
    up = jnp.concatenate([weight[1:], weight[:1]], axis=0)
    down = jnp.concatenate([weight[-1:], weight[:-1]], axis=0)
    mass = weight + jnp.where((row % 4 == 3) & (row % 32 != 31), up, 0.0)
    mass = mass + jnp.where((row % 4 == 0) & (row % 32 != 0), down, 0.0)
    return f, mass


def column(f, c):
    return [t[:, c : c + 1] for t in f]


def fetch(sources, buffers, sems):
    copies = [pltpu.make_async_copy(s, d, sems.at[k]) for k, (s, d) in enumerate(zip(sources, buffers))]
    for copy in copies:
        copy.start()
    return copies


def either(even, a, b):
    return jnp.where(even, a, b)


def side_columns(want_west, u_ref, f, mass, left_ref, diff_ref, rim_out_ref, layers_ref, q_ref, m_ref):
    lane = lax.broadcasted_iota(jnp.int32, (PTS, PTS), 1)
    raw, part = {}, {}
    flux = jnp.concatenate([fluxes(diff_ref, *column(f, k)) for k in range(HALO + 1)], axis=1)
    together = product(left_ref[0], left_ref[1], flux)
    for k in range(HALO + 1):
        m = together[:, PTS * k : PTS * k + PTS]
        m_ref[jnp.where(want_west, k, EX - HALO - 1 + k)] = m
        m_hi, m_lo = halves(m)
        q = product(m_hi, m_lo, u_ref[k].reshape(PTS, FL))
        for i in range(4):
            raw[k, i] = q[32 * i : 32 * i + 32]
            part[k, i] = mass[32 * i : 32 * i + 32, k : k + 1]
    for values in (raw, part):
        for k in range(HALO):
            values[k, 3] = values[k + 1, 0] = values[k, 3] + values[k + 1, 0]
    for k in range(HALO + 1):
        c = jnp.where(want_west, k, EX - HALO - 1 + k)
        for i in range(4):
            q_ref[c, i, :, 0:FL] = raw[k, i]
            q_ref[c, i, :, FL:LANES] = jnp.broadcast_to(part[k, i], (32, TAIL))
    sub = lax.broadcasted_iota(jnp.int32, (8, LANES), 0)
    for g in range(GROUPS):
        k, i = (g // 3, g % 3) if g < GROUPS - 1 else (HALO - 1, 3)
        row = either(want_west, raw[k, i], raw[k + 1, i])
        tail = jnp.broadcast_to(either(want_west, part[k, i], part[k + 1, i]), (32, TAIL))
        for lanes, value in ((slice(0, FL), row), (slice(FL, LANES), tail)):
            rim_out_ref[8 * g : 8 * g + 8, lanes] = jnp.where(sub[:, lanes] < 4, value[0:8], value[24:32])
            layers_ref[32 * g : 32 * g + 32, lanes] = value
    x = jnp.zeros((PTS, PTS), F32)
    for t in range(3):
        for k in range(HALO):
            x = jnp.where(lane == HALO * t + k, either(want_west, f[t][:, k : k + 1], f[t][:, k + 1 : k + 2]), x)
    x = jnp.transpose(x)
    rim_out_ref[RIM:SENT, 0:PTS] = x[0:8]
    rim_out_ref[RIM:SENT, PTS : 2 * PTS] = x[8:16]
    rim_out_ref[RIM:SENT, 2 * PTS :] = jnp.zeros((8, PTS), F32)


def gather_rest(layers_ref, out_ref):
    for g in range(GROUPS):
        for ey in range(1, 7):
            size = 3 if ey < 6 else 2
            to = REST * g + 3 * (ey - 1)
            at = 32 * g + 4 * ey + 1
            out_ref[to : to + size, :] = layers_ref[at : at + size, :]
    out_ref[REST * GROUPS :, :] = jnp.zeros((6, LANES), F32)


def nearest(want_west, t):
    return either(want_west, t[:, 0 : HALO + 1], t[:, EX - HALO - 1 : EX])


def first_kernel(u_hbm, jac_hbm, xx_hbm, yy_hbm, xy_hbm, left_hbm, diff_hbm, rim_hbm, near_hbm, rim_out_ref, layers_ref, other_ref, f_ref, mass_ref, left_ref, diff_ref, rim_ref, near_ref, low_ref, high_ref, q_ref, m_ref, u_ref, jac_ref, xx_ref, yy_ref, xy_ref, sems):
    want_west = even_column()
    size = HALO + 1
    here = jnp.where(want_west, 0, EX - size)
    there = jnp.where(want_west, EX - size, 0)
    copies = fetch(
        (jac_hbm, xx_hbm, yy_hbm, xy_hbm, left_hbm, diff_hbm, u_hbm.at[0, pl.ds(here, size)], u_hbm.at[0, pl.ds(there, size)], rim_hbm, near_hbm, u_hbm.at[0, :, :, 0], u_hbm.at[0, :, :, 7]),
        (jac_ref, xx_ref, yy_ref, xy_ref, left_ref, diff_ref, u_ref, other_ref, rim_ref, near_ref, low_ref, high_ref),
        sems,
    )
    for copy in copies[:6]:
        copy.wait()
    f, mass = geometry(jac_ref, xx_ref, yy_ref, xy_ref)
    for t in range(3):
        f_ref[t] = f[t]
    mass_ref[...] = mass
    copies[6].wait()
    side_columns(want_west, u_ref, [nearest(want_west, t) for t in f], nearest(want_west, mass), left_ref, diff_ref, rim_out_ref, layers_ref, q_ref, m_ref)
    for copy in copies[7:]:
        copy.wait()


def other_kernel(u_ref, f_ref, mass_ref, left_ref, diff_ref, q_in, m_in, rim_out_ref, layers_ref, q_ref, m_ref):
    del q_in, m_in
    want_west = jnp.logical_not(even_column())
    f = [nearest(want_west, f_ref[t]) for t in range(3)]
    side_columns(want_west, u_ref, f, nearest(want_west, mass_ref[...]), left_ref, diff_ref, rim_out_ref, layers_ref, q_ref, m_ref)


def rest_kernel(first_ref, other_ref, one_ref, two_ref):
    gather_rest(first_ref, one_ref)
    gather_rest(other_ref, two_ref)


def end_rows(f):
    return [jnp.concatenate([t[32 * i + a : 32 * i + a + 4] for i in range(4) for a in (0, 28)], axis=0) for t in f]


def rows_kernel(low_ref, high_ref, rim_ref, near_ref, f_ref, mass_ref, e_ref, south_ref, north_ref):
    f = end_rows([f_ref[t] for t in range(3)])
    for c in range(EX):
        e_ref[c] = form(rim_ref, near_ref, column(f, c))[0:8]
    matrices = [quad([e_ref[c + k] for k in range(4)]) for c in range(0, EX, 4)]
    mass = mass_ref[...]
    outs = (south_ref, north_ref)
    carry = [None, None]
    for c in range(0, EX, 4):
        tiles = [ref[c + k, i] for k in range(4) for i in range(4) for ref in (low_ref, high_ref)]
        r = rim_product(matrices[c // 4], jnp.concatenate(tiles, axis=0))
        for side, out in enumerate(outs):
            rows = with_carry(r, side, carry[side])
            carry[side] = rows[12:13]
            out[3 * c : 3 * c + 12, 0:FL] = rows[0:12]
    for side, (out, at) in enumerate(zip(outs, (0, 31))):
        out[48:49, 0:FL] = carry[side]
        for c in range(EX):
            for i in range(4 if c == EX - 1 else 3):
                row = 3 * c + i
                part = mass[32 * i + at : 32 * i + at + 1, c : c + 1]
                if i == 0 and c > 0:
                    part = part + mass[96 + at : 97 + at, c - 1 : c]
                out[row : row + 1, FL:LANES] = jnp.broadcast_to(part, (1, TAIL))
        out[49:56, :] = jnp.zeros((7, LANES), F32)


def quad(es):
    blocks = []
    for k, e in enumerate(es):
        rows = []
        for side in range(2):
            if k:
                rows.append(jnp.zeros((3 * k, 32), F32))
            rows.append(e[4 * side : 4 * side + 4])
            rows.append(jnp.zeros((12 - 3 * k, 32), F32))
        blocks.append(jnp.concatenate(rows, axis=0))
    high, low = halves(jnp.concatenate(blocks, axis=1))
    return jnp.concatenate(
        [jnp.concatenate([high, high], axis=1), jnp.concatenate([low, jnp.zeros_like(low)], axis=1)], axis=0
    )


def rim_product(matrix, value):
    v_hi, v_lo = halves(value)
    both = dot(matrix, jnp.concatenate([v_hi, v_lo], axis=0))
    return both[0:32] + both[32:64]


def with_carry(r, side, carry):
    rows = r[16 * side : 16 * side + 16]
    if carry is None:
        return rows
    sub = lax.broadcasted_iota(jnp.int32, rows.shape, 0)
    return rows + jnp.where(sub == 0, carry, 0.0)


def own_kernel(u_hbm, after_ref, f_ref, mass_ref, left_ref, diff_ref, q_in, m_in, q_ref, m_ref, u_ref, sems):
    del after_ref, q_in, m_in
    first, final = HALO + 1, EX - HALO - 2
    copies = fetch(
        [u_hbm.at[0, c : c + 4] for c in range(first, final, 4)], [u_ref.at[c : c + 4] for c in range(0, 8, 4)], sems
    )
    f = [f_ref[t] for t in range(3)]
    mass = mass_ref[...]
    for c in range(first, final + 1):
        m = form(left_ref, diff_ref, column(f, c))
        m_ref[c] = m
        m_hi, m_lo = halves(m)
        if (c - first) % 4 == 0:
            copies[(c - first) // 4].wait()
        q = product(m_hi, m_lo, u_ref[c - first].reshape(PTS, FL))
        for i in range(4):
            q_ref[c, i, :, 0:FL] = q[32 * i : 32 * i + 32]
            q_ref[c, i, :, FL:LANES] = jnp.broadcast_to(mass[32 * i : 32 * i + 32, c : c + 1], (32, TAIL))
        join_own(q_ref, c)
    join_own(q_ref, final + 1)


def join_own(q_ref, c):
    shared = q_ref[c - 1, 3] + q_ref[c, 0]
    q_ref[c - 1, 3] = shared
    q_ref[c, 0] = shared


def merge_kernel(one_ref, two_ref, own_south_ref, own_north_ref, south_ref, north_ref):
    even = even_column()
    for out, own, at in ((south_ref, own_south_ref, 0), (north_ref, own_north_ref, 7)):
        out[10:57, :] = own[1:48, :]
        for g in range(GROUPS - 1):
            r = 8 * g + at
            out[g : g + 1, :] = either(even, one_ref[r : r + 1, :], two_ref[r : r + 1, :])
            r = 8 * (g + 1) + at
            out[58 + g : 59 + g, :] = either(even, two_ref[r : r + 1, :], one_ref[r : r + 1, :])
        r = 8 * (GROUPS - 1) + at
        out[9:10, :] = either(even, one_ref[r : r + 1, :], two_ref[r : r + 1, :]) + own[0:1, :]
        out[57:58, :] = own[48:49, :] + either(even, two_ref[at : at + 1, :], one_ref[at : at + 1, :])
        out[67:72, :] = jnp.zeros((5, LANES), F32)


def halo_kernel(one_ref, two_ref, own_e_ref, left_ref, rim_ref, diff_ref, near_ref, m_ref, e_ref, west_ref, east_ref, quads_ref):
    even = even_column()
    west_ref[...] = either(even, one_ref[...], two_ref[...])
    east_ref[...] = either(even, two_ref[...], one_ref[...])
    for side, ref in enumerate((west_ref, east_ref)):
        x = jnp.concatenate(
            [ref[RIM:SENT, 0:PTS], ref[RIM:SENT, PTS : 2 * PTS], jnp.zeros((PTS - 16, PTS), F32)], axis=0
        )
        x = jnp.transpose(x)
        for k in range(HALO):
            fs = [x[:, HALO * t + k : HALO * t + k + 1] for t in range(3)]
            m_ref[HALO * side + k] = form(left_ref, diff_ref, fs)
            e_ref[HALO * side + k] = form(rim_ref, near_ref, end_rows(fs))[0:8]
    put_quads(rim_matrix(own_e_ref, e_ref), quads_ref)


def put_quads(matrix, quads_ref):
    for q in range(QUADS):
        columns = range(4 * q, 4 * q + 4)
        quads_ref[q] = quad([matrix(e) if e < WIDE else jnp.zeros((8, 32), F32) for e in columns])


def place():
    return lax.axis_index("face") * 64 + lax.axis_index("blk")


def even_column():
    return lax.rem(lax.div(place(), PY), 2) == 0


def has_side(side):
    return lax.rem(place(), PY) != (0, PY - 1)[side]


def edge_masks():
    sub = lax.broadcasted_iota(jnp.int32, (8, LANES), 0)
    return (sub == 0) & (has_side(0)), (sub == 7) & (has_side(1))


def first_tile(value, south_ref, row, masks):
    return value + jnp.where(masks[0], south_ref[row : row + 1, :], 0.0)


def last_tile(value, north_ref, row, masks):
    return value + jnp.where(masks[1], north_ref[row : row + 1, :], 0.0)


def column_value(part, e, lo, south_ref, north_ref, masks):
    tiles = []
    for i in range(4):
        row = 3 * (e - lo) + i
        tiles.append(first_tile(part(e, i, 0, 8), south_ref, row, masks))
        tiles.append(part(e, i, 8, 24))
        tiles.append(last_tile(part(e, i, 24, 32), north_ref, row, masks))
    return jnp.concatenate(tiles, axis=0)


def rim_value(part, e, lo, south_ref, north_ref, masks):
    tiles = []
    for i in range(4):
        row = 3 * (e - lo) + i
        tiles.append(last_tile(first_tile(part(e, i), south_ref, row, masks), north_ref, row, masks))
    return jnp.concatenate(tiles, axis=0)


def both_ends(ref, k, i):
    sub = lax.broadcasted_iota(jnp.int32, (8, LANES), 0)
    return jnp.where(sub < 4, ref[k, i, 0:8], ref[k, i, 24:32])


def group_of(k, i):
    return 3 * k + i


def rim_part(q_ref, west_ref, east_ref):
    def part(e, i):
        if (e, i) in ((HALO - 1, 3), (HALO, 0)):
            g = 8 * (GROUPS - 1)
            return west_ref[g : g + 8] + both_ends(q_ref, 0, 0)
        if (e, i) in ((HALO + EX - 1, 3), (HALO + EX, 0)):
            return both_ends(q_ref, EX - 1, 3) + east_ref[0:8]
        if HALO <= e < HALO + EX:
            return both_ends(q_ref, e - HALO, i)
        ref, k = (west_ref, e) if e < HALO else (east_ref, e - HALO - EX)
        g = 8 * group_of(k, i)
        return ref[g : g + 8]

    return part


def edges(part, lo, scales, from_south_ref, from_north_ref, quads_ref, south_ref, north_ref):
    hi = WIDE - 1 - lo
    masks = edge_masks()
    start, stop = 3 * (lo + 1), 3 * (hi - 1) + 4
    carry = [None, None]
    for q in range(QUADS):
        values = []
        for e in range(4 * q, 4 * q + 4):
            if lo <= e <= hi:
                value = rim_value(part, e, lo, from_south_ref, from_north_ref, masks)
                if scales is not None:
                    value = value * (1.0 / value[:, FL : FL + 1])
                values.append(value)
            else:
                values.append(jnp.zeros((32, LANES), F32))
        r = rim_product(quads_ref[q], jnp.concatenate(values, axis=0))
        for side, out in enumerate((south_ref, north_ref)):
            rows = with_carry(r, side, carry[side])
            carry[side] = rows[12:13]
            a, b = max(start, 12 * q), min(stop, 12 * q + 12)
            if a < b:
                rows = rows[a - 12 * q : b - 12 * q]
                if scales is not None:
                    rows = rows * scales[side][a:b]
                out[a - start : b - start, :] = rows
    for out in (south_ref, north_ref):
        out[stop - start :, :] = jnp.zeros((out.shape[0] - stop + start, LANES), F32)


def second_edges(q_ref, west_ref, east_ref, quads_ref, sent_south_ref, sent_north_ref, from_south_ref, from_north_ref, south_ref, north_ref):
    scales = []
    for side, (sent, got) in enumerate(((sent_south_ref, from_south_ref), (sent_north_ref, from_north_ref))):
        other = jnp.where(has_side(side), got[:, FL : FL + 1], 0.0)
        scales.append(1.0 / (sent[:, FL : FL + 1] + other))
    part = rim_part(q_ref, west_ref, east_ref)
    edges(part, 0, scales, from_south_ref, from_north_ref, quads_ref, south_ref, north_ref)


def rim_matrix(e_ref, halo_e_ref):
    def matrix(e):
        if HALO <= e < HALO + EX:
            return e_ref[e - HALO]
        return halo_e_ref[e if e < HALO else e - EX]

    return matrix


def third_edges(inner_ref, outer_ref, joint_ref, quads_ref, from_south_ref, from_north_ref, south_ref, north_ref):
    sub = lax.broadcasted_iota(jnp.int32, (8, LANES), 0)
    whole = split_part(inner_ref, outer_ref, joint_ref)

    def part(e, i):
        return jnp.where(sub < 4, whole(e, i, 0, 8), whole(e, i, 24, 32))

    edges(part, 1, None, from_south_ref, from_north_ref, quads_ref, south_ref, north_ref)


def fourth_edges(f_ref, quads_ref, from_south_ref, from_north_ref, south_ref, north_ref):
    def part(e, i):
        return both_ends(f_ref, e, i)

    edges(part, 2, None, from_south_ref, from_north_ref, quads_ref, south_ref, north_ref)


def join(out_ref, e, q):
    shared = out_ref[e - 1, 3] + q[0:32]
    out_ref[e - 1, 3] = shared
    out_ref[e, 0] = shared


def put(out_ref, e, first, q):
    for i in range(4):
        out_ref[e, i] = q[32 * i : 32 * i + 32]
    if e > first:
        join(out_ref, e, q)


INNER = range(HALO + 1, HALO + EX - 1)
OUTER = [e for e in range(WIDE) if e not in INNER]


def split_at(e):
    return (True, e - INNER[0]) if e in INNER else (False, OUTER.index(e))


def split_part(inner_ref, outer_ref, joint_ref):
    def part(e, i, a, b):
        if (e, i) in ((INNER[0] - 1, 3), (INNER[0], 0)):
            return joint_ref[0, a:b]
        if (e, i) in ((INNER[-1], 3), (INNER[-1] + 1, 0)):
            return joint_ref[1, a:b]
        inner, k = split_at(e)
        return (inner_ref if inner else outer_ref)[k, i, a:b]

    return part


def second_column(value, m, k, rim, out_ref, join_before, twice_ref, lo_ref, scaled_ref):
    inverse = 1.0 / value[:, FL : FL + 1]
    m_hi, m_lo = halves(m * inverse)
    twice = jnp.concatenate([m_hi, m_hi], axis=1)
    twice_ref[k] = twice
    lo_ref[k] = m_lo
    put(out_ref, k, 0 if join_before else k, applied(twice, m_lo, value * inverse))
    rows = jnp.concatenate(
        [inverse[32 * i : 32 * i + 1] for i in range(4)] + [inverse[32 * i + 31 : 32 * i + 32] for i in range(4)], axis=0
    )
    scaled_ref[k] = rim * rows


def second_inner(q_ref, e_ref, from_south_ref, from_north_ref, m_ref, out_ref, twice_ref, lo_ref, scaled_ref):
    def part(e, i, a, b):
        return q_ref[e - HALO, i, a:b]

    masks = edge_masks()
    for k, e in enumerate(INNER):
        value = column_value(part, e, 0, from_south_ref, from_north_ref, masks)
        second_column(value, m_ref[e - HALO], k, e_ref[e - HALO], out_ref, k > 0, twice_ref, lo_ref, scaled_ref)


def second_outer(q_ref, west_ref, east_ref, one_rest_ref, two_rest_ref, spread_rim_ref, spread_ref, e_ref, halo_e_ref, from_south_ref, from_north_ref, m_ref, mh_ref, inner_ref, in_e_ref, out_ref, joint_ref, twice_ref, lo_ref, scaled_ref, quads_ref):
    even = even_column()
    rests = (either(even, one_rest_ref[...], two_rest_ref[...]), either(even, two_rest_ref[...], one_rest_ref[...]))
    wide = [
        moved_rows(spread_rim_ref[...], rim[0:RIM]) + moved_rows(spread_ref[...], rest)
        for rim, rest in zip((west_ref, east_ref), rests)
    ]

    def part(e, i, a, b):
        if (e, i) in ((HALO - 1, 3), (HALO, 0)):
            g = 32 * (GROUPS - 1)
            return wide[0][g + a : g + b] + q_ref[0, 0, a:b]
        if (e, i) in ((HALO + EX - 1, 3), (HALO + EX, 0)):
            return q_ref[EX - 1, 3, a:b] + wide[1][a:b]
        if HALO <= e < HALO + EX:
            return q_ref[e - HALO, i, a:b]
        side, k = (0, e) if e < HALO else (1, e - HALO - EX)
        g = 32 * group_of(k, i)
        return wide[side][g + a : g + b]

    masks = edge_masks()
    for k, e in enumerate(OUTER):
        value = column_value(part, e, 0, from_south_ref, from_north_ref, masks)
        if e < HALO:
            m = mh_ref[e]
        elif e < HALO + EX:
            m = m_ref[e - HALO]
        else:
            m = mh_ref[e - EX]
        second_column(value, m, k, rim_matrix(e_ref, halo_e_ref)(e), out_ref, k not in (0, len(OUTER) // 2), twice_ref, lo_ref, scaled_ref)
    half = len(OUTER) // 2
    joint_ref[0] = out_ref[half - 1, 3] + inner_ref[0, 0]
    joint_ref[1] = inner_ref[len(INNER) - 1, 3] + out_ref[half, 0]

    def matrix(e):
        inner, k = split_at(e)
        return (in_e_ref if inner else scaled_ref)[k]

    put_quads(matrix, quads_ref)


def matrices(e, inner, outer):
    is_inner, k = split_at(e)
    twice_ref, lo_ref = inner if is_inner else outer
    return twice_ref[k], lo_ref[k]


def third_full(inner_ref, outer_ref, joint_ref, from_south_ref, from_north_ref, in_twice, in_lo, out_twice, out_lo, u_ref, out_ref, kept_ref):
    part = split_part(inner_ref, outer_ref, joint_ref)
    masks = edge_masks()
    for e in range(1, WIDE - 1):
        value = column_value(part, e, 1, from_south_ref, from_north_ref, masks)
        if HALO <= e < HALO + EX:
            c = e - HALO
            kept_ref[c] = u_ref[0, c].reshape(PTS, FL) - (2.0 * VISCOSITY) * value[:, 0:FL]
        put(out_ref, e, 1, applied(*matrices(e, (in_twice, in_lo), (out_twice, out_lo)), value))


def fourth_full(f_ref, from_south_ref, from_north_ref, in_twice, in_lo, out_twice, out_lo, kept_ref, out_ref, rim_south_ref, rim_north_ref, z_ref):
    def part(e, i, a, b):
        return f_ref[e, i, a:b]

    masks = edge_masks()
    for e in range(2, WIDE - 2):
        value = column_value(part, e, 2, from_south_ref, from_north_ref, masks)
        put(z_ref, e, 2, applied(*matrices(e, (in_twice, in_lo), (out_twice, out_lo)), value))
        c = e - HALO - 1
        if 0 <= c < EX:
            z = jnp.concatenate([z_ref[e - 1, i, :, 0:FL] for i in range(4)], axis=0)
            done = (kept_ref[c] + (VISCOSITY * VISCOSITY) * z).reshape(4, 8, 4, FL)
            out_ref[0, c] = done
            rim_south_ref[c] = done[:, 0]
            rim_north_ref[c] = done[:, 7]


def patch_kernel(old_ref, rim_south_ref, rim_north_ref, from_south_ref, from_north_ref, out_ref, south_buf, north_buf, sems):
    del old_ref
    sub = lax.broadcasted_iota(jnp.int32, (4, FL), 0)
    masks = ((sub == 0) & (has_side(0)), (sub == 3) & (has_side(1)))
    copies = []
    for b in range(0, EX, 4):
        for side, (rim, got, buf) in enumerate(
            ((rim_south_ref, from_south_ref, south_buf), (rim_north_ref, from_north_ref, north_buf))
        ):
            for c in range(b, b + 4):
                for i in range(4):
                    row = 3 * c + i
                    more = (VISCOSITY * VISCOSITY) * got[row : row + 1, 0:FL]
                    buf[c, i] = rim[c, i] + jnp.where(masks[side], more, 0.0)
            copies.append(
                pltpu.make_async_copy(buf.at[b : b + 4], out_ref.at[0, b : b + 4, :, 7 * side], sems.at[len(copies)])
            )
            copies[-1].start()
    for copy in copies:
        copy.wait()


VM = pl.BlockSpec(memory_space=pltpu.VMEM)
ANY = pl.BlockSpec(memory_space=pl.ANY)
HBM = pl.BlockSpec(memory_space=pltpu.HBM)


def call(body, outs, specs, name, scratch=(), out_specs=None, aliases=None):
    return pl.pallas_call(
        body,
        out_shape=[jax.ShapeDtypeStruct(s, d) for s, d in outs],
        in_specs=specs,
        out_specs=out_specs or [VM] * len(outs),
        scratch_shapes=list(scratch),
        input_output_aliases=aliases or {},
        compiler_params=pltpu.CompilerParams(vmem_limit_bytes=24 * 1024 * 1024),
        name=name,
    )


def moved(array, columns, rows):
    pairs = []
    for i in range(256):
        c, r = divmod(i, PY)
        pairs.append((i, (c + columns) % 32 * PY + (r + rows) % PY))
    return lax.ppermute(array, AXES, pairs)


def swapped(array, odd):
    pairs = []
    for i in range(256):
        c, r = divmod(i, PY)
        pairs.append((i, (((c + odd) ^ 1) - odd) % 32 * PY + r))
    return lax.ppermute(array, AXES, pairs)


def across(to_south, to_north):
    return moved(to_north, 0, 1), moved(to_south, 0, -1)


def per_device(state, jacobian, metric_xx, metric_yy, metric_xy):
    left, rim, diff, near, spread_rim, spread = (jnp.asarray(t) for t in tables())
    flat = [jnp.transpose(g[0], (1, 2, 3, 0)).reshape(PTS, EX) for g in (jacobian, metric_xx, metric_yy, metric_xy)]
    rows = lambda n: ((n, LANES), F32)
    wide = ((WIDE, 4, 32, LANES), F32)
    pinned = lambda *ts: [pltpu.with_memory_space_constraint(t, pltpu.HBM) for t in ts]
    four = (HALO + 1, 4, 8, 4, FL)

    own = [((EX, 4, 32, LANES), F32), ((EX, PTS, PTS), F32)]
    rim_one, layers_one, other, f, mass, left_in, diff_in, rim_in, near_in, low, high, q, m = call(
        first_kernel,
        [rows(SENT), rows(32 * GROUPS), (four, F32), ((3, PTS, EX), F32), ((PTS, EX), F32), (left.shape, BF16), (diff.shape, F32), (rim.shape, BF16), (near.shape, F32), *[((EX, 4, 4, FL), F32)] * 2, *own],
        [HBM] * 9,
        "first",
        scratch=[pltpu.VMEM(four, F32), *[pltpu.VMEM((PTS, EX), F32)] * 4, pltpu.SemaphoreType.DMA((12,))],
    )(*pinned(state, *flat, left, diff, rim, near))
    one = swapped(rim_one, 1)
    rim_two, layers_two, q, m = call(
        other_kernel, [rows(SENT), rows(32 * GROUPS), *own], [VM] * 7, "other", aliases={5: 2, 6: 3}
    )(other, f, mass, left_in, diff_in, q, m)
    two = swapped(rim_two, 0)
    rest_one, rest_two = call(rest_kernel, [rows(176)] * 2, [VM] * 2, "rest")(layers_one, layers_two)
    rest_one = swapped(rest_one, 1)
    rest_two = swapped(rest_two, 0)
    e, own_south, own_north = call(
        rows_kernel,
        [((EX, 8, 32), F32), rows(56), rows(56)],
        [VM] * 6,
        "rows",
    )(low, high, rim_in, near_in, f, mass)
    to_south, to_north = call(merge_kernel, [rows(72)] * 2, [VM] * 4, "merge")(one, two, own_south, own_north)
    south1, north1 = across(to_south, to_north)
    q, m = call(
        own_kernel,
        own,
        [HBM, ANY] + [VM] * 6,
        "own",
        scratch=[pltpu.VMEM((8, 4, 8, 4, FL), F32), pltpu.SemaphoreType.DMA((2,))],
        aliases={6: 0, 7: 1},
    )(*pinned(state), to_south, f, mass, left_in, diff_in, q, m)
    mh, halo_e, west, east, quads = call(
        halo_kernel,
        [((2 * HALO, PTS, PTS), F32), ((2 * HALO, 8, 32), F32), rows(SENT), rows(SENT), ((QUADS, 64, 2 * PTS), BF16)],
        [VM] * 7,
        "halo",
    )(one, two, e, left_in, rim_in, diff_in, near_in)
    to_south, to_north = call(second_edges, [rows(64)] * 2, [VM] * 8, "edges2")(
        q, west, east, quads, to_south, to_north, south1, north1
    )
    south2, north2 = across(to_south, to_north)
    matrix = lambda n: [((n, PTS, 2 * PTS), BF16), ((n, PTS, PTS), BF16), ((n, 8, 32), F32)]
    inner, in_twice, in_lo, in_e = call(
        second_inner, [((14, 4, 32, LANES), F32), *matrix(14)], [VM] * 5, "inner2"
    )(q, e, south1, north1, m)
    outer, joint, out_twice, out_lo, _, quads = call(
        second_outer, [((8, 4, 32, LANES), F32), ((2, 32, LANES), F32), *matrix(8), ((QUADS, 64, 2 * PTS), BF16)], [VM] * 15, "outer2"
    )(q, west, east, rest_one, rest_two, spread_rim, spread, e, halo_e, south1, north1, m, mh, inner, in_e)
    to_south, to_north = call(third_edges, [rows(56)] * 2, [VM] * 6, "edges3")(
        inner, outer, joint, quads, south2, north2
    )
    south3, north3 = across(to_south, to_north)
    f, kept = call(third_full, [wide, ((EX, PTS, FL), F32)], [VM] * 10, "full3")(
        inner, outer, joint, south2, north2, in_twice, in_lo, out_twice, out_lo, state
    )
    to_south, to_north = call(fourth_edges, [rows(56)] * 2, [VM] * 4, "edges4")(
        f, quads, south3, north3
    )
    south4, north4 = across(to_south, to_north)
    out, rim_south, rim_north = call(
        fourth_full,
        [((1, EX, 4, 8, 4, FL), F32), ((EX, 4, 4, FL), F32), ((EX, 4, 4, FL), F32)],
        [VM] * 8,
        "full4",
        scratch=[pltpu.VMEM((WIDE, 4, 32, LANES), F32)],
    )(f, south3, north3, in_twice, in_lo, out_twice, out_lo, kept)
    (out,) = call(
        patch_kernel,
        [((1, EX, 4, 8, 4, FL), F32)],
        [ANY] + [VM] * 4,
        "patch",
        scratch=[pltpu.VMEM((EX, 4, 4, FL), F32), pltpu.VMEM((EX, 4, 4, FL), F32), pltpu.SemaphoreType.DMA((8,))],
        out_specs=[ANY],
        aliases={0: 0},
    )(out, rim_south, rim_north, south4, north4)
    return out


def solution(mesh):
    spec = P(AXES)
    return jax.shard_map(per_device, mesh=mesh, in_specs=(spec,) * 5, out_specs=spec, check_vma=False)
```

```python
import math

import jax
import jax.numpy as jnp
import numpy as np
from jax import lax
from jax.experimental import pallas as pl
from jax.experimental.pallas import tpu as pltpu
from jax.sharding import PartitionSpec as P

PY = 8
EX = 16
FL = 360
LANES = 384
PTS = 128
HALO = 3
WIDE = EX + 2 * HALO
GROUPS = 3 * HALO + 1
LINE = 25
RIM = 8 * GROUPS
REST = 17
ROWS = REST * GROUPS
USED = FL + 1 - 256
SHARE = USED // 5
FULL = 142
PACKED = 488
TAIL = LANES - FL
QUADS = -(-WIDE // 4)
AXES = ("face", "blk")
VISCOSITY = 1e-4
F32 = jnp.float32
BF16 = jnp.bfloat16


def gll_tables():
    root = 1.0 / math.sqrt(5.0)
    points = np.array([-1.0, -root, root, 1.0])
    weights = np.array([1.0 / 6.0, 5.0 / 6.0, 5.0 / 6.0, 1.0 / 6.0])
    scales = np.array(
        [np.prod([points[t] - points[o] for o in range(4) if o != t]) for t in range(4)]
    )
    derivative = np.zeros((4, 4))
    for t in range(4):
        for s in range(4):
            if t != s:
                derivative[t, s] = scales[t] / (scales[s] * (points[t] - points[s]))
        derivative[t, t] = -np.sum(derivative[t])
    return weights, derivative


def tables():
    derivative = gll_tables()[1]
    d_x = np.kron(derivative, np.eye(32))
    d_y = np.kron(np.eye(32), derivative)
    share = np.eye(PTS)
    for r in range(PTS):
        if r % 4 == 3 and r % 32 != 31:
            share[r, r + 1] = 1.0
            share[r + 1, r] = 1.0
    left = (-share @ np.concatenate([d_x.T, d_y.T], axis=1)).astype(np.float32)
    ends = np.concatenate([np.r_[32 * i : 32 * i + 4, 32 * i + 28 : 32 * i + 32] for i in range(4)])
    rim = np.zeros((16, 64), np.float32)
    rim[0:4] = left[0::32][:, np.concatenate([ends, PTS + ends])]
    rim[4:8] = left[31::32][:, np.concatenate([ends, PTS + ends])]
    diff = np.stack([d_x, d_y]).astype(np.float32)
    spread_rim = np.zeros((32 * GROUPS, RIM), np.float32)
    spread = np.zeros((32 * GROUPS, 176), np.float32)
    for g in range(GROUPS):
        for ey in range(8):
            for j in range(4):
                k = 3 * ey + j
                row = 32 * g + 4 * ey + j
                if k < 4:
                    spread_rim[row, 8 * g + k] = 1.0
                elif k > 20:
                    spread_rim[row, 8 * g + k - 17] = 1.0
                else:
                    spread[row, REST * g + k - 4] = 1.0

    def pair(a):
        high = a.astype(jnp.bfloat16)
        return np.stack([high, (a - high.astype(np.float32)).astype(jnp.bfloat16)])

    return (
        pair(left),
        pair(rim),
        diff,
        diff[:, ends][:, :, ends],
        spread_rim.astype(jnp.bfloat16),
        spread.astype(jnp.bfloat16),
    )


def halves(value):
    high = value.astype(BF16)
    low = (value - high.astype(F32)).astype(BF16)
    return high, low


def dot(a, b):
    return jnp.dot(a, b, preferred_element_type=F32)


def product(a_hi, a_lo, b):
    b_hi, b_lo = halves(b)
    return dot(a_hi, b_hi) + (dot(a_hi, b_lo) + dot(a_lo, b_hi))


def applied(m_twice, m_lo, value):
    v_hi, v_lo = halves(value)
    return dot(m_twice, jnp.concatenate([v_hi, v_lo], axis=0)) + dot(m_lo, v_hi)


def moved_rows(choice, value):
    a = value.astype(BF16)
    rest = value - a.astype(F32)
    b = rest.astype(BF16)
    c = (rest - b.astype(F32)).astype(BF16)
    return (dot(choice, c) + dot(choice, b)) + dot(choice, a)


def fluxes(diff_ref, fxx, fxy, fyy):
    d_x = diff_ref[0]
    d_y = diff_ref[1]
    return jnp.concatenate([fxx * d_x + fxy * d_y, fxy * d_x + fyy * d_y], axis=0)


def form(left_ref, diff_ref, f):
    return product(left_ref[0], left_ref[1], fluxes(diff_ref, *f))


def geometry(jac_ref, xx_ref, yy_ref, xy_ref):
    ends, inner = (float(w) for w in gll_tables()[0][0:2])
    row = lax.broadcasted_iota(jnp.int32, (PTS, EX), 0)
    along = jnp.where((row < 32) | (row >= 96), ends, inner)
    weight = jac_ref[...] * (along * jnp.where((row % 4 == 0) | (row % 4 == 3), ends, inner))
    f = (weight * xx_ref[...], weight * xy_ref[...], weight * yy_ref[...])
    up = jnp.concatenate([weight[1:], weight[:1]], axis=0)
    down = jnp.concatenate([weight[-1:], weight[:-1]], axis=0)
    mass = weight + jnp.where((row % 4 == 3) & (row % 32 != 31), up, 0.0)
    mass = mass + jnp.where((row % 4 == 0) & (row % 32 != 0), down, 0.0)
    return f, mass


def column(f, c):
    return [t[:, c : c + 1] for t in f]


def fetch(sources, buffers, sems):
    copies = [pltpu.make_async_copy(s, d, sems.at[k]) for k, (s, d) in enumerate(zip(sources, buffers))]
    for copy in copies:
        copy.start()
    return copies


def either(even, a, b):
    return jnp.where(even, a, b)


def side_columns(want_west, u_ref, f, mass, left_ref, diff_ref, rim_out_ref, layers_ref, q_ref, m_ref):
    raw, part = {}, {}
    flux = jnp.concatenate([fluxes(diff_ref, *column(f, k)) for k in range(HALO + 1)], axis=1)
    together = product(left_ref[0], left_ref[1], flux)
    for k in range(HALO + 1):
        m = together[:, PTS * k : PTS * k + PTS]
        m_ref[jnp.where(want_west, k, EX - HALO - 1 + k)] = m
        m_hi, m_lo = halves(m)
        q = product(m_hi, m_lo, u_ref[k].reshape(PTS, FL))
        for i in range(4):
            raw[k, i] = q[32 * i : 32 * i + 32]
            part[k, i] = mass[32 * i : 32 * i + 32, k : k + 1]
    for values in (raw, part):
        for k in range(HALO):
            values[k, 3] = values[k + 1, 0] = values[k, 3] + values[k + 1, 0]
    for k in range(HALO + 1):
        c = jnp.where(want_west, k, EX - HALO - 1 + k)
        for i in range(4):
            q_ref[c, i, :, 0:FL] = raw[k, i]
            q_ref[c, i, :, FL:LANES] = jnp.broadcast_to(part[k, i], (32, TAIL))
    sub = lax.broadcasted_iota(jnp.int32, (8, LANES), 0)
    for g in range(GROUPS):
        k, i = (g // 3, g % 3) if g < GROUPS - 1 else (HALO - 1, 3)
        row = either(want_west, raw[k, i], raw[k + 1, i])
        tail = jnp.broadcast_to(either(want_west, part[k, i], part[k + 1, i]), (32, TAIL))
        for lanes, value in ((slice(0, FL), row), (slice(FL, LANES), tail)):
            rim_out_ref[8 * g : 8 * g + 8, lanes] = jnp.where(sub[:, lanes] < 4, value[0:8], value[24:32])
            layers_ref[32 * g : 32 * g + 32, lanes] = value
    at = FL + 1
    for t in range(3):
        for k in range(HALO):
            value = either(want_west, f[t][:, k : k + 1], f[t][:, k + 1 : k + 2])
            rim_out_ref[:, at : at + 1] = value[0:RIM]
            rim_out_ref[0 : PTS - RIM, at + 9 : at + 10] = value[RIM:PTS]
            at += 1


def gather_rest(layers_ref, out_ref, third_ref):
    for g in range(GROUPS):
        for ey in range(1, 7):
            size = 3 if ey < 6 else 2
            to = REST * g + 3 * (ey - 1)
            at = 32 * g + 4 * ey + 1
            out_ref[to : to + size, :] = layers_ref[at : at + size, 0:128]
            out_ref[ROWS + to : ROWS + to + size, :] = layers_ref[at : at + size, 128:256]
            third_ref[to : to + size, :] = layers_ref[at : at + size, 256:384]
    last = third_ref[FULL:ROWS, :]
    size = ROWS - FULL
    lane = lax.broadcasted_iota(jnp.int32, (size, 128), 1)
    for p in range(5):
        shifted = pltpu.roll(last, USED - SHARE * p, 1)
        rows = slice(size * p, size * p + size)
        out_ref[2 * ROWS + rows.start : 2 * ROWS + rows.stop, :] = jnp.where(lane < USED, third_ref[rows, :], shifted)
    out_ref[2 * ROWS + 5 * size : 2 * ROWS + FULL, :] = third_ref[5 * size : FULL, :]
    out_ref[2 * ROWS + FULL :, :] = jnp.zeros((PACKED - 2 * ROWS - FULL, 128), F32)


def unpack_rest(got, out_ref):
    size = ROWS - FULL
    lane = lax.broadcasted_iota(jnp.int32, (size, 128), 1)
    out_ref[0:ROWS, 0:128] = got[0:ROWS]
    out_ref[0:ROWS, 128:256] = got[ROWS : 2 * ROWS]
    out_ref[0:FULL, 256:384] = got[2 * ROWS : 2 * ROWS + FULL]
    last = jnp.zeros((size, 128), F32)
    for p in range(5):
        at = 2 * ROWS + size * p
        shifted = pltpu.roll(got[at : at + size], 128 - (USED - SHARE * p), 1)
        last = jnp.where((lane >= SHARE * p) & (lane < SHARE * p + SHARE), shifted, last)
    out_ref[FULL:ROWS, 256:384] = last
    out_ref[ROWS:, :] = jnp.zeros((out_ref.shape[0] - ROWS, LANES), F32)


def nearest(want_west, t):
    return either(want_west, t[:, 0 : HALO + 1], t[:, EX - HALO - 1 : EX])


def first_kernel(u_hbm, jac_hbm, xx_hbm, yy_hbm, xy_hbm, left_hbm, diff_hbm, rim_hbm, near_hbm, rim_out_ref, layers_ref, other_ref, f_ref, mass_ref, left_ref, diff_ref, rim_ref, near_ref, low_ref, high_ref, q_ref, m_ref, u_ref, jac_ref, xx_ref, yy_ref, xy_ref, sems):
    want_west = even_column()
    size = HALO + 1
    here = jnp.where(want_west, 0, EX - size)
    there = jnp.where(want_west, EX - size, 0)
    copies = fetch(
        (jac_hbm, xx_hbm, yy_hbm, xy_hbm, left_hbm, diff_hbm, u_hbm.at[0, pl.ds(here, size)], u_hbm.at[0, pl.ds(there, size)], rim_hbm, near_hbm, u_hbm.at[0, :, :, 0], u_hbm.at[0, :, :, 7]),
        (jac_ref, xx_ref, yy_ref, xy_ref, left_ref, diff_ref, u_ref, other_ref, rim_ref, near_ref, low_ref, high_ref),
        sems,
    )
    for copy in copies[:6]:
        copy.wait()
    f, mass = geometry(jac_ref, xx_ref, yy_ref, xy_ref)
    for t in range(3):
        f_ref[t] = f[t]
    mass_ref[...] = mass
    copies[6].wait()
    side_columns(want_west, u_ref, [nearest(want_west, t) for t in f], nearest(want_west, mass), left_ref, diff_ref, rim_out_ref, layers_ref, q_ref, m_ref)
    for copy in copies[7:]:
        copy.wait()


def other_kernel(u_ref, f_ref, mass_ref, left_ref, diff_ref, q_in, m_in, rim_out_ref, layers_ref, q_ref, m_ref):
    del q_in, m_in
    want_west = jnp.logical_not(even_column())
    f = [nearest(want_west, f_ref[t]) for t in range(3)]
    side_columns(want_west, u_ref, f, nearest(want_west, mass_ref[...]), left_ref, diff_ref, rim_out_ref, layers_ref, q_ref, m_ref)


def rest_kernel(first_ref, other_ref, one_ref, two_ref, third_ref):
    gather_rest(first_ref, one_ref, third_ref)
    gather_rest(other_ref, two_ref, third_ref)


def end_rows(f):
    return [jnp.concatenate([t[32 * i + a : 32 * i + a + 4] for i in range(4) for a in (0, 28)], axis=0) for t in f]


def rows_kernel(low_ref, high_ref, rim_ref, near_ref, f_ref, mass_ref, e_ref, south_ref, north_ref):
    f = end_rows([f_ref[t] for t in range(3)])
    for c in range(EX):
        e_ref[c] = form(rim_ref, near_ref, column(f, c))[0:8]
    matrices = [quad([e_ref[c + k] for k in range(4)]) for c in range(0, EX, 4)]
    mass = mass_ref[...]
    outs = (south_ref, north_ref)
    carry = [None, None]
    for c in range(0, EX, 4):
        tiles = [ref[c + k, i] for k in range(4) for i in range(4) for ref in (low_ref, high_ref)]
        r = rim_product(matrices[c // 4], jnp.concatenate(tiles, axis=0))
        for side, out in enumerate(outs):
            rows = with_carry(r, side, carry[side])
            carry[side] = rows[12:13]
            out[3 * c : 3 * c + 12, 0:FL] = rows[0:12]
    for side, (out, at) in enumerate(zip(outs, (0, 31))):
        out[48:49, 0:FL] = carry[side]
        for c in range(EX):
            for i in range(4 if c == EX - 1 else 3):
                row = 3 * c + i
                part = mass[32 * i + at : 32 * i + at + 1, c : c + 1]
                if i == 0 and c > 0:
                    part = part + mass[96 + at : 97 + at, c - 1 : c]
                out[row : row + 1, FL:LANES] = jnp.broadcast_to(part, (1, TAIL))
        out[49:56, :] = jnp.zeros((7, LANES), F32)


def quad(es):
    blocks = []
    for k, e in enumerate(es):
        rows = []
        for side in range(2):
            if k:
                rows.append(jnp.zeros((3 * k, 32), F32))
            rows.append(e[4 * side : 4 * side + 4])
            rows.append(jnp.zeros((12 - 3 * k, 32), F32))
        blocks.append(jnp.concatenate(rows, axis=0))
    high, low = halves(jnp.concatenate(blocks, axis=1))
    return jnp.concatenate(
        [jnp.concatenate([high, high], axis=1), jnp.concatenate([low, jnp.zeros_like(low)], axis=1)], axis=0
    )


def rim_product(matrix, value):
    v_hi, v_lo = halves(value)
    both = dot(matrix, jnp.concatenate([v_hi, v_lo], axis=0))
    return both[0:32] + both[32:64]


def with_carry(r, side, carry):
    rows = r[16 * side : 16 * side + 16]
    if carry is None:
        return rows
    sub = lax.broadcasted_iota(jnp.int32, rows.shape, 0)
    return rows + jnp.where(sub == 0, carry, 0.0)


def own_kernel(u_hbm, after_ref, f_ref, mass_ref, left_ref, diff_ref, q_in, m_in, q_ref, m_ref, u_ref, sems):
    del after_ref, q_in, m_in
    first, final = HALO + 1, EX - HALO - 2
    copies = fetch(
        [u_hbm.at[0, c : c + 4] for c in range(first, final, 4)], [u_ref.at[c : c + 4] for c in range(0, 8, 4)], sems
    )
    f = [f_ref[t] for t in range(3)]
    mass = mass_ref[...]
    for c in range(first, final + 1):
        m = form(left_ref, diff_ref, column(f, c))
        m_ref[c] = m
        m_hi, m_lo = halves(m)
        if (c - first) % 4 == 0:
            copies[(c - first) // 4].wait()
        q = product(m_hi, m_lo, u_ref[c - first].reshape(PTS, FL))
        for i in range(4):
            q_ref[c, i, :, 0:FL] = q[32 * i : 32 * i + 32]
            q_ref[c, i, :, FL:LANES] = jnp.broadcast_to(mass[32 * i : 32 * i + 32, c : c + 1], (32, TAIL))
        join_own(q_ref, c)
    join_own(q_ref, final + 1)


def join_own(q_ref, c):
    shared = q_ref[c - 1, 3] + q_ref[c, 0]
    q_ref[c - 1, 3] = shared
    q_ref[c, 0] = shared


def merge_kernel(one_ref, two_ref, own_south_ref, own_north_ref, south_ref, north_ref):
    even = even_column()
    for out, own, at in ((south_ref, own_south_ref, 0), (north_ref, own_north_ref, 7)):
        out[10:57, :] = own[1:48, :]
        for g in range(GROUPS - 1):
            r = 8 * g + at
            out[g : g + 1, :] = either(even, one_ref[r : r + 1, :], two_ref[r : r + 1, :])
            r = 8 * (g + 1) + at
            out[58 + g : 59 + g, :] = either(even, two_ref[r : r + 1, :], one_ref[r : r + 1, :])
        r = 8 * (GROUPS - 1) + at
        out[9:10, :] = either(even, one_ref[r : r + 1, :], two_ref[r : r + 1, :]) + own[0:1, :]
        out[57:58, :] = own[48:49, :] + either(even, two_ref[at : at + 1, :], one_ref[at : at + 1, :])
        out[67:72, :] = jnp.zeros((5, LANES), F32)


def halo_kernel(one_ref, two_ref, own_e_ref, left_ref, rim_ref, diff_ref, near_ref, m_ref, e_ref, west_ref, east_ref, quads_ref):
    even = even_column()
    west_ref[...] = either(even, one_ref[...], two_ref[...])
    east_ref[...] = either(even, two_ref[...], one_ref[...])
    for side, ref in enumerate((west_ref, east_ref)):
        at = FL + 1
        for k in range(HALO):
            lanes = [at + HALO * t + k for t in range(3)]
            fs = [jnp.concatenate([ref[:, a : a + 1], ref[0 : PTS - RIM, a + 9 : a + 10]], axis=0) for a in lanes]
            m_ref[HALO * side + k] = form(left_ref, diff_ref, fs)
            e_ref[HALO * side + k] = form(rim_ref, near_ref, end_rows(fs))[0:8]
    put_quads(rim_matrix(own_e_ref, e_ref), quads_ref)


def put_quads(matrix, quads_ref):
    for q in range(QUADS):
        columns = range(4 * q, 4 * q + 4)
        quads_ref[q] = quad([matrix(e) if e < WIDE else jnp.zeros((8, 32), F32) for e in columns])


def place():
    return lax.axis_index("face") * 64 + lax.axis_index("blk")


def even_column():
    return lax.rem(lax.div(place(), PY), 2) == 0


def has_side(side):
    return lax.rem(place(), PY) != (0, PY - 1)[side]


def edge_masks():
    sub = lax.broadcasted_iota(jnp.int32, (8, LANES), 0)
    return (sub == 0) & (has_side(0)), (sub == 7) & (has_side(1))


def first_tile(value, south_ref, row, masks):
    return value + jnp.where(masks[0], south_ref[row : row + 1, :], 0.0)


def last_tile(value, north_ref, row, masks):
    return value + jnp.where(masks[1], north_ref[row : row + 1, :], 0.0)


def column_value(part, e, lo, south_ref, north_ref, masks):
    tiles = []
    for i in range(4):
        row = 3 * (e - lo) + i
        tiles.append(first_tile(part(e, i, 0, 8), south_ref, row, masks))
        tiles.append(part(e, i, 8, 24))
        tiles.append(last_tile(part(e, i, 24, 32), north_ref, row, masks))
    return jnp.concatenate(tiles, axis=0)


def rim_value(part, e, lo, south_ref, north_ref, masks):
    tiles = []
    for i in range(4):
        row = 3 * (e - lo) + i
        tiles.append(last_tile(first_tile(part(e, i), south_ref, row, masks), north_ref, row, masks))
    return jnp.concatenate(tiles, axis=0)


def both_ends(ref, k, i):
    sub = lax.broadcasted_iota(jnp.int32, (8, LANES), 0)
    return jnp.where(sub < 4, ref[k, i, 0:8], ref[k, i, 24:32])


def group_of(k, i):
    return 3 * k + i


def rim_part(q_ref, west_ref, east_ref):
    def part(e, i):
        if (e, i) in ((HALO - 1, 3), (HALO, 0)):
            g = 8 * (GROUPS - 1)
            return west_ref[g : g + 8] + both_ends(q_ref, 0, 0)
        if (e, i) in ((HALO + EX - 1, 3), (HALO + EX, 0)):
            return both_ends(q_ref, EX - 1, 3) + east_ref[0:8]
        if HALO <= e < HALO + EX:
            return both_ends(q_ref, e - HALO, i)
        ref, k = (west_ref, e) if e < HALO else (east_ref, e - HALO - EX)
        g = 8 * group_of(k, i)
        return ref[g : g + 8]

    return part


def edges(part, lo, scales, from_south_ref, from_north_ref, quads_ref, south_ref, north_ref):
    hi = WIDE - 1 - lo
    masks = edge_masks()
    start, stop = 3 * (lo + 1), 3 * (hi - 1) + 4
    carry = [None, None]
    for q in range(QUADS):
        values = []
        for e in range(4 * q, 4 * q + 4):
            if lo <= e <= hi:
                value = rim_value(part, e, lo, from_south_ref, from_north_ref, masks)
                if scales is not None:
                    value = value * (1.0 / value[:, FL : FL + 1])
                values.append(value)
            else:
                values.append(jnp.zeros((32, LANES), F32))
        r = rim_product(quads_ref[q], jnp.concatenate(values, axis=0))
        for side, out in enumerate((south_ref, north_ref)):
            rows = with_carry(r, side, carry[side])
            carry[side] = rows[12:13]
            a, b = max(start, 12 * q), min(stop, 12 * q + 12)
            if a < b:
                rows = rows[a - 12 * q : b - 12 * q]
                if scales is not None:
                    rows = rows * scales[side][a:b]
                out[a - start : b - start, :] = rows
    for out in (south_ref, north_ref):
        out[stop - start :, :] = jnp.zeros((out.shape[0] - stop + start, LANES), F32)


def second_edges(q_ref, west_ref, east_ref, quads_ref, sent_south_ref, sent_north_ref, from_south_ref, from_north_ref, south_ref, north_ref):
    scales = []
    for side, (sent, got) in enumerate(((sent_south_ref, from_south_ref), (sent_north_ref, from_north_ref))):
        other = jnp.where(has_side(side), got[:, FL : FL + 1], 0.0)
        scales.append(1.0 / (sent[:, FL : FL + 1] + other))
    part = rim_part(q_ref, west_ref, east_ref)
    edges(part, 0, scales, from_south_ref, from_north_ref, quads_ref, south_ref, north_ref)


def rim_matrix(e_ref, halo_e_ref):
    def matrix(e):
        if HALO <= e < HALO + EX:
            return e_ref[e - HALO]
        return halo_e_ref[e if e < HALO else e - EX]

    return matrix


def third_edges(inner_ref, outer_ref, joint_ref, quads_ref, from_south_ref, from_north_ref, south_ref, north_ref):
    sub = lax.broadcasted_iota(jnp.int32, (8, LANES), 0)
    whole = split_part(inner_ref, outer_ref, joint_ref)

    def part(e, i):
        return jnp.where(sub < 4, whole(e, i, 0, 8), whole(e, i, 24, 32))

    edges(part, 1, None, from_south_ref, from_north_ref, quads_ref, south_ref, north_ref)


def fourth_edges(f_ref, quads_ref, from_south_ref, from_north_ref, south_ref, north_ref):
    def part(e, i):
        return both_ends(f_ref, e, i)

    edges(part, 2, None, from_south_ref, from_north_ref, quads_ref, south_ref, north_ref)


def join(out_ref, e, q):
    shared = out_ref[e - 1, 3] + q[0:32]
    out_ref[e - 1, 3] = shared
    out_ref[e, 0] = shared


def put(out_ref, e, first, q):
    for i in range(4):
        out_ref[e, i] = q[32 * i : 32 * i + 32]
    if e > first:
        join(out_ref, e, q)


INNER = range(HALO + 1, HALO + EX - 1)
OUTER = [e for e in range(WIDE) if e not in INNER]


def split_at(e):
    return (True, e - INNER[0]) if e in INNER else (False, OUTER.index(e))


def split_part(inner_ref, outer_ref, joint_ref):
    def part(e, i, a, b):
        if (e, i) in ((INNER[0] - 1, 3), (INNER[0], 0)):
            return joint_ref[0, a:b]
        if (e, i) in ((INNER[-1], 3), (INNER[-1] + 1, 0)):
            return joint_ref[1, a:b]
        inner, k = split_at(e)
        return (inner_ref if inner else outer_ref)[k, i, a:b]

    return part


def second_column(value, m, k, rim, out_ref, join_before, twice_ref, lo_ref, scaled_ref):
    inverse = 1.0 / value[:, FL : FL + 1]
    m_hi, m_lo = halves(m * inverse)
    twice = jnp.concatenate([m_hi, m_hi], axis=1)
    twice_ref[k] = twice
    lo_ref[k] = m_lo
    put(out_ref, k, 0 if join_before else k, applied(twice, m_lo, value * inverse))
    rows = jnp.concatenate(
        [inverse[32 * i : 32 * i + 1] for i in range(4)] + [inverse[32 * i + 31 : 32 * i + 32] for i in range(4)], axis=0
    )
    scaled_ref[k] = rim * rows


def second_inner(q_ref, e_ref, from_south_ref, from_north_ref, m_ref, out_ref, twice_ref, lo_ref, scaled_ref):
    def part(e, i, a, b):
        return q_ref[e - HALO, i, a:b]

    masks = edge_masks()
    for k, e in enumerate(INNER):
        value = column_value(part, e, 0, from_south_ref, from_north_ref, masks)
        second_column(value, m_ref[e - HALO], k, e_ref[e - HALO], out_ref, k > 0, twice_ref, lo_ref, scaled_ref)


def second_outer(q_ref, west_ref, east_ref, one_rest_ref, two_rest_ref, spread_rim_ref, spread_ref, e_ref, halo_e_ref, from_south_ref, from_north_ref, m_ref, mh_ref, inner_ref, in_e_ref, out_ref, joint_ref, twice_ref, lo_ref, scaled_ref, quads_ref, rest_a, rest_b):
    even = even_column()
    unpack_rest(either(even, one_rest_ref[...], two_rest_ref[...]), rest_a)
    unpack_rest(either(even, two_rest_ref[...], one_rest_ref[...]), rest_b)
    rests = (rest_a[...], rest_b[...])
    wide = [
        moved_rows(spread_rim_ref[...], rim[...]) + moved_rows(spread_ref[...], rest)
        for rim, rest in zip((west_ref, east_ref), rests)
    ]

    def part(e, i, a, b):
        if (e, i) in ((HALO - 1, 3), (HALO, 0)):
            g = 32 * (GROUPS - 1)
            return wide[0][g + a : g + b] + q_ref[0, 0, a:b]
        if (e, i) in ((HALO + EX - 1, 3), (HALO + EX, 0)):
            return q_ref[EX - 1, 3, a:b] + wide[1][a:b]
        if HALO <= e < HALO + EX:
            return q_ref[e - HALO, i, a:b]
        side, k = (0, e) if e < HALO else (1, e - HALO - EX)
        g = 32 * group_of(k, i)
        return wide[side][g + a : g + b]

    masks = edge_masks()
    for k, e in enumerate(OUTER):
        value = column_value(part, e, 0, from_south_ref, from_north_ref, masks)
        if e < HALO:
            m = mh_ref[e]
        elif e < HALO + EX:
            m = m_ref[e - HALO]
        else:
            m = mh_ref[e - EX]
        second_column(value, m, k, rim_matrix(e_ref, halo_e_ref)(e), out_ref, k not in (0, len(OUTER) // 2), twice_ref, lo_ref, scaled_ref)
    half = len(OUTER) // 2
    joint_ref[0] = out_ref[half - 1, 3] + inner_ref[0, 0]
    joint_ref[1] = inner_ref[len(INNER) - 1, 3] + out_ref[half, 0]

    def matrix(e):
        inner, k = split_at(e)
        return (in_e_ref if inner else scaled_ref)[k]

    put_quads(matrix, quads_ref)


def matrices(e, inner, outer):
    is_inner, k = split_at(e)
    twice_ref, lo_ref = inner if is_inner else outer
    return twice_ref[k], lo_ref[k]


def third_full(inner_ref, outer_ref, joint_ref, from_south_ref, from_north_ref, in_twice, in_lo, out_twice, out_lo, u_ref, out_ref, kept_ref):
    part = split_part(inner_ref, outer_ref, joint_ref)
    masks = edge_masks()
    for e in range(1, WIDE - 1):
        value = column_value(part, e, 1, from_south_ref, from_north_ref, masks)
        if HALO <= e < HALO + EX:
            c = e - HALO
            kept_ref[c] = u_ref[0, c].reshape(PTS, FL) - (2.0 * VISCOSITY) * value[:, 0:FL]
        put(out_ref, e, 1, applied(*matrices(e, (in_twice, in_lo), (out_twice, out_lo)), value))


def fourth_full(f_ref, from_south_ref, from_north_ref, in_twice, in_lo, out_twice, out_lo, kept_ref, out_ref, rim_south_ref, rim_north_ref, z_ref):
    def part(e, i, a, b):
        return f_ref[e, i, a:b]

    masks = edge_masks()
    for e in range(2, WIDE - 2):
        value = column_value(part, e, 2, from_south_ref, from_north_ref, masks)
        put(z_ref, e, 2, applied(*matrices(e, (in_twice, in_lo), (out_twice, out_lo)), value))
        c = e - HALO - 1
        if 0 <= c < EX:
            z = jnp.concatenate([z_ref[e - 1, i, :, 0:FL] for i in range(4)], axis=0)
            done = (kept_ref[c] + (VISCOSITY * VISCOSITY) * z).reshape(4, 8, 4, FL)
            out_ref[0, c] = done
            rim_south_ref[c] = done[:, 0]
            rim_north_ref[c] = done[:, 7]


def patch_kernel(old_ref, rim_south_ref, rim_north_ref, from_south_ref, from_north_ref, out_ref, south_buf, north_buf, sems):
    del old_ref
    sub = lax.broadcasted_iota(jnp.int32, (4, FL), 0)
    masks = ((sub == 0) & (has_side(0)), (sub == 3) & (has_side(1)))
    copies = []
    for b in range(0, EX, 4):
        for side, (rim, got, buf) in enumerate(
            ((rim_south_ref, from_south_ref, south_buf), (rim_north_ref, from_north_ref, north_buf))
        ):
            for c in range(b, b + 4):
                for i in range(4):
                    row = 3 * c + i
                    more = (VISCOSITY * VISCOSITY) * got[row : row + 1, 0:FL]
                    buf[c, i] = rim[c, i] + jnp.where(masks[side], more, 0.0)
            copies.append(
                pltpu.make_async_copy(buf.at[b : b + 4], out_ref.at[0, b : b + 4, :, 7 * side], sems.at[len(copies)])
            )
            copies[-1].start()
    for copy in copies:
        copy.wait()


VM = pl.BlockSpec(memory_space=pltpu.VMEM)
ANY = pl.BlockSpec(memory_space=pl.ANY)
HBM = pl.BlockSpec(memory_space=pltpu.HBM)


def call(body, outs, specs, name, scratch=(), out_specs=None, aliases=None):
    return pl.pallas_call(
        body,
        out_shape=[jax.ShapeDtypeStruct(s, d) for s, d in outs],
        in_specs=specs,
        out_specs=out_specs or [VM] * len(outs),
        scratch_shapes=list(scratch),
        input_output_aliases=aliases or {},
        compiler_params=pltpu.CompilerParams(vmem_limit_bytes=24 * 1024 * 1024),
        name=name,
    )


def moved(array, columns, rows):
    pairs = []
    for i in range(256):
        c, r = divmod(i, PY)
        pairs.append((i, (c + columns) % 32 * PY + (r + rows) % PY))
    return lax.ppermute(array, AXES, pairs)


def swapped(array, odd):
    pairs = []
    for i in range(256):
        c, r = divmod(i, PY)
        pairs.append((i, (((c + odd) ^ 1) - odd) % 32 * PY + r))
    return lax.ppermute(array, AXES, pairs)


def across(to_south, to_north):
    return moved(to_north, 0, 1), moved(to_south, 0, -1)


def per_device(state, jacobian, metric_xx, metric_yy, metric_xy):
    left, rim, diff, near, spread_rim, spread = (jnp.asarray(t) for t in tables())
    flat = [jnp.transpose(g[0], (1, 2, 3, 0)).reshape(PTS, EX) for g in (jacobian, metric_xx, metric_yy, metric_xy)]
    rows = lambda n: ((n, LANES), F32)
    wide = ((WIDE, 4, 32, LANES), F32)
    pinned = lambda *ts: [pltpu.with_memory_space_constraint(t, pltpu.HBM) for t in ts]
    four = (HALO + 1, 4, 8, 4, FL)

    own = [((EX, 4, 32, LANES), F32), ((EX, PTS, PTS), F32)]
    rim_one, layers_one, other, f, mass, left_in, diff_in, rim_in, near_in, low, high, q, m = call(
        first_kernel,
        [rows(RIM), rows(32 * GROUPS), (four, F32), ((3, PTS, EX), F32), ((PTS, EX), F32), (left.shape, BF16), (diff.shape, F32), (rim.shape, BF16), (near.shape, F32), *[((EX, 4, 4, FL), F32)] * 2, *own],
        [HBM] * 9,
        "first",
        scratch=[pltpu.VMEM(four, F32), *[pltpu.VMEM((PTS, EX), F32)] * 4, pltpu.SemaphoreType.DMA((12,))],
    )(*pinned(state, *flat, left, diff, rim, near))
    one = swapped(rim_one, 1)
    rim_two, layers_two, q, m = call(
        other_kernel, [rows(RIM), rows(32 * GROUPS), *own], [VM] * 7, "other", aliases={5: 2, 6: 3}
    )(other, f, mass, left_in, diff_in, q, m)
    two = swapped(rim_two, 0)
    rest_one, rest_two = call(
        rest_kernel, [((PACKED, 128), F32)] * 2, [VM] * 2, "rest", scratch=[pltpu.VMEM((176, 128), F32)]
    )(layers_one, layers_two)
    rest_one = swapped(rest_one, 1)
    rest_two = swapped(rest_two, 0)
    e, own_south, own_north = call(
        rows_kernel,
        [((EX, 8, 32), F32), rows(56), rows(56)],
        [VM] * 6,
        "rows",
    )(low, high, rim_in, near_in, f, mass)
    to_south, to_north = call(merge_kernel, [rows(72)] * 2, [VM] * 4, "merge")(one, two, own_south, own_north)
    south1, north1 = across(to_south, to_north)
    q, m = call(
        own_kernel,
        own,
        [HBM, ANY] + [VM] * 6,
        "own",
        scratch=[pltpu.VMEM((8, 4, 8, 4, FL), F32), pltpu.SemaphoreType.DMA((2,))],
        aliases={6: 0, 7: 1},
    )(*pinned(state), to_south, f, mass, left_in, diff_in, q, m)
    mh, halo_e, west, east, quads = call(
        halo_kernel,
        [((2 * HALO, PTS, PTS), F32), ((2 * HALO, 8, 32), F32), rows(RIM), rows(RIM), ((QUADS, 64, 2 * PTS), BF16)],
        [VM] * 7,
        "halo",
    )(one, two, e, left_in, rim_in, diff_in, near_in)
    to_south, to_north = call(second_edges, [rows(64)] * 2, [VM] * 8, "edges2")(
        q, west, east, quads, to_south, to_north, south1, north1
    )
    south2, north2 = across(to_south, to_north)
    matrix = lambda n: [((n, PTS, 2 * PTS), BF16), ((n, PTS, PTS), BF16), ((n, 8, 32), F32)]
    inner, in_twice, in_lo, in_e = call(
        second_inner, [((14, 4, 32, LANES), F32), *matrix(14)], [VM] * 5, "inner2"
    )(q, e, south1, north1, m)
    outer, joint, out_twice, out_lo, _, quads = call(
        second_outer, [((8, 4, 32, LANES), F32), ((2, 32, LANES), F32), *matrix(8), ((QUADS, 64, 2 * PTS), BF16)], [VM] * 15, "outer2", scratch=[pltpu.VMEM((176, LANES), F32)] * 2
    )(q, west, east, rest_one, rest_two, spread_rim, spread, e, halo_e, south1, north1, m, mh, inner, in_e)
    to_south, to_north = call(third_edges, [rows(56)] * 2, [VM] * 6, "edges3")(
        inner, outer, joint, quads, south2, north2
    )
    south3, north3 = across(to_south, to_north)
    f, kept = call(third_full, [wide, ((EX, PTS, FL), F32)], [VM] * 10, "full3")(
        inner, outer, joint, south2, north2, in_twice, in_lo, out_twice, out_lo, state
    )
    to_south, to_north = call(fourth_edges, [rows(56)] * 2, [VM] * 4, "edges4")(
        f, quads, south3, north3
    )
    south4, north4 = across(to_south, to_north)
    out, rim_south, rim_north = call(
        fourth_full,
        [((1, EX, 4, 8, 4, FL), F32), ((EX, 4, 4, FL), F32), ((EX, 4, 4, FL), F32)],
        [VM] * 8,
        "full4",
        scratch=[pltpu.VMEM((WIDE, 4, 32, LANES), F32)],
    )(f, south3, north3, in_twice, in_lo, out_twice, out_lo, kept)
    (out,) = call(
        patch_kernel,
        [((1, EX, 4, 8, 4, FL), F32)],
        [ANY] + [VM] * 4,
        "patch",
        scratch=[pltpu.VMEM((EX, 4, 4, FL), F32), pltpu.VMEM((EX, 4, 4, FL), F32), pltpu.SemaphoreType.DMA((8,))],
        out_specs=[ANY],
        aliases={0: 0},
    )(out, rim_south, rim_north, south4, north4)
    return out


def solution(mesh):
    spec = P(AXES)
    return jax.shard_map(per_device, mesh=mesh, in_specs=(spec,) * 5, out_specs=spec, check_vma=False)
```

```python
import math

import jax
import jax.numpy as jnp
import numpy as np
from jax import lax
from jax.experimental import pallas as pl
from jax.experimental.pallas import tpu as pltpu
from jax.sharding import PartitionSpec as P

PY = 8
EX = 16
FL = 360
LANES = 384
PTS = 128
HALO = 3
WIDE = EX + 2 * HALO
GROUPS = 3 * HALO + 1
LINE = 25
RIM = 8 * GROUPS
REST = 17
ROWS = REST * GROUPS
USED = FL + 1 - 256
SHARE = USED // 5
FULL = 142
PACKED = 488
TAIL = LANES - FL
QUADS = -(-WIDE // 4)
AXES = ("face", "blk")
VISCOSITY = 1e-4
F32 = jnp.float32
BF16 = jnp.bfloat16


def gll_tables():
    root = 1.0 / math.sqrt(5.0)
    points = np.array([-1.0, -root, root, 1.0])
    weights = np.array([1.0 / 6.0, 5.0 / 6.0, 5.0 / 6.0, 1.0 / 6.0])
    scales = np.array(
        [np.prod([points[t] - points[o] for o in range(4) if o != t]) for t in range(4)]
    )
    derivative = np.zeros((4, 4))
    for t in range(4):
        for s in range(4):
            if t != s:
                derivative[t, s] = scales[t] / (scales[s] * (points[t] - points[s]))
        derivative[t, t] = -np.sum(derivative[t])
    return weights, derivative


def tables():
    derivative = gll_tables()[1]
    d_x = np.kron(derivative, np.eye(32))
    d_y = np.kron(np.eye(32), derivative)
    share = np.eye(PTS)
    for r in range(PTS):
        if r % 4 == 3 and r % 32 != 31:
            share[r, r + 1] = 1.0
            share[r + 1, r] = 1.0
    left = (-share @ np.concatenate([d_x.T, d_y.T], axis=1)).astype(np.float32)
    ends = np.concatenate([np.r_[32 * i : 32 * i + 4, 32 * i + 28 : 32 * i + 32] for i in range(4)])
    rim = np.zeros((16, 64), np.float32)
    rim[0:4] = left[0::32][:, np.concatenate([ends, PTS + ends])]
    rim[4:8] = left[31::32][:, np.concatenate([ends, PTS + ends])]
    diff = np.stack([d_x, d_y]).astype(np.float32)
    spread_rim = np.zeros((32 * GROUPS, RIM), np.float32)
    spread = np.zeros((32 * GROUPS, 176), np.float32)
    for g in range(GROUPS):
        for ey in range(8):
            for j in range(4):
                k = 3 * ey + j
                row = 32 * g + 4 * ey + j
                if k < 4:
                    spread_rim[row, 8 * g + k] = 1.0
                elif k > 20:
                    spread_rim[row, 8 * g + k - 17] = 1.0
                else:
                    spread[row, REST * g + k - 4] = 1.0

    def pair(a):
        high = a.astype(jnp.bfloat16)
        return np.stack([high, (a - high.astype(np.float32)).astype(jnp.bfloat16)])

    return (
        pair(left),
        pair(rim),
        diff,
        diff[:, ends][:, :, ends],
        spread_rim.astype(jnp.bfloat16),
        spread.astype(jnp.bfloat16),
    )


def halves(value):
    high = value.astype(BF16)
    low = (value - high.astype(F32)).astype(BF16)
    return high, low


def dot(a, b):
    return jnp.dot(a, b, preferred_element_type=F32)


def product(a_hi, a_lo, b):
    b_hi, b_lo = halves(b)
    return dot(a_hi, b_hi) + (dot(a_hi, b_lo) + dot(a_lo, b_hi))


def applied(m_twice, m_lo, value):
    v_hi, v_lo = halves(value)
    return dot(m_twice, jnp.concatenate([v_hi, v_lo], axis=0)) + dot(m_lo, v_hi)


def moved_rows(choice, value):
    a = value.astype(BF16)
    rest = value - a.astype(F32)
    b = rest.astype(BF16)
    c = (rest - b.astype(F32)).astype(BF16)
    return (dot(choice, c) + dot(choice, b)) + dot(choice, a)


def fluxes(diff_ref, fxx, fxy, fyy):
    d_x = diff_ref[0]
    d_y = diff_ref[1]
    return jnp.concatenate([fxx * d_x + fxy * d_y, fxy * d_x + fyy * d_y], axis=0)


def form(left_ref, diff_ref, f):
    return product(left_ref[0], left_ref[1], fluxes(diff_ref, *f))


def geometry(jac_ref, xx_ref, yy_ref, xy_ref):
    ends, inner = (float(w) for w in gll_tables()[0][0:2])
    row = lax.broadcasted_iota(jnp.int32, (PTS, EX), 0)
    along = jnp.where((row < 32) | (row >= 96), ends, inner)
    weight = jac_ref[...] * (along * jnp.where((row % 4 == 0) | (row % 4 == 3), ends, inner))
    f = (weight * xx_ref[...], weight * xy_ref[...], weight * yy_ref[...])
    up = jnp.concatenate([weight[1:], weight[:1]], axis=0)
    down = jnp.concatenate([weight[-1:], weight[:-1]], axis=0)
    mass = weight + jnp.where((row % 4 == 3) & (row % 32 != 31), up, 0.0)
    mass = mass + jnp.where((row % 4 == 0) & (row % 32 != 0), down, 0.0)
    return f, mass


def column(f, c):
    return [t[:, c : c + 1] for t in f]


def fetch(sources, buffers, sems):
    copies = [pltpu.make_async_copy(s, d, sems.at[k]) for k, (s, d) in enumerate(zip(sources, buffers))]
    for copy in copies:
        copy.start()
    return copies


def either(even, a, b):
    return jnp.where(even, a, b)


def side_columns(want_west, u_ref, f, mass, left_ref, diff_ref, rim_out_ref, layers_ref, q_ref, m_ref):
    flux = jnp.concatenate([fluxes(diff_ref, *column(f, k)) for k in range(HALO)], axis=1)
    together = product(left_ref[0], left_ref[1], flux)
    raw, part = {}, {}
    for k in range(HALO):
        m = together[:, PTS * k : PTS * k + PTS]
        m_ref[jnp.where(want_west, k, EX - HALO + k)] = m
        m_hi, m_lo = halves(m)
        q = product(m_hi, m_lo, u_ref[k].reshape(PTS, FL))
        for i in range(4):
            raw[k, i] = q[32 * i : 32 * i + 32]
            part[k, i] = mass[32 * i : 32 * i + 32, k : k + 1]
    for values in (raw, part):
        for k in range(HALO - 1):
            values[k, 3] = values[k + 1, 0] = values[k, 3] + values[k + 1, 0]
    for k in range(HALO):
        c = jnp.where(want_west, k, EX - HALO + k)
        for i in range(4):
            q_ref[c, i, :, 0:FL] = raw[k, i]
            q_ref[c, i, :, FL:LANES] = jnp.broadcast_to(part[k, i], (32, TAIL))
    near = [either(want_west, left_ref[p, 0:32, :], left_ref[p, 96:128, :]) for p in range(2)]
    m_hi, m_lo = halves(product(near[0], near[1], fluxes(diff_ref, *column(f, HALO))))
    extra = product(m_hi, m_lo, u_ref[HALO].reshape(PTS, FL))
    extra_part = either(want_west, mass[0:32, HALO : HALO + 1], mass[96:128, HALO : HALO + 1])
    sub = lax.broadcasted_iota(jnp.int32, (8, LANES), 0)
    for g in range(GROUPS):
        k, i = (g // 3, g % 3) if g < GROUPS - 1 else (HALO - 1, 3)
        row, more = raw[k, i], part[k, i]
        if g in (0, GROUPS - 1):
            joined = want_west if g else jnp.logical_not(want_west)
            row = row + either(joined, extra, 0.0)
            more = more + either(joined, extra_part, 0.0)
        tail = jnp.broadcast_to(more, (32, TAIL))
        for lanes, value in ((slice(0, FL), row), (slice(FL, LANES), tail)):
            rim_out_ref[8 * g : 8 * g + 8, lanes] = jnp.where(sub[:, lanes] < 4, value[0:8], value[24:32])
            layers_ref[32 * g : 32 * g + 32, lanes] = value
    at = FL + 1
    for t in range(3):
        for k in range(HALO):
            value = f[t][:, k : k + 1]
            rim_out_ref[:, at : at + 1] = value[0:RIM]
            rim_out_ref[0 : PTS - RIM, at + 9 : at + 10] = value[RIM:PTS]
            at += 1


def gather_rest(layers_ref, out_ref, third_ref):
    for g in range(GROUPS):
        for ey in range(1, 7):
            size = 3 if ey < 6 else 2
            to = REST * g + 3 * (ey - 1)
            at = 32 * g + 4 * ey + 1
            out_ref[to : to + size, :] = layers_ref[at : at + size, 0:128]
            out_ref[ROWS + to : ROWS + to + size, :] = layers_ref[at : at + size, 128:256]
            third_ref[to : to + size, :] = layers_ref[at : at + size, 256:384]
    last = third_ref[FULL:ROWS, :]
    size = ROWS - FULL
    lane = lax.broadcasted_iota(jnp.int32, (size, 128), 1)
    for p in range(5):
        shifted = pltpu.roll(last, USED - SHARE * p, 1)
        rows = slice(size * p, size * p + size)
        out_ref[2 * ROWS + rows.start : 2 * ROWS + rows.stop, :] = jnp.where(lane < USED, third_ref[rows, :], shifted)
    out_ref[2 * ROWS + 5 * size : 2 * ROWS + FULL, :] = third_ref[5 * size : FULL, :]
    out_ref[2 * ROWS + FULL :, :] = jnp.zeros((PACKED - 2 * ROWS - FULL, 128), F32)


def unpack_rest(got, out_ref):
    size = ROWS - FULL
    lane = lax.broadcasted_iota(jnp.int32, (size, 128), 1)
    out_ref[0:ROWS, 0:128] = got[0:ROWS]
    out_ref[0:ROWS, 128:256] = got[ROWS : 2 * ROWS]
    out_ref[0:FULL, 256:384] = got[2 * ROWS : 2 * ROWS + FULL]
    last = jnp.zeros((size, 128), F32)
    for p in range(5):
        at = 2 * ROWS + size * p
        shifted = pltpu.roll(got[at : at + size], 128 - (USED - SHARE * p), 1)
        last = jnp.where((lane >= SHARE * p) & (lane < SHARE * p + SHARE), shifted, last)
    out_ref[FULL:ROWS, 256:384] = last
    out_ref[ROWS:, :] = jnp.zeros((out_ref.shape[0] - ROWS, LANES), F32)


def nearest(want_west, t):
    at = EX - HALO
    return jnp.concatenate([either(want_west, t[:, 0:HALO], t[:, at:EX]), either(want_west, t[:, HALO : HALO + 1], t[:, at - 1 : at])], axis=1)


def first_kernel(u_hbm, jac_hbm, xx_hbm, yy_hbm, xy_hbm, left_hbm, diff_hbm, rim_hbm, near_hbm, rim_out_ref, layers_ref, other_ref, f_ref, mass_ref, left_ref, diff_ref, rim_ref, near_ref, low_ref, high_ref, q_ref, m_ref, u_ref, jac_ref, xx_ref, yy_ref, xy_ref, sems):
    want_west = even_column()
    here = jnp.where(want_west, 0, EX - HALO)
    there = EX - HALO - here
    here_next = jnp.where(want_west, HALO, EX - HALO - 1)
    there_next = EX - 1 - here_next
    copies = fetch(
        (jac_hbm, xx_hbm, yy_hbm, xy_hbm, left_hbm, diff_hbm, u_hbm.at[0, pl.ds(here, HALO)], u_hbm.at[0, pl.ds(here_next, 1)], u_hbm.at[0, pl.ds(there, HALO)], u_hbm.at[0, pl.ds(there_next, 1)], rim_hbm, near_hbm, u_hbm.at[0, :, :, 0], u_hbm.at[0, :, :, 7]),
        (jac_ref, xx_ref, yy_ref, xy_ref, left_ref, diff_ref, u_ref.at[0:HALO], u_ref.at[HALO:], other_ref.at[0:HALO], other_ref.at[HALO:], rim_ref, near_ref, low_ref, high_ref),
        sems,
    )
    for copy in copies[:6]:
        copy.wait()
    f, mass = geometry(jac_ref, xx_ref, yy_ref, xy_ref)
    for t in range(3):
        f_ref[t] = f[t]
    mass_ref[...] = mass
    copies[6].wait()
    copies[7].wait()
    side_columns(want_west, u_ref, [nearest(want_west, t) for t in f], nearest(want_west, mass), left_ref, diff_ref, rim_out_ref, layers_ref, q_ref, m_ref)
    for copy in copies[8:]:
        copy.wait()


def other_kernel(u_ref, f_ref, mass_ref, left_ref, diff_ref, q_in, m_in, rim_out_ref, layers_ref, q_ref, m_ref):
    del q_in, m_in
    want_west = jnp.logical_not(even_column())
    f = [nearest(want_west, f_ref[t]) for t in range(3)]
    side_columns(want_west, u_ref, f, nearest(want_west, mass_ref[...]), left_ref, diff_ref, rim_out_ref, layers_ref, q_ref, m_ref)


def rest_kernel(first_ref, other_ref, one_ref, two_ref, third_ref):
    gather_rest(first_ref, one_ref, third_ref)
    gather_rest(other_ref, two_ref, third_ref)


def end_rows(f):
    return [jnp.concatenate([t[32 * i + a : 32 * i + a + 4] for i in range(4) for a in (0, 28)], axis=0) for t in f]


def rows_kernel(low_ref, high_ref, rim_ref, near_ref, f_ref, mass_ref, e_ref, south_ref, north_ref):
    f = end_rows([f_ref[t] for t in range(3)])
    for c in range(EX):
        e_ref[c] = form(rim_ref, near_ref, column(f, c))[0:8]
    matrices = [quad([e_ref[c + k] for k in range(4)]) for c in range(0, EX, 4)]
    mass = mass_ref[...]
    outs = (south_ref, north_ref)
    carry = [None, None]
    for c in range(0, EX, 4):
        tiles = [ref[c + k, i] for k in range(4) for i in range(4) for ref in (low_ref, high_ref)]
        r = rim_product(matrices[c // 4], jnp.concatenate(tiles, axis=0))
        for side, out in enumerate(outs):
            rows = with_carry(r, side, carry[side])
            carry[side] = rows[12:13]
            out[3 * c : 3 * c + 12, 0:FL] = rows[0:12]
    for side, (out, at) in enumerate(zip(outs, (0, 31))):
        out[48:49, 0:FL] = carry[side]
        for c in range(EX):
            for i in range(4 if c == EX - 1 else 3):
                row = 3 * c + i
                part = mass[32 * i + at : 32 * i + at + 1, c : c + 1]
                if i == 0 and c > 0:
                    part = part + mass[96 + at : 97 + at, c - 1 : c]
                out[row : row + 1, FL:LANES] = jnp.broadcast_to(part, (1, TAIL))
        out[49:56, :] = jnp.zeros((7, LANES), F32)


def quad(es):
    blocks = []
    for k, e in enumerate(es):
        rows = []
        for side in range(2):
            if k:
                rows.append(jnp.zeros((3 * k, 32), F32))
            rows.append(e[4 * side : 4 * side + 4])
            rows.append(jnp.zeros((12 - 3 * k, 32), F32))
        blocks.append(jnp.concatenate(rows, axis=0))
    high, low = halves(jnp.concatenate(blocks, axis=1))
    return jnp.concatenate(
        [jnp.concatenate([high, high], axis=1), jnp.concatenate([low, jnp.zeros_like(low)], axis=1)], axis=0
    )


def rim_product(matrix, value):
    v_hi, v_lo = halves(value)
    both = dot(matrix, jnp.concatenate([v_hi, v_lo], axis=0))
    return both[0:32] + both[32:64]


def with_carry(r, side, carry):
    rows = r[16 * side : 16 * side + 16]
    if carry is None:
        return rows
    sub = lax.broadcasted_iota(jnp.int32, rows.shape, 0)
    return rows + jnp.where(sub == 0, carry, 0.0)


def own_kernel(u_hbm, after_ref, f_ref, mass_ref, left_ref, diff_ref, q_in, m_in, q_ref, m_ref, u_ref, sems):
    del after_ref, q_in, m_in
    first, final = HALO, EX - HALO - 1
    copies = fetch(
        [u_hbm.at[0, c : c + 5] for c in range(first, final, 5)], [u_ref.at[c : c + 5] for c in range(0, 10, 5)], sems
    )
    f = [f_ref[t] for t in range(3)]
    mass = mass_ref[...]
    for c in range(first, final + 1):
        m = form(left_ref, diff_ref, column(f, c))
        m_ref[c] = m
        m_hi, m_lo = halves(m)
        if (c - first) % 5 == 0:
            copies[(c - first) // 5].wait()
        q = product(m_hi, m_lo, u_ref[c - first].reshape(PTS, FL))
        for i in range(4):
            q_ref[c, i, :, 0:FL] = q[32 * i : 32 * i + 32]
            q_ref[c, i, :, FL:LANES] = jnp.broadcast_to(mass[32 * i : 32 * i + 32, c : c + 1], (32, TAIL))
        join_own(q_ref, c)
    join_own(q_ref, final + 1)


def join_own(q_ref, c):
    shared = q_ref[c - 1, 3] + q_ref[c, 0]
    q_ref[c - 1, 3] = shared
    q_ref[c, 0] = shared


def merge_kernel(one_ref, two_ref, own_south_ref, own_north_ref, south_ref, north_ref):
    even = even_column()
    for out, own, at in ((south_ref, own_south_ref, 0), (north_ref, own_north_ref, 7)):
        out[10:57, :] = own[1:48, :]
        for g in range(GROUPS - 1):
            r = 8 * g + at
            out[g : g + 1, :] = either(even, one_ref[r : r + 1, :], two_ref[r : r + 1, :])
            r = 8 * (g + 1) + at
            out[58 + g : 59 + g, :] = either(even, two_ref[r : r + 1, :], one_ref[r : r + 1, :])
        r = 8 * (GROUPS - 1) + at
        out[9:10, :] = either(even, one_ref[r : r + 1, :], two_ref[r : r + 1, :]) + own[0:1, :]
        out[57:58, :] = own[48:49, :] + either(even, two_ref[at : at + 1, :], one_ref[at : at + 1, :])
        out[67:72, :] = jnp.zeros((5, LANES), F32)


def halo_kernel(one_ref, two_ref, own_e_ref, left_ref, rim_ref, diff_ref, near_ref, m_ref, e_ref, west_ref, east_ref, quads_ref):
    even = even_column()
    west_ref[...] = either(even, one_ref[...], two_ref[...])
    east_ref[...] = either(even, two_ref[...], one_ref[...])
    for side, ref in enumerate((west_ref, east_ref)):
        at = FL + 1
        for k in range(HALO):
            lanes = [at + HALO * t + k for t in range(3)]
            fs = [jnp.concatenate([ref[:, a : a + 1], ref[0 : PTS - RIM, a + 9 : a + 10]], axis=0) for a in lanes]
            m_ref[HALO * side + k] = form(left_ref, diff_ref, fs)
            e_ref[HALO * side + k] = form(rim_ref, near_ref, end_rows(fs))[0:8]
    put_quads(rim_matrix(own_e_ref, e_ref), quads_ref)


def put_quads(matrix, quads_ref):
    for q in range(QUADS):
        columns = range(4 * q, 4 * q + 4)
        quads_ref[q] = quad([matrix(e) if e < WIDE else jnp.zeros((8, 32), F32) for e in columns])


def place():
    return lax.axis_index("face") * 64 + lax.axis_index("blk")


def even_column():
    return lax.rem(lax.div(place(), PY), 2) == 0


def has_side(side):
    return lax.rem(place(), PY) != (0, PY - 1)[side]


def edge_masks():
    sub = lax.broadcasted_iota(jnp.int32, (8, LANES), 0)
    return (sub == 0) & (has_side(0)), (sub == 7) & (has_side(1))


def first_tile(value, south_ref, row, masks):
    return value + jnp.where(masks[0], south_ref[row : row + 1, :], 0.0)


def last_tile(value, north_ref, row, masks):
    return value + jnp.where(masks[1], north_ref[row : row + 1, :], 0.0)


def column_value(part, e, lo, south_ref, north_ref, masks):
    tiles = []
    for i in range(4):
        row = 3 * (e - lo) + i
        tiles.append(first_tile(part(e, i, 0, 8), south_ref, row, masks))
        tiles.append(part(e, i, 8, 24))
        tiles.append(last_tile(part(e, i, 24, 32), north_ref, row, masks))
    return jnp.concatenate(tiles, axis=0)


def rim_value(part, e, lo, south_ref, north_ref, masks):
    tiles = []
    for i in range(4):
        row = 3 * (e - lo) + i
        tiles.append(last_tile(first_tile(part(e, i), south_ref, row, masks), north_ref, row, masks))
    return jnp.concatenate(tiles, axis=0)


def both_ends(ref, k, i):
    sub = lax.broadcasted_iota(jnp.int32, (8, LANES), 0)
    return jnp.where(sub < 4, ref[k, i, 0:8], ref[k, i, 24:32])


def group_of(k, i):
    return 3 * k + i


def rim_part(q_ref, west_ref, east_ref):
    def part(e, i):
        if (e, i) in ((HALO - 1, 3), (HALO, 0)):
            g = 8 * (GROUPS - 1)
            return west_ref[g : g + 8] + both_ends(q_ref, 0, 0)
        if (e, i) in ((HALO + EX - 1, 3), (HALO + EX, 0)):
            return both_ends(q_ref, EX - 1, 3) + east_ref[0:8]
        if HALO <= e < HALO + EX:
            return both_ends(q_ref, e - HALO, i)
        ref, k = (west_ref, e) if e < HALO else (east_ref, e - HALO - EX)
        g = 8 * group_of(k, i)
        return ref[g : g + 8]

    return part


def edges(part, lo, scales, from_south_ref, from_north_ref, quads_ref, south_ref, north_ref):
    hi = WIDE - 1 - lo
    masks = edge_masks()
    start, stop = 3 * (lo + 1), 3 * (hi - 1) + 4
    carry = [None, None]
    for q in range(QUADS):
        values = []
        for e in range(4 * q, 4 * q + 4):
            if lo <= e <= hi:
                value = rim_value(part, e, lo, from_south_ref, from_north_ref, masks)
                if scales is not None:
                    value = value * (1.0 / value[:, FL : FL + 1])
                values.append(value)
            else:
                values.append(jnp.zeros((32, LANES), F32))
        r = rim_product(quads_ref[q], jnp.concatenate(values, axis=0))
        for side, out in enumerate((south_ref, north_ref)):
            rows = with_carry(r, side, carry[side])
            carry[side] = rows[12:13]
            a, b = max(start, 12 * q), min(stop, 12 * q + 12)
            if a < b:
                rows = rows[a - 12 * q : b - 12 * q]
                if scales is not None:
                    rows = rows * scales[side][a:b]
                out[a - start : b - start, :] = rows
    for out in (south_ref, north_ref):
        out[stop - start :, :] = jnp.zeros((out.shape[0] - stop + start, LANES), F32)


def second_edges(q_ref, west_ref, east_ref, quads_ref, sent_south_ref, sent_north_ref, from_south_ref, from_north_ref, south_ref, north_ref):
    scales = []
    for side, (sent, got) in enumerate(((sent_south_ref, from_south_ref), (sent_north_ref, from_north_ref))):
        other = jnp.where(has_side(side), got[:, FL : FL + 1], 0.0)
        scales.append(1.0 / (sent[:, FL : FL + 1] + other))
    part = rim_part(q_ref, west_ref, east_ref)
    edges(part, 0, scales, from_south_ref, from_north_ref, quads_ref, south_ref, north_ref)


def rim_matrix(e_ref, halo_e_ref):
    def matrix(e):
        if HALO <= e < HALO + EX:
            return e_ref[e - HALO]
        return halo_e_ref[e if e < HALO else e - EX]

    return matrix


def third_edges(inner_ref, outer_ref, joint_ref, quads_ref, from_south_ref, from_north_ref, south_ref, north_ref):
    sub = lax.broadcasted_iota(jnp.int32, (8, LANES), 0)
    whole = split_part(inner_ref, outer_ref, joint_ref)

    def part(e, i):
        return jnp.where(sub < 4, whole(e, i, 0, 8), whole(e, i, 24, 32))

    edges(part, 1, None, from_south_ref, from_north_ref, quads_ref, south_ref, north_ref)


def fourth_edges(f_ref, quads_ref, from_south_ref, from_north_ref, south_ref, north_ref):
    def part(e, i):
        return both_ends(f_ref, e, i)

    edges(part, 2, None, from_south_ref, from_north_ref, quads_ref, south_ref, north_ref)


def join(out_ref, e, q):
    shared = out_ref[e - 1, 3] + q[0:32]
    out_ref[e - 1, 3] = shared
    out_ref[e, 0] = shared


def put(out_ref, e, first, q):
    for i in range(4):
        out_ref[e, i] = q[32 * i : 32 * i + 32]
    if e > first:
        join(out_ref, e, q)


INNER = range(HALO + 1, HALO + EX - 1)
OUTER = [e for e in range(WIDE) if e not in INNER]


def split_at(e):
    return (True, e - INNER[0]) if e in INNER else (False, OUTER.index(e))


def split_part(inner_ref, outer_ref, joint_ref):
    def part(e, i, a, b):
        if (e, i) in ((INNER[0] - 1, 3), (INNER[0], 0)):
            return joint_ref[0, a:b]
        if (e, i) in ((INNER[-1], 3), (INNER[-1] + 1, 0)):
            return joint_ref[1, a:b]
        inner, k = split_at(e)
        return (inner_ref if inner else outer_ref)[k, i, a:b]

    return part


def second_column(value, m, k, rim, out_ref, join_before, twice_ref, lo_ref, scaled_ref):
    inverse = 1.0 / value[:, FL : FL + 1]
    m_hi, m_lo = halves(m * inverse)
    twice = jnp.concatenate([m_hi, m_hi], axis=1)
    twice_ref[k] = twice
    lo_ref[k] = m_lo
    put(out_ref, k, 0 if join_before else k, applied(twice, m_lo, value * inverse))
    rows = jnp.concatenate(
        [inverse[32 * i : 32 * i + 1] for i in range(4)] + [inverse[32 * i + 31 : 32 * i + 32] for i in range(4)], axis=0
    )
    scaled_ref[k] = rim * rows


def second_inner(q_ref, e_ref, from_south_ref, from_north_ref, m_ref, out_ref, twice_ref, lo_ref, scaled_ref):
    def part(e, i, a, b):
        return q_ref[e - HALO, i, a:b]

    masks = edge_masks()
    for k, e in enumerate(INNER):
        value = column_value(part, e, 0, from_south_ref, from_north_ref, masks)
        second_column(value, m_ref[e - HALO], k, e_ref[e - HALO], out_ref, k > 0, twice_ref, lo_ref, scaled_ref)


def second_outer(q_ref, west_ref, east_ref, one_rest_ref, two_rest_ref, spread_rim_ref, spread_ref, e_ref, halo_e_ref, from_south_ref, from_north_ref, m_ref, mh_ref, inner_ref, in_e_ref, out_ref, joint_ref, twice_ref, lo_ref, scaled_ref, quads_ref, rest_a, rest_b):
    even = even_column()
    unpack_rest(either(even, one_rest_ref[...], two_rest_ref[...]), rest_a)
    unpack_rest(either(even, two_rest_ref[...], one_rest_ref[...]), rest_b)
    rests = (rest_a[...], rest_b[...])
    wide = [
        moved_rows(spread_rim_ref[...], rim[...]) + moved_rows(spread_ref[...], rest)
        for rim, rest in zip((west_ref, east_ref), rests)
    ]

    def part(e, i, a, b):
        if (e, i) in ((HALO - 1, 3), (HALO, 0)):
            g = 32 * (GROUPS - 1)
            return wide[0][g + a : g + b] + q_ref[0, 0, a:b]
        if (e, i) in ((HALO + EX - 1, 3), (HALO + EX, 0)):
            return q_ref[EX - 1, 3, a:b] + wide[1][a:b]
        if HALO <= e < HALO + EX:
            return q_ref[e - HALO, i, a:b]
        side, k = (0, e) if e < HALO else (1, e - HALO - EX)
        g = 32 * group_of(k, i)
        return wide[side][g + a : g + b]

    masks = edge_masks()
    for k, e in enumerate(OUTER):
        value = column_value(part, e, 0, from_south_ref, from_north_ref, masks)
        if e < HALO:
            m = mh_ref[e]
        elif e < HALO + EX:
            m = m_ref[e - HALO]
        else:
            m = mh_ref[e - EX]
        second_column(value, m, k, rim_matrix(e_ref, halo_e_ref)(e), out_ref, k not in (0, len(OUTER) // 2), twice_ref, lo_ref, scaled_ref)
    half = len(OUTER) // 2
    joint_ref[0] = out_ref[half - 1, 3] + inner_ref[0, 0]
    joint_ref[1] = inner_ref[len(INNER) - 1, 3] + out_ref[half, 0]

    def matrix(e):
        inner, k = split_at(e)
        return (in_e_ref if inner else scaled_ref)[k]

    put_quads(matrix, quads_ref)


def matrices(e, inner, outer):
    is_inner, k = split_at(e)
    twice_ref, lo_ref = inner if is_inner else outer
    return twice_ref[k], lo_ref[k]


def third_full(inner_ref, outer_ref, joint_ref, from_south_ref, from_north_ref, in_twice, in_lo, out_twice, out_lo, u_ref, out_ref, kept_ref):
    part = split_part(inner_ref, outer_ref, joint_ref)
    masks = edge_masks()
    for e in range(1, WIDE - 1):
        value = column_value(part, e, 1, from_south_ref, from_north_ref, masks)
        if HALO <= e < HALO + EX:
            c = e - HALO
            kept_ref[c] = u_ref[0, c].reshape(PTS, FL) - (2.0 * VISCOSITY) * value[:, 0:FL]
        put(out_ref, e, 1, applied(*matrices(e, (in_twice, in_lo), (out_twice, out_lo)), value))


def fourth_full(f_ref, from_south_ref, from_north_ref, in_twice, in_lo, out_twice, out_lo, kept_ref, out_ref, rim_south_ref, rim_north_ref, z_ref):
    def part(e, i, a, b):
        return f_ref[e, i, a:b]

    masks = edge_masks()
    for e in range(2, WIDE - 2):
        value = column_value(part, e, 2, from_south_ref, from_north_ref, masks)
        put(z_ref, e, 2, applied(*matrices(e, (in_twice, in_lo), (out_twice, out_lo)), value))
        c = e - HALO - 1
        if 0 <= c < EX:
            z = jnp.concatenate([z_ref[e - 1, i, :, 0:FL] for i in range(4)], axis=0)
            done = (kept_ref[c] + (VISCOSITY * VISCOSITY) * z).reshape(4, 8, 4, FL)
            out_ref[0, c] = done
            rim_south_ref[c] = done[:, 0]
            rim_north_ref[c] = done[:, 7]


def patch_kernel(old_ref, rim_south_ref, rim_north_ref, from_south_ref, from_north_ref, out_ref, south_buf, north_buf, sems):
    del old_ref
    sub = lax.broadcasted_iota(jnp.int32, (4, FL), 0)
    masks = ((sub == 0) & (has_side(0)), (sub == 3) & (has_side(1)))
    copies = []
    for b in range(0, EX, 4):
        for side, (rim, got, buf) in enumerate(
            ((rim_south_ref, from_south_ref, south_buf), (rim_north_ref, from_north_ref, north_buf))
        ):
            for c in range(b, b + 4):
                for i in range(4):
                    row = 3 * c + i
                    more = (VISCOSITY * VISCOSITY) * got[row : row + 1, 0:FL]
                    buf[c, i] = rim[c, i] + jnp.where(masks[side], more, 0.0)
            copies.append(
                pltpu.make_async_copy(buf.at[b : b + 4], out_ref.at[0, b : b + 4, :, 7 * side], sems.at[len(copies)])
            )
            copies[-1].start()
    for copy in copies:
        copy.wait()


VM = pl.BlockSpec(memory_space=pltpu.VMEM)
ANY = pl.BlockSpec(memory_space=pl.ANY)
HBM = pl.BlockSpec(memory_space=pltpu.HBM)


def call(body, outs, specs, name, scratch=(), out_specs=None, aliases=None):
    return pl.pallas_call(
        body,
        out_shape=[jax.ShapeDtypeStruct(s, d) for s, d in outs],
        in_specs=specs,
        out_specs=out_specs or [VM] * len(outs),
        scratch_shapes=list(scratch),
        input_output_aliases=aliases or {},
        compiler_params=pltpu.CompilerParams(vmem_limit_bytes=24 * 1024 * 1024),
        name=name,
    )


def moved(array, columns, rows):
    pairs = []
    for i in range(256):
        c, r = divmod(i, PY)
        pairs.append((i, (c + columns) % 32 * PY + (r + rows) % PY))
    return lax.ppermute(array, AXES, pairs)


def swapped(array, odd):
    pairs = []
    for i in range(256):
        c, r = divmod(i, PY)
        pairs.append((i, (((c + odd) ^ 1) - odd) % 32 * PY + r))
    return lax.ppermute(array, AXES, pairs)


def across(to_south, to_north):
    return moved(to_north, 0, 1), moved(to_south, 0, -1)


def per_device(state, jacobian, metric_xx, metric_yy, metric_xy):
    left, rim, diff, near, spread_rim, spread = (jnp.asarray(t) for t in tables())
    flat = [jnp.transpose(g[0], (1, 2, 3, 0)).reshape(PTS, EX) for g in (jacobian, metric_xx, metric_yy, metric_xy)]
    rows = lambda n: ((n, LANES), F32)
    wide = ((WIDE, 4, 32, LANES), F32)
    pinned = lambda *ts: [pltpu.with_memory_space_constraint(t, pltpu.HBM) for t in ts]
    four = (HALO + 1, 4, 8, 4, FL)

    own = [((EX, 4, 32, LANES), F32), ((EX, PTS, PTS), F32)]
    rim_one, layers_one, other, f, mass, left_in, diff_in, rim_in, near_in, low, high, q, m = call(
        first_kernel,
        [rows(RIM), rows(32 * GROUPS), (four, F32), ((3, PTS, EX), F32), ((PTS, EX), F32), (left.shape, BF16), (diff.shape, F32), (rim.shape, BF16), (near.shape, F32), *[((EX, 4, 4, FL), F32)] * 2, *own],
        [HBM] * 9,
        "first",
        scratch=[pltpu.VMEM(four, F32), *[pltpu.VMEM((PTS, EX), F32)] * 4, pltpu.SemaphoreType.DMA((14,))],
    )(*pinned(state, *flat, left, diff, rim, near))
    one = swapped(rim_one, 1)
    rim_two, layers_two, q, m = call(
        other_kernel, [rows(RIM), rows(32 * GROUPS), *own], [VM] * 7, "other", aliases={5: 2, 6: 3}
    )(other, f, mass, left_in, diff_in, q, m)
    two = swapped(rim_two, 0)
    rest_one, rest_two = call(
        rest_kernel, [((PACKED, 128), F32)] * 2, [VM] * 2, "rest", scratch=[pltpu.VMEM((176, 128), F32)]
    )(layers_one, layers_two)
    rest_one = swapped(rest_one, 1)
    rest_two = swapped(rest_two, 0)
    e, own_south, own_north = call(
        rows_kernel,
        [((EX, 8, 32), F32), rows(56), rows(56)],
        [VM] * 6,
        "rows",
    )(low, high, rim_in, near_in, f, mass)
    to_south, to_north = call(merge_kernel, [rows(72)] * 2, [VM] * 4, "merge")(one, two, own_south, own_north)
    south1, north1 = across(to_south, to_north)
    q, m = call(
        own_kernel,
        own,
        [HBM, ANY] + [VM] * 6,
        "own",
        scratch=[pltpu.VMEM((10, 4, 8, 4, FL), F32), pltpu.SemaphoreType.DMA((2,))],
        aliases={6: 0, 7: 1},
    )(*pinned(state), to_south, f, mass, left_in, diff_in, q, m)
    mh, halo_e, west, east, quads = call(
        halo_kernel,
        [((2 * HALO, PTS, PTS), F32), ((2 * HALO, 8, 32), F32), rows(RIM), rows(RIM), ((QUADS, 64, 2 * PTS), BF16)],
        [VM] * 7,
        "halo",
    )(one, two, e, left_in, rim_in, diff_in, near_in)
    to_south, to_north = call(second_edges, [rows(64)] * 2, [VM] * 8, "edges2")(
        q, west, east, quads, to_south, to_north, south1, north1
    )
    south2, north2 = across(to_south, to_north)
    matrix = lambda n: [((n, PTS, 2 * PTS), BF16), ((n, PTS, PTS), BF16), ((n, 8, 32), F32)]
    inner, in_twice, in_lo, in_e = call(
        second_inner, [((14, 4, 32, LANES), F32), *matrix(14)], [VM] * 5, "inner2"
    )(q, e, south1, north1, m)
    outer, joint, out_twice, out_lo, _, quads = call(
        second_outer, [((8, 4, 32, LANES), F32), ((2, 32, LANES), F32), *matrix(8), ((QUADS, 64, 2 * PTS), BF16)], [VM] * 15, "outer2", scratch=[pltpu.VMEM((176, LANES), F32)] * 2
    )(q, west, east, rest_one, rest_two, spread_rim, spread, e, halo_e, south1, north1, m, mh, inner, in_e)
    to_south, to_north = call(third_edges, [rows(56)] * 2, [VM] * 6, "edges3")(
        inner, outer, joint, quads, south2, north2
    )
    south3, north3 = across(to_south, to_north)
    f, kept = call(third_full, [wide, ((EX, PTS, FL), F32)], [VM] * 10, "full3")(
        inner, outer, joint, south2, north2, in_twice, in_lo, out_twice, out_lo, state
    )
    to_south, to_north = call(fourth_edges, [rows(56)] * 2, [VM] * 4, "edges4")(
        f, quads, south3, north3
    )
    south4, north4 = across(to_south, to_north)
    out, rim_south, rim_north = call(
        fourth_full,
        [((1, EX, 4, 8, 4, FL), F32), ((EX, 4, 4, FL), F32), ((EX, 4, 4, FL), F32)],
        [VM] * 8,
        "full4",
        scratch=[pltpu.VMEM((WIDE, 4, 32, LANES), F32)],
    )(f, south3, north3, in_twice, in_lo, out_twice, out_lo, kept)
    (out,) = call(
        patch_kernel,
        [((1, EX, 4, 8, 4, FL), F32)],
        [ANY] + [VM] * 4,
        "patch",
        scratch=[pltpu.VMEM((EX, 4, 4, FL), F32), pltpu.VMEM((EX, 4, 4, FL), F32), pltpu.SemaphoreType.DMA((8,))],
        out_specs=[ANY],
        aliases={0: 0},
    )(out, rim_south, rim_north, south4, north4)
    return out


def solution(mesh):
    spec = P(AXES)
    return jax.shard_map(per_device, mesh=mesh, in_specs=(spec,) * 5, out_specs=spec, check_vma=False)
```

```python
import math

import jax
import jax.numpy as jnp
import numpy as np
from jax import lax
from jax.experimental import pallas as pl
from jax.experimental.pallas import tpu as pltpu
from jax.sharding import PartitionSpec as P

PY = 8
EX = 16
FL = 360
LANES = 384
PTS = 128
HALO = 3
WIDE = EX + 2 * HALO
GROUPS = 3 * HALO + 1
LINE = 25
RIM = 8 * GROUPS
REST = 17
ROWS = REST * GROUPS
USED = FL + 1 - 256
SHARE = USED // 5
FULL = 142
PACKED = 488
TAIL = LANES - FL
QUADS = -(-WIDE // 4)
AXES = ("face", "blk")
VISCOSITY = 1e-4
F32 = jnp.float32
BF16 = jnp.bfloat16


def gll_tables():
    root = 1.0 / math.sqrt(5.0)
    points = np.array([-1.0, -root, root, 1.0])
    weights = np.array([1.0 / 6.0, 5.0 / 6.0, 5.0 / 6.0, 1.0 / 6.0])
    scales = np.array(
        [np.prod([points[t] - points[o] for o in range(4) if o != t]) for t in range(4)]
    )
    derivative = np.zeros((4, 4))
    for t in range(4):
        for s in range(4):
            if t != s:
                derivative[t, s] = scales[t] / (scales[s] * (points[t] - points[s]))
        derivative[t, t] = -np.sum(derivative[t])
    return weights, derivative


def tables():
    derivative = gll_tables()[1]
    d_x = np.kron(derivative, np.eye(32))
    d_y = np.kron(np.eye(32), derivative)
    share = np.eye(PTS)
    for r in range(PTS):
        if r % 4 == 3 and r % 32 != 31:
            share[r, r + 1] = 1.0
            share[r + 1, r] = 1.0
    left = (-share @ np.concatenate([d_x.T, d_y.T], axis=1)).astype(np.float32)
    ends = np.concatenate([np.r_[32 * i : 32 * i + 4, 32 * i + 28 : 32 * i + 32] for i in range(4)])
    rim = np.zeros((16, 64), np.float32)
    rim[0:4] = left[0::32][:, np.concatenate([ends, PTS + ends])]
    rim[4:8] = left[31::32][:, np.concatenate([ends, PTS + ends])]
    diff = np.stack([d_x, d_y]).astype(np.float32)
    spread_rim = np.zeros((32 * GROUPS, RIM), np.float32)
    spread = np.zeros((32 * GROUPS, 176), np.float32)
    for g in range(GROUPS):
        for ey in range(8):
            for j in range(4):
                k = 3 * ey + j
                row = 32 * g + 4 * ey + j
                if k < 4:
                    spread_rim[row, 8 * g + k] = 1.0
                elif k > 20:
                    spread_rim[row, 8 * g + k - 17] = 1.0
                else:
                    spread[row, REST * g + k - 4] = 1.0

    def pair(a):
        high = a.astype(jnp.bfloat16)
        return np.stack([high, (a - high.astype(np.float32)).astype(jnp.bfloat16)])

    return (
        pair(left),
        pair(rim),
        diff,
        diff[:, ends][:, :, ends],
        spread_rim.astype(jnp.bfloat16),
        spread.astype(jnp.bfloat16),
    )


def halves(value):
    high = value.astype(BF16)
    low = (value - high.astype(F32)).astype(BF16)
    return high, low


def dot(a, b):
    return jnp.dot(a, b, preferred_element_type=F32)


def product(a_hi, a_lo, b):
    b_hi, b_lo = halves(b)
    return dot(a_hi, b_hi) + (dot(a_hi, b_lo) + dot(a_lo, b_hi))


def applied(m_twice, m_lo, value):
    v_hi, v_lo = halves(value)
    return dot(m_twice, jnp.concatenate([v_hi, v_lo], axis=0)) + dot(m_lo, v_hi)


def moved_rows(choice, value):
    a = value.astype(BF16)
    rest = value - a.astype(F32)
    b = rest.astype(BF16)
    c = (rest - b.astype(F32)).astype(BF16)
    return (dot(choice, c) + dot(choice, b)) + dot(choice, a)


def fluxes(diff_ref, fxx, fxy, fyy):
    d_x = diff_ref[0]
    d_y = diff_ref[1]
    return jnp.concatenate([fxx * d_x + fxy * d_y, fxy * d_x + fyy * d_y], axis=0)


def form(left_ref, diff_ref, f):
    return product(left_ref[0], left_ref[1], fluxes(diff_ref, *f))


def geometry(jac_ref, xx_ref, yy_ref, xy_ref):
    ends, inner = (float(w) for w in gll_tables()[0][0:2])
    row = lax.broadcasted_iota(jnp.int32, (PTS, EX), 0)
    along = jnp.where((row < 32) | (row >= 96), ends, inner)
    weight = jac_ref[...] * (along * jnp.where((row % 4 == 0) | (row % 4 == 3), ends, inner))
    f = (weight * xx_ref[...], weight * xy_ref[...], weight * yy_ref[...])
    up = jnp.concatenate([weight[1:], weight[:1]], axis=0)
    down = jnp.concatenate([weight[-1:], weight[:-1]], axis=0)
    mass = weight + jnp.where((row % 4 == 3) & (row % 32 != 31), up, 0.0)
    mass = mass + jnp.where((row % 4 == 0) & (row % 32 != 0), down, 0.0)
    return f, mass


def column(f, c):
    return [t[:, c : c + 1] for t in f]


def fetch(sources, buffers, sems):
    copies = [pltpu.make_async_copy(s, d, sems.at[k]) for k, (s, d) in enumerate(zip(sources, buffers))]
    for copy in copies:
        copy.start()
    return copies


def either(even, a, b):
    return jnp.where(even, a, b)


def side_columns(want_west, u_ref, f, mass, left_ref, diff_ref, rim_out_ref, layers_ref, q_ref, m_ref):
    flux = jnp.concatenate([fluxes(diff_ref, *column(f, k)) for k in range(HALO)], axis=1)
    together = product(left_ref[0], left_ref[1], flux)
    raw, part = {}, {}
    for k in range(HALO):
        m = together[:, PTS * k : PTS * k + PTS]
        m_ref[jnp.where(want_west, k, EX - HALO + k)] = m
        m_hi, m_lo = halves(m)
        q = product(m_hi, m_lo, u_ref[jnp.where(want_west, k, EX - HALO + k)].reshape(PTS, FL))
        for i in range(4):
            raw[k, i] = q[32 * i : 32 * i + 32]
            part[k, i] = mass[32 * i : 32 * i + 32, k : k + 1]
    for values in (raw, part):
        for k in range(HALO - 1):
            values[k, 3] = values[k + 1, 0] = values[k, 3] + values[k + 1, 0]
    for k in range(HALO):
        c = jnp.where(want_west, k, EX - HALO + k)
        for i in range(4):
            q_ref[c, i, :, 0:FL] = raw[k, i]
            q_ref[c, i, :, FL:LANES] = jnp.broadcast_to(part[k, i], (32, TAIL))
    near = [either(want_west, left_ref[p, 0:32, :], left_ref[p, 96:128, :]) for p in range(2)]
    m_hi, m_lo = halves(product(near[0], near[1], fluxes(diff_ref, *column(f, HALO))))
    extra = product(m_hi, m_lo, u_ref[jnp.where(want_west, HALO, EX - HALO - 1)].reshape(PTS, FL))
    extra_part = either(want_west, mass[0:32, HALO : HALO + 1], mass[96:128, HALO : HALO + 1])
    sub = lax.broadcasted_iota(jnp.int32, (8, LANES), 0)
    for g in range(GROUPS):
        k, i = (g // 3, g % 3) if g < GROUPS - 1 else (HALO - 1, 3)
        row, more = raw[k, i], part[k, i]
        if g in (0, GROUPS - 1):
            joined = want_west if g else jnp.logical_not(want_west)
            row = row + either(joined, extra, 0.0)
            more = more + either(joined, extra_part, 0.0)
        tail = jnp.broadcast_to(more, (32, TAIL))
        for lanes, value in ((slice(0, FL), row), (slice(FL, LANES), tail)):
            rim_out_ref[8 * g : 8 * g + 8, lanes] = jnp.where(sub[:, lanes] < 4, value[0:8], value[24:32])
            layers_ref[32 * g : 32 * g + 32, lanes] = value
    at = FL + 1
    for t in range(3):
        for k in range(HALO):
            value = f[t][:, k : k + 1]
            rim_out_ref[:, at : at + 1] = value[0:RIM]
            rim_out_ref[0 : PTS - RIM, at + 9 : at + 10] = value[RIM:PTS]
            at += 1


def gather_rest(layers_ref, out_ref, third_ref):
    for g in range(GROUPS):
        for ey in range(1, 7):
            size = 3 if ey < 6 else 2
            to = REST * g + 3 * (ey - 1)
            at = 32 * g + 4 * ey + 1
            out_ref[to : to + size, :] = layers_ref[at : at + size, 0:128]
            out_ref[ROWS + to : ROWS + to + size, :] = layers_ref[at : at + size, 128:256]
            third_ref[to : to + size, :] = layers_ref[at : at + size, 256:384]
    last = third_ref[FULL:ROWS, :]
    size = ROWS - FULL
    lane = lax.broadcasted_iota(jnp.int32, (size, 128), 1)
    for p in range(5):
        shifted = pltpu.roll(last, USED - SHARE * p, 1)
        rows = slice(size * p, size * p + size)
        out_ref[2 * ROWS + rows.start : 2 * ROWS + rows.stop, :] = jnp.where(lane < USED, third_ref[rows, :], shifted)
    out_ref[2 * ROWS + 5 * size : 2 * ROWS + FULL, :] = third_ref[5 * size : FULL, :]
    out_ref[2 * ROWS + FULL :, :] = jnp.zeros((PACKED - 2 * ROWS - FULL, 128), F32)


def unpack_rest(got, out_ref):
    size = ROWS - FULL
    lane = lax.broadcasted_iota(jnp.int32, (size, 128), 1)
    out_ref[0:ROWS, 0:128] = got[0:ROWS]
    out_ref[0:ROWS, 128:256] = got[ROWS : 2 * ROWS]
    out_ref[0:FULL, 256:384] = got[2 * ROWS : 2 * ROWS + FULL]
    last = jnp.zeros((size, 128), F32)
    for p in range(5):
        at = 2 * ROWS + size * p
        shifted = pltpu.roll(got[at : at + size], 128 - (USED - SHARE * p), 1)
        last = jnp.where((lane >= SHARE * p) & (lane < SHARE * p + SHARE), shifted, last)
    out_ref[FULL:ROWS, 256:384] = last
    out_ref[ROWS:, :] = jnp.zeros((out_ref.shape[0] - ROWS, LANES), F32)


def nearest(want_west, t):
    at = EX - HALO
    return jnp.concatenate([either(want_west, t[:, 0:HALO], t[:, at:EX]), either(want_west, t[:, HALO : HALO + 1], t[:, at - 1 : at])], axis=1)


def first_kernel(u_hbm, jac_hbm, xx_hbm, yy_hbm, xy_hbm, left_hbm, diff_hbm, rim_hbm, near_hbm, rim_out_ref, layers_ref, f_ref, mass_ref, left_ref, diff_ref, rim_ref, near_ref, q_ref, m_ref, u_ref, jac_ref, xx_ref, yy_ref, xy_ref, sems):
    want_west = even_column()
    size = HALO + 1
    here = pl.ds(jnp.where(want_west, 0, EX - size), size)
    copies = fetch(
        (jac_hbm, xx_hbm, yy_hbm, xy_hbm, left_hbm, diff_hbm, u_hbm.at[0, here], rim_hbm, near_hbm),
        (jac_ref, xx_ref, yy_ref, xy_ref, left_ref, diff_ref, u_ref.at[here], rim_ref, near_ref),
        sems,
    )
    for copy in copies[:6]:
        copy.wait()
    f, mass = geometry(jac_ref, xx_ref, yy_ref, xy_ref)
    for t in range(3):
        f_ref[t] = f[t]
    mass_ref[...] = mass
    copies[6].wait()
    side_columns(want_west, u_ref, [nearest(want_west, t) for t in f], nearest(want_west, mass), left_ref, diff_ref, rim_out_ref, layers_ref, q_ref, m_ref)
    for copy in copies[7:]:
        copy.wait()


def other_kernel(u_ref, f_ref, mass_ref, left_ref, diff_ref, q_in, m_in, rim_out_ref, layers_ref, q_ref, m_ref):
    del q_in, m_in
    want_west = jnp.logical_not(even_column())
    f = [nearest(want_west, f_ref[t]) for t in range(3)]
    side_columns(want_west, u_ref, f, nearest(want_west, mass_ref[...]), left_ref, diff_ref, rim_out_ref, layers_ref, q_ref, m_ref)


def rest_kernel(first_ref, other_ref, one_ref, two_ref, third_ref):
    gather_rest(first_ref, one_ref, third_ref)
    gather_rest(other_ref, two_ref, third_ref)


def end_rows(f):
    return [jnp.concatenate([t[32 * i + a : 32 * i + a + 4] for i in range(4) for a in (0, 28)], axis=0) for t in f]


def rows_kernel(u_ref, rim_ref, near_ref, f_ref, mass_ref, e_ref, south_ref, north_ref):
    f = end_rows([f_ref[t] for t in range(3)])
    for c in range(EX):
        e_ref[c] = form(rim_ref, near_ref, column(f, c))[0:8]
    matrices = [quad([e_ref[c + k] for k in range(4)]) for c in range(0, EX, 4)]
    mass = mass_ref[...]
    outs = (south_ref, north_ref)
    carry = [None, None]
    for c in range(0, EX, 4):
        tiles = [u_ref[c + k, i, ey] for k in range(4) for i in range(4) for ey in (0, 7)]
        r = rim_product(matrices[c // 4], jnp.concatenate(tiles, axis=0))
        for side, out in enumerate(outs):
            rows = with_carry(r, side, carry[side])
            carry[side] = rows[12:13]
            out[3 * c : 3 * c + 12, 0:FL] = rows[0:12]
    for side, (out, at) in enumerate(zip(outs, (0, 31))):
        out[48:49, 0:FL] = carry[side]
        for c in range(EX):
            for i in range(4 if c == EX - 1 else 3):
                row = 3 * c + i
                part = mass[32 * i + at : 32 * i + at + 1, c : c + 1]
                if i == 0 and c > 0:
                    part = part + mass[96 + at : 97 + at, c - 1 : c]
                out[row : row + 1, FL:LANES] = jnp.broadcast_to(part, (1, TAIL))
        out[49:56, :] = jnp.zeros((7, LANES), F32)


def quad(es):
    blocks = []
    for k, e in enumerate(es):
        rows = []
        for side in range(2):
            if k:
                rows.append(jnp.zeros((3 * k, 32), F32))
            rows.append(e[4 * side : 4 * side + 4])
            rows.append(jnp.zeros((12 - 3 * k, 32), F32))
        blocks.append(jnp.concatenate(rows, axis=0))
    high, low = halves(jnp.concatenate(blocks, axis=1))
    return jnp.concatenate(
        [jnp.concatenate([high, high], axis=1), jnp.concatenate([low, jnp.zeros_like(low)], axis=1)], axis=0
    )


def rim_product(matrix, value):
    v_hi, v_lo = halves(value)
    both = dot(matrix, jnp.concatenate([v_hi, v_lo], axis=0))
    return both[0:32] + both[32:64]


def with_carry(r, side, carry):
    rows = r[16 * side : 16 * side + 16]
    if carry is None:
        return rows
    sub = lax.broadcasted_iota(jnp.int32, rows.shape, 0)
    return rows + jnp.where(sub == 0, carry, 0.0)


def own_kernel(u_ref, after_ref, f_ref, mass_ref, left_ref, diff_ref, q_in, m_in, q_ref, m_ref):
    del after_ref, q_in, m_in
    first, final = HALO, EX - HALO - 1
    f = [f_ref[t] for t in range(3)]
    mass = mass_ref[...]
    for c in range(first, final + 1):
        m = form(left_ref, diff_ref, column(f, c))
        m_ref[c] = m
        m_hi, m_lo = halves(m)
        q = product(m_hi, m_lo, u_ref[c].reshape(PTS, FL))
        for i in range(4):
            q_ref[c, i, :, 0:FL] = q[32 * i : 32 * i + 32]
            q_ref[c, i, :, FL:LANES] = jnp.broadcast_to(mass[32 * i : 32 * i + 32, c : c + 1], (32, TAIL))
        join_own(q_ref, c)
    join_own(q_ref, final + 1)


def join_own(q_ref, c):
    shared = q_ref[c - 1, 3] + q_ref[c, 0]
    q_ref[c - 1, 3] = shared
    q_ref[c, 0] = shared


def merge_kernel(one_ref, two_ref, own_south_ref, own_north_ref, south_ref, north_ref):
    even = even_column()
    for out, own, at in ((south_ref, own_south_ref, 0), (north_ref, own_north_ref, 7)):
        out[10:57, :] = own[1:48, :]
        for g in range(GROUPS - 1):
            r = 8 * g + at
            out[g : g + 1, :] = either(even, one_ref[r : r + 1, :], two_ref[r : r + 1, :])
            r = 8 * (g + 1) + at
            out[58 + g : 59 + g, :] = either(even, two_ref[r : r + 1, :], one_ref[r : r + 1, :])
        r = 8 * (GROUPS - 1) + at
        out[9:10, :] = either(even, one_ref[r : r + 1, :], two_ref[r : r + 1, :]) + own[0:1, :]
        out[57:58, :] = own[48:49, :] + either(even, two_ref[at : at + 1, :], one_ref[at : at + 1, :])
        out[67:72, :] = jnp.zeros((5, LANES), F32)


def halo_kernel(one_ref, two_ref, own_e_ref, left_ref, rim_ref, diff_ref, near_ref, m_ref, e_ref, west_ref, east_ref, quads_ref):
    even = even_column()
    west_ref[...] = either(even, one_ref[...], two_ref[...])
    east_ref[...] = either(even, two_ref[...], one_ref[...])
    for side, ref in enumerate((west_ref, east_ref)):
        at = FL + 1
        for k in range(HALO):
            lanes = [at + HALO * t + k for t in range(3)]
            fs = [jnp.concatenate([ref[:, a : a + 1], ref[0 : PTS - RIM, a + 9 : a + 10]], axis=0) for a in lanes]
            m_ref[HALO * side + k] = form(left_ref, diff_ref, fs)
            e_ref[HALO * side + k] = form(rim_ref, near_ref, end_rows(fs))[0:8]
    put_quads(rim_matrix(own_e_ref, e_ref), quads_ref)


def put_quads(matrix, quads_ref):
    for q in range(QUADS):
        columns = range(4 * q, 4 * q + 4)
        quads_ref[q] = quad([matrix(e) if e < WIDE else jnp.zeros((8, 32), F32) for e in columns])


def place():
    return lax.axis_index("face") * 64 + lax.axis_index("blk")


def even_column():
    return lax.rem(lax.div(place(), PY), 2) == 0


def has_side(side):
    return lax.rem(place(), PY) != (0, PY - 1)[side]


def edge_masks():
    sub = lax.broadcasted_iota(jnp.int32, (8, LANES), 0)
    return (sub == 0) & (has_side(0)), (sub == 7) & (has_side(1))


def first_tile(value, south_ref, row, masks):
    return value + jnp.where(masks[0], south_ref[row : row + 1, :], 0.0)


def last_tile(value, north_ref, row, masks):
    return value + jnp.where(masks[1], north_ref[row : row + 1, :], 0.0)


def column_value(part, e, lo, south_ref, north_ref, masks):
    tiles = []
    for i in range(4):
        row = 3 * (e - lo) + i
        tiles.append(first_tile(part(e, i, 0, 8), south_ref, row, masks))
        tiles.append(part(e, i, 8, 24))
        tiles.append(last_tile(part(e, i, 24, 32), north_ref, row, masks))
    return jnp.concatenate(tiles, axis=0)


def rim_value(part, e, lo, south_ref, north_ref, masks):
    tiles = []
    for i in range(4):
        row = 3 * (e - lo) + i
        tiles.append(last_tile(first_tile(part(e, i), south_ref, row, masks), north_ref, row, masks))
    return jnp.concatenate(tiles, axis=0)


def both_ends(ref, k, i):
    sub = lax.broadcasted_iota(jnp.int32, (8, LANES), 0)
    return jnp.where(sub < 4, ref[k, i, 0:8], ref[k, i, 24:32])


def group_of(k, i):
    return 3 * k + i


def rim_part(q_ref, west_ref, east_ref):
    def part(e, i):
        if (e, i) in ((HALO - 1, 3), (HALO, 0)):
            g = 8 * (GROUPS - 1)
            return west_ref[g : g + 8] + both_ends(q_ref, 0, 0)
        if (e, i) in ((HALO + EX - 1, 3), (HALO + EX, 0)):
            return both_ends(q_ref, EX - 1, 3) + east_ref[0:8]
        if HALO <= e < HALO + EX:
            return both_ends(q_ref, e - HALO, i)
        ref, k = (west_ref, e) if e < HALO else (east_ref, e - HALO - EX)
        g = 8 * group_of(k, i)
        return ref[g : g + 8]

    return part


def edges(part, lo, scales, from_south_ref, from_north_ref, quads_ref, south_ref, north_ref):
    hi = WIDE - 1 - lo
    masks = edge_masks()
    start, stop = 3 * (lo + 1), 3 * (hi - 1) + 4
    carry = [None, None]
    for q in range(QUADS):
        values = []
        for e in range(4 * q, 4 * q + 4):
            if lo <= e <= hi:
                value = rim_value(part, e, lo, from_south_ref, from_north_ref, masks)
                if scales is not None:
                    value = value * (1.0 / value[:, FL : FL + 1])
                values.append(value)
            else:
                values.append(jnp.zeros((32, LANES), F32))
        r = rim_product(quads_ref[q], jnp.concatenate(values, axis=0))
        for side, out in enumerate((south_ref, north_ref)):
            rows = with_carry(r, side, carry[side])
            carry[side] = rows[12:13]
            a, b = max(start, 12 * q), min(stop, 12 * q + 12)
            if a < b:
                rows = rows[a - 12 * q : b - 12 * q]
                if scales is not None:
                    rows = rows * scales[side][a:b]
                out[a - start : b - start, :] = rows
    for out in (south_ref, north_ref):
        out[stop - start :, :] = jnp.zeros((out.shape[0] - stop + start, LANES), F32)


def second_edges(q_ref, west_ref, east_ref, quads_ref, sent_south_ref, sent_north_ref, from_south_ref, from_north_ref, south_ref, north_ref):
    scales = []
    for side, (sent, got) in enumerate(((sent_south_ref, from_south_ref), (sent_north_ref, from_north_ref))):
        other = jnp.where(has_side(side), got[:, FL : FL + 1], 0.0)
        scales.append(1.0 / (sent[:, FL : FL + 1] + other))
    part = rim_part(q_ref, west_ref, east_ref)
    edges(part, 0, scales, from_south_ref, from_north_ref, quads_ref, south_ref, north_ref)


def rim_matrix(e_ref, halo_e_ref):
    def matrix(e):
        if HALO <= e < HALO + EX:
            return e_ref[e - HALO]
        return halo_e_ref[e if e < HALO else e - EX]

    return matrix


def third_edges(inner_ref, outer_ref, joint_ref, quads_ref, from_south_ref, from_north_ref, south_ref, north_ref):
    sub = lax.broadcasted_iota(jnp.int32, (8, LANES), 0)
    whole = split_part(inner_ref, outer_ref, joint_ref)

    def part(e, i):
        return jnp.where(sub < 4, whole(e, i, 0, 8), whole(e, i, 24, 32))

    edges(part, 1, None, from_south_ref, from_north_ref, quads_ref, south_ref, north_ref)


def fourth_edges(f_ref, quads_ref, from_south_ref, from_north_ref, south_ref, north_ref):
    def part(e, i):
        return both_ends(f_ref, e, i)

    edges(part, 2, None, from_south_ref, from_north_ref, quads_ref, south_ref, north_ref)


def join(out_ref, e, q):
    shared = out_ref[e - 1, 3] + q[0:32]
    out_ref[e - 1, 3] = shared
    out_ref[e, 0] = shared


def put(out_ref, e, first, q):
    for i in range(4):
        out_ref[e, i] = q[32 * i : 32 * i + 32]
    if e > first:
        join(out_ref, e, q)


INNER = range(HALO + 1, HALO + EX - 1)
OUTER = [e for e in range(WIDE) if e not in INNER]


def split_at(e):
    return (True, e - INNER[0]) if e in INNER else (False, OUTER.index(e))


def split_part(inner_ref, outer_ref, joint_ref):
    def part(e, i, a, b):
        if (e, i) in ((INNER[0] - 1, 3), (INNER[0], 0)):
            return joint_ref[0, a:b]
        if (e, i) in ((INNER[-1], 3), (INNER[-1] + 1, 0)):
            return joint_ref[1, a:b]
        inner, k = split_at(e)
        return (inner_ref if inner else outer_ref)[k, i, a:b]

    return part


def second_column(value, m, k, rim, out_ref, join_before, twice_ref, lo_ref, scaled_ref):
    inverse = 1.0 / value[:, FL : FL + 1]
    m_hi, m_lo = halves(m * inverse)
    twice = jnp.concatenate([m_hi, m_hi], axis=1)
    twice_ref[k] = twice
    lo_ref[k] = m_lo
    put(out_ref, k, 0 if join_before else k, applied(twice, m_lo, value * inverse))
    rows = jnp.concatenate(
        [inverse[32 * i : 32 * i + 1] for i in range(4)] + [inverse[32 * i + 31 : 32 * i + 32] for i in range(4)], axis=0
    )
    scaled_ref[k] = rim * rows


def second_inner(q_ref, e_ref, from_south_ref, from_north_ref, m_ref, out_ref, twice_ref, lo_ref, scaled_ref):
    def part(e, i, a, b):
        return q_ref[e - HALO, i, a:b]

    masks = edge_masks()
    for k, e in enumerate(INNER):
        value = column_value(part, e, 0, from_south_ref, from_north_ref, masks)
        second_column(value, m_ref[e - HALO], k, e_ref[e - HALO], out_ref, k > 0, twice_ref, lo_ref, scaled_ref)


def second_outer(q_ref, west_ref, east_ref, one_rest_ref, two_rest_ref, spread_rim_ref, spread_ref, e_ref, halo_e_ref, from_south_ref, from_north_ref, m_ref, mh_ref, inner_ref, in_e_ref, out_ref, joint_ref, twice_ref, lo_ref, scaled_ref, quads_ref, rest_a, rest_b):
    even = even_column()
    unpack_rest(either(even, one_rest_ref[...], two_rest_ref[...]), rest_a)
    unpack_rest(either(even, two_rest_ref[...], one_rest_ref[...]), rest_b)
    rests = (rest_a[...], rest_b[...])
    wide = [
        moved_rows(spread_rim_ref[...], rim[...]) + moved_rows(spread_ref[...], rest)
        for rim, rest in zip((west_ref, east_ref), rests)
    ]

    def part(e, i, a, b):
        if (e, i) in ((HALO - 1, 3), (HALO, 0)):
            g = 32 * (GROUPS - 1)
            return wide[0][g + a : g + b] + q_ref[0, 0, a:b]
        if (e, i) in ((HALO + EX - 1, 3), (HALO + EX, 0)):
            return q_ref[EX - 1, 3, a:b] + wide[1][a:b]
        if HALO <= e < HALO + EX:
            return q_ref[e - HALO, i, a:b]
        side, k = (0, e) if e < HALO else (1, e - HALO - EX)
        g = 32 * group_of(k, i)
        return wide[side][g + a : g + b]

    masks = edge_masks()
    for k, e in enumerate(OUTER):
        value = column_value(part, e, 0, from_south_ref, from_north_ref, masks)
        if e < HALO:
            m = mh_ref[e]
        elif e < HALO + EX:
            m = m_ref[e - HALO]
        else:
            m = mh_ref[e - EX]
        second_column(value, m, k, rim_matrix(e_ref, halo_e_ref)(e), out_ref, k not in (0, len(OUTER) // 2), twice_ref, lo_ref, scaled_ref)
    half = len(OUTER) // 2
    joint_ref[0] = out_ref[half - 1, 3] + inner_ref[0, 0]
    joint_ref[1] = inner_ref[len(INNER) - 1, 3] + out_ref[half, 0]

    def matrix(e):
        inner, k = split_at(e)
        return (in_e_ref if inner else scaled_ref)[k]

    put_quads(matrix, quads_ref)


def matrices(e, inner, outer):
    is_inner, k = split_at(e)
    twice_ref, lo_ref = inner if is_inner else outer
    return twice_ref[k], lo_ref[k]


def third_full(inner_ref, outer_ref, joint_ref, from_south_ref, from_north_ref, in_twice, in_lo, out_twice, out_lo, u_ref, out_ref, kept_ref):
    part = split_part(inner_ref, outer_ref, joint_ref)
    masks = edge_masks()
    for e in range(1, WIDE - 1):
        value = column_value(part, e, 1, from_south_ref, from_north_ref, masks)
        if HALO <= e < HALO + EX:
            c = e - HALO
            kept_ref[c] = u_ref[0, c].reshape(PTS, FL) - (2.0 * VISCOSITY) * value[:, 0:FL]
        put(out_ref, e, 1, applied(*matrices(e, (in_twice, in_lo), (out_twice, out_lo)), value))


def fourth_full(f_ref, from_south_ref, from_north_ref, in_twice, in_lo, out_twice, out_lo, kept_ref, out_ref, rim_south_ref, rim_north_ref, z_ref):
    def part(e, i, a, b):
        return f_ref[e, i, a:b]

    masks = edge_masks()
    for e in range(2, WIDE - 2):
        value = column_value(part, e, 2, from_south_ref, from_north_ref, masks)
        put(z_ref, e, 2, applied(*matrices(e, (in_twice, in_lo), (out_twice, out_lo)), value))
        c = e - HALO - 1
        if 0 <= c < EX:
            z = jnp.concatenate([z_ref[e - 1, i, :, 0:FL] for i in range(4)], axis=0)
            done = (kept_ref[c] + (VISCOSITY * VISCOSITY) * z).reshape(4, 8, 4, FL)
            out_ref[0, c] = done
            rim_south_ref[c] = done[:, 0]
            rim_north_ref[c] = done[:, 7]


def patch_kernel(old_ref, rim_south_ref, rim_north_ref, from_south_ref, from_north_ref, out_ref, south_buf, north_buf, sems):
    del old_ref
    sub = lax.broadcasted_iota(jnp.int32, (4, FL), 0)
    masks = ((sub == 0) & (has_side(0)), (sub == 3) & (has_side(1)))
    copies = []
    for b in range(0, EX, 4):
        for side, (rim, got, buf) in enumerate(
            ((rim_south_ref, from_south_ref, south_buf), (rim_north_ref, from_north_ref, north_buf))
        ):
            for c in range(b, b + 4):
                for i in range(4):
                    row = 3 * c + i
                    more = (VISCOSITY * VISCOSITY) * got[row : row + 1, 0:FL]
                    buf[c, i] = rim[c, i] + jnp.where(masks[side], more, 0.0)
            copies.append(
                pltpu.make_async_copy(buf.at[b : b + 4], out_ref.at[0, b : b + 4, :, 7 * side], sems.at[len(copies)])
            )
            copies[-1].start()
    for copy in copies:
        copy.wait()


VM = pl.BlockSpec(memory_space=pltpu.VMEM)
ANY = pl.BlockSpec(memory_space=pl.ANY)
HBM = pl.BlockSpec(memory_space=pltpu.HBM)


def call(body, outs, specs, name, scratch=(), out_specs=None, aliases=None):
    return pl.pallas_call(
        body,
        out_shape=[jax.ShapeDtypeStruct(s, d) for s, d in outs],
        in_specs=specs,
        out_specs=out_specs or [VM] * len(outs),
        scratch_shapes=list(scratch),
        input_output_aliases=aliases or {},
        compiler_params=pltpu.CompilerParams(vmem_limit_bytes=24 * 1024 * 1024),
        name=name,
    )


def moved(array, columns, rows):
    pairs = []
    for i in range(256):
        c, r = divmod(i, PY)
        pairs.append((i, (c + columns) % 32 * PY + (r + rows) % PY))
    return lax.ppermute(array, AXES, pairs)


def swapped(array, odd):
    pairs = []
    for i in range(256):
        c, r = divmod(i, PY)
        pairs.append((i, (((c + odd) ^ 1) - odd) % 32 * PY + r))
    return lax.ppermute(array, AXES, pairs)


def across(to_south, to_north):
    return moved(to_north, 0, 1), moved(to_south, 0, -1)


def per_device(state, jacobian, metric_xx, metric_yy, metric_xy):
    left, rim, diff, near, spread_rim, spread = (jnp.asarray(t) for t in tables())
    flat = [jnp.transpose(g[0], (1, 2, 3, 0)).reshape(PTS, EX) for g in (jacobian, metric_xx, metric_yy, metric_xy)]
    rows = lambda n: ((n, LANES), F32)
    wide = ((WIDE, 4, 32, LANES), F32)
    pinned = lambda *ts: [pltpu.with_memory_space_constraint(t, pltpu.HBM) for t in ts]
    every = (EX, 4, 8, 4, FL)

    own = [((EX, 4, 32, LANES), F32), ((EX, PTS, PTS), F32)]
    u = state.reshape(every)
    rim_one, layers_one, f, mass, left_in, diff_in, rim_in, near_in, q, m = call(
        first_kernel,
        [rows(RIM), rows(32 * GROUPS), ((3, PTS, EX), F32), ((PTS, EX), F32), (left.shape, BF16), (diff.shape, F32), (rim.shape, BF16), (near.shape, F32), *own],
        [HBM] * 9,
        "first",
        scratch=[pltpu.VMEM(every, F32), *[pltpu.VMEM((PTS, EX), F32)] * 4, pltpu.SemaphoreType.DMA((10,))],
    )(*pinned(state, *flat, left, diff, rim, near))
    one = swapped(rim_one, 1)
    rim_two, layers_two, q, m = call(
        other_kernel, [rows(RIM), rows(32 * GROUPS), *own], [VM] * 7, "other", aliases={5: 2, 6: 3}
    )(u, f, mass, left_in, diff_in, q, m)
    two = swapped(rim_two, 0)
    rest_one, rest_two = call(
        rest_kernel, [((PACKED, 128), F32)] * 2, [VM] * 2, "rest", scratch=[pltpu.VMEM((176, 128), F32)]
    )(layers_one, layers_two)
    rest_one = swapped(rest_one, 1)
    rest_two = swapped(rest_two, 0)
    e, own_south, own_north = call(
        rows_kernel,
        [((EX, 8, 32), F32), rows(56), rows(56)],
        [VM] * 5,
        "rows",
    )(u, rim_in, near_in, f, mass)
    to_south, to_north = call(merge_kernel, [rows(72)] * 2, [VM] * 4, "merge")(one, two, own_south, own_north)
    south1, north1 = across(to_south, to_north)
    q, m = call(
        own_kernel,
        own,
        [VM, ANY] + [VM] * 6,
        "own",
        aliases={6: 0, 7: 1},
    )(u, to_south, f, mass, left_in, diff_in, q, m)
    mh, halo_e, west, east, quads = call(
        halo_kernel,
        [((2 * HALO, PTS, PTS), F32), ((2 * HALO, 8, 32), F32), rows(RIM), rows(RIM), ((QUADS, 64, 2 * PTS), BF16)],
        [VM] * 7,
        "halo",
    )(one, two, e, left_in, rim_in, diff_in, near_in)
    to_south, to_north = call(second_edges, [rows(64)] * 2, [VM] * 8, "edges2")(
        q, west, east, quads, to_south, to_north, south1, north1
    )
    south2, north2 = across(to_south, to_north)
    matrix = lambda n: [((n, PTS, 2 * PTS), BF16), ((n, PTS, PTS), BF16), ((n, 8, 32), F32)]
    inner, in_twice, in_lo, in_e = call(
        second_inner, [((14, 4, 32, LANES), F32), *matrix(14)], [VM] * 5, "inner2"
    )(q, e, south1, north1, m)
    outer, joint, out_twice, out_lo, _, quads = call(
        second_outer, [((8, 4, 32, LANES), F32), ((2, 32, LANES), F32), *matrix(8), ((QUADS, 64, 2 * PTS), BF16)], [VM] * 15, "outer2", scratch=[pltpu.VMEM((176, LANES), F32)] * 2
    )(q, west, east, rest_one, rest_two, spread_rim, spread, e, halo_e, south1, north1, m, mh, inner, in_e)
    to_south, to_north = call(third_edges, [rows(56)] * 2, [VM] * 6, "edges3")(
        inner, outer, joint, quads, south2, north2
    )
    south3, north3 = across(to_south, to_north)
    f, kept = call(third_full, [wide, ((EX, PTS, FL), F32)], [VM] * 10, "full3")(
        inner, outer, joint, south2, north2, in_twice, in_lo, out_twice, out_lo, state
    )
    to_south, to_north = call(fourth_edges, [rows(56)] * 2, [VM] * 4, "edges4")(
        f, quads, south3, north3
    )
    south4, north4 = across(to_south, to_north)
    out, rim_south, rim_north = call(
        fourth_full,
        [((1, EX, 4, 8, 4, FL), F32), ((EX, 4, 4, FL), F32), ((EX, 4, 4, FL), F32)],
        [VM] * 8,
        "full4",
        scratch=[pltpu.VMEM((WIDE, 4, 32, LANES), F32)],
    )(f, south3, north3, in_twice, in_lo, out_twice, out_lo, kept)
    (out,) = call(
        patch_kernel,
        [((1, EX, 4, 8, 4, FL), F32)],
        [ANY] + [VM] * 4,
        "patch",
        scratch=[pltpu.VMEM((EX, 4, 4, FL), F32), pltpu.VMEM((EX, 4, 4, FL), F32), pltpu.SemaphoreType.DMA((8,))],
        out_specs=[ANY],
        aliases={0: 0},
    )(out, rim_south, rim_north, south4, north4)
    return out


def solution(mesh):
    spec = P(AXES)
    return jax.shard_map(per_device, mesh=mesh, in_specs=(spec,) * 5, out_specs=spec, check_vma=False)
```
